128 devices in a mesh: space: 32 (over x, y, core), depth: 4 (over z).
Axes of the slice: x: 4, y: 4, z: 4, core: 2. Of those that a mesh axis runs over, the one named last changes fastest.
Arguments:
- positions: float32 [3, 32, 4, 4096], P(None, 'space', 'depth'), as said below
- species: int32 [32, 4, 4096], P('space', 'depth'), may hold values from 0 to 3
- neighbours: int32 [8, 32, 4, 4096], P(None, 'space', 'depth'), may hold values from 0 to 36608, as said below
- counts: int32 [32, 4, 4096], P('space', 'depth'), may hold values from 1 to 8
- species_table: bfloat16 [4, 64], replicated, may hold values from -6 to 6
- w_two_in: bfloat16 [136, 256], replicated, may hold values from -0.5 to 0.5
- w_two_out: bfloat16 [256, 64], replicated, may hold values from -0.375 to 0.375
- w_env: bfloat16 [64, 32], replicated, may hold values from -0.75 to 0.75
- w_lat_in: bfloat16 [96, 256], replicated, may hold values from -0.625 to 0.625
- w_lat_out: bfloat16 [256, 64], replicated, may hold values from -0.375 to 0.375
- readout: float32 [64], replicated, may hold values from -0.75 to 0.75
Outputs:
- forces: float32 [3, 32, 4, 4096], P(None, 'space', 'depth')
- atom_energy: float32 [32, 4, 4096], P('space', 'depth')
- virial: float32 [3, 3], replicated
The draws below stay inside these ranges and needn't reach their ends.
Inputs may be any that keep to these rules, and one draw needn't show every extreme that they name: `positions`: an atom of block (s, d) has first coordinate in [2.0 * 16 s, 2.0 * 16 (s + 1)), second in [0, 2.0 * 16), third in [2.0 * 16 d, 2.0 * 16 (d + 1)). `neighbours`: the block an entry names always exists (no offset leads off the slab), no atom names itself, and every live slot names an atom within 5 of the atom.
All inputs are finite; a program needn't handle non-finite values.
Results may differ from the reference program's by a relative error of at most 0.0075.
Values sent between devices are 32-bit elements; how exact they have to be, the bound alone decides.
A program may use at most 192 MiB of HBM per device.

```python
import jax
import jax.numpy as jnp
import numpy as np
from jax import lax

ATOMS = 4096
SIDE = 16
LAYERS = 16
NBR = 8
SPECIES = 4
EMB = 64
LAT = 64
HID = 256
TENS = 32
IN = 136
SPACE_BLOCKS = 32
DEPTH_BLOCKS = 4
N_SPACE = 32
N_DEPTH = 4


LATTICE_STEP = 2.0


JITTER = 0.2


def offset_table():
    rows = []
    for step_x in (-2, -1, 0, 1, 2):
        for step_y in (-2, -1, 0, 1, 2):
            for step_z in (-2, -1, 0, 1, 2):
                total = abs(step_x) + abs(step_y) + abs(step_z)
                widest = max(abs(step_x), abs(step_y), abs(step_z))
                if widest <= 1 and total >= 1 and (total <= 2):
                    rows.append((step_x, step_y, step_z))
                if widest == 2 and total == 2:
                    rows.append((step_x, step_y, step_z))
    return np.array(rows, dtype=np.int32)


def offset_row(table, target):
    for position in range(table.shape[0]):
        if tuple((int(v) for v in table[position])) == target:
            return position
    return 0


def lattice_sites():
    atom_index = jnp.arange(ATOMS, dtype=jnp.int32)
    site_x = atom_index % SIDE
    site_z = atom_index // SIDE % SIDE
    site_y = atom_index // (SIDE * SIDE)
    return (site_x, site_y, site_z)


def neighbour_plan(key):
    key_score, key_inner, key_outer = jax.random.split(jax.random.fold_in(key, 11), 3)
    table = offset_table()
    offset_total = table.shape[0]
    upper_row = offset_row(table, (1, 0, 1))
    lower_row = offset_row(table, (-1, 0, -1))
    step_x = jnp.asarray(table[:, 0])[:, None, None, None]
    step_y = jnp.asarray(table[:, 1])[:, None, None, None]
    step_z = jnp.asarray(table[:, 2])[:, None, None, None]
    site_x, site_y, site_z = lattice_sites()
    space_index = jnp.arange(N_SPACE, dtype=jnp.int32)[:, None, None]
    depth_index = jnp.arange(N_DEPTH, dtype=jnp.int32)[None, :, None]
    global_x = space_index * SIDE + site_x[None, None, :]
    global_z = depth_index * SIDE + site_z[None, None, :]
    near_x = global_x[None] + step_x
    near_y = site_y[None, None, None, :] + step_y
    near_z = global_z[None] + step_z
    valid = (near_x >= 0) & (near_x < N_SPACE * SIDE) & (near_y >= 0) & (near_y < LAYERS) & (near_z >= 0) & (near_z < N_DEPTH * SIDE)
    full_shape = (offset_total, N_SPACE, N_DEPTH, ATOMS)
    order_tag = jnp.arange(offset_total, dtype=jnp.int32)[:, None, None, None]
    atom_tag = jnp.arange(ATOMS, dtype=jnp.int32)[None, None, None, :]
    scores = jax.random.randint(key_score, full_shape, 0, 1 << 20) * 32 + 32 + order_tag
    forced = (order_tag == upper_row) & (atom_tag == ATOMS - 1) | (order_tag == lower_row) & (atom_tag == 0)
    scores = jnp.where(forced, order_tag, scores)
    scores = jnp.where(valid, scores, (1 << 26) + order_tag)
    order = jnp.argsort(scores, axis=0, stable=True)[:NBR]
    pick_x = jnp.take_along_axis(jnp.broadcast_to(near_x, full_shape), order, axis=0)
    pick_y = jnp.take_along_axis(jnp.broadcast_to(near_y, full_shape), order, axis=0)
    pick_z = jnp.take_along_axis(jnp.broadcast_to(near_z, full_shape), order, axis=0)
    pick_ok = jnp.take_along_axis(valid, order, axis=0)
    block_x = pick_x // SIDE - space_index[None]
    block_z = pick_z // SIDE - depth_index[None]
    local = pick_x % SIDE + SIDE * (pick_z % SIDE + SIDE * pick_y)
    entries = ((block_x + 1) * 3 + block_z + 1) * ATOMS + local
    entries = jnp.where(pick_ok, entries, entries[0:1])
    valid_count = jnp.sum(valid.astype(jnp.int32), axis=0)
    count_shape = (N_SPACE, N_DEPTH, ATOMS)
    light = jax.random.randint(key_inner, count_shape, 1, NBR // 4 + 1)
    heavy_block = jax.random.randint(key_outer, (), 0, N_SPACE)
    heavy = space_index == heavy_block
    drawn = jnp.minimum(jnp.where(heavy, NBR, light), valid_count)
    drawn = drawn.at[:, :, 1 + SIDE + SIDE * SIDE].set(NBR)
    drawn = drawn.at[:, 0, 1].set(1)
    return (entries.astype(jnp.int32), drawn.astype(jnp.int32))


def draw_positions(key, part):
    key = jax.random.fold_in(key, 1)
    jitter = jax.random.uniform(key, (3, N_SPACE, N_DEPTH, ATOMS), jnp.float32, -JITTER, JITTER)
    site_x, site_y, site_z = lattice_sites()
    zeros = jnp.zeros((N_SPACE, N_DEPTH, ATOMS), jnp.float32)
    space_anchor = jnp.arange(N_SPACE, dtype=jnp.float32)[:, None, None] * SIDE + zeros
    depth_anchor = jnp.arange(N_DEPTH, dtype=jnp.float32)[None, :, None] * SIDE + zeros
    coord_x = space_anchor + site_x.astype(jnp.float32)[None, None, :] + 0.5
    coord_y = zeros + site_y.astype(jnp.float32)[None, None, :] + 0.5
    coord_z = depth_anchor + site_z.astype(jnp.float32)[None, None, :] + 0.5
    lattice = jnp.stack([coord_x, coord_y, coord_z], 0)
    return LATTICE_STEP * (lattice + jitter)


def draw_neighbours(key, part):
    entries, drawn = neighbour_plan(key)
    return entries


def draw_counts(key, part):
    entries, drawn = neighbour_plan(key)
    return drawn


def with_ends(values, rng, smallest, high):
    shape = values.shape
    index_at = [jax.random.randint(jax.random.fold_in(rng, axis), (), 0, shape[axis]) for axis in range(len(shape))]
    values = values.at[tuple(index_at)].set(smallest)
    longest = shape.index(max(shape))
    index_at[longest] = (index_at[longest] + 1) % shape[longest]
    return values.at[tuple(index_at)].set(high)


def centred(own_key, extent, scale, most, kind=jnp.bfloat16):
    values = scale * jax.random.normal(own_key, extent, jnp.float32)
    return jnp.clip(values, min=-most, max=most).astype(kind)


def setup_inputs(seed: int = 0) -> dict:
    key_of = jax.random.split(jax.random.key(seed), 12)
    positions = draw_positions(jax.random.fold_in(key_of[11], 71), 0)
    species = with_ends(jax.random.randint(key_of[1], (SPACE_BLOCKS, DEPTH_BLOCKS, ATOMS), 0, SPECIES), jax.random.fold_in(key_of[1], 1), 0, SPECIES - 1).astype(jnp.int32)
    neighbours = draw_neighbours(jax.random.fold_in(key_of[11], 71), 0)
    counts = draw_counts(jax.random.fold_in(key_of[11], 71), 0)
    species_table = centred(key_of[4], (SPECIES, EMB), 1.0, 6.0)
    w_two_in = centred(key_of[5], (IN, HID), IN ** -0.5, 0.5)
    w_two_out = centred(key_of[6], (HID, LAT), HID ** -0.5, 0.375)
    w_env = centred(key_of[7], (LAT, TENS), LAT ** -0.5, 0.75)
    w_lat_in = centred(key_of[8], (LAT + TENS, HID), (LAT + TENS) ** -0.5, 0.625)
    w_lat_out = centred(key_of[9], (HID, LAT), HID ** -0.5, 0.375)
    readout = centred(key_of[10], (LAT,), LAT ** -0.5, 0.75, jnp.float32)
    return dict(positions=positions, species=species, neighbours=neighbours, counts=counts, species_table=species_table, w_two_in=w_two_in, w_two_out=w_two_out, w_env=w_env, w_lat_in=w_lat_in, w_lat_out=w_lat_out, readout=readout)


CUTOFF_RADIUS = 5.0
SOFT_CORE = 0.25

def local_energy(center, nbr_pos, emb_center, emb_nbr, live_mask, w_two_in, w_two_out, w_env, w_lat_in, w_lat_out, readout):
    slot_count, atom_width = live_mask.shape
    edge_count = slot_count * atom_width
    relative = nbr_pos - center[:, None, :]
    squared = lax.optimization_barrier(jnp.sum(relative * relative, axis=0))
    distance = jnp.sqrt(squared + SOFT_CORE)
    direction = relative / distance[None]
    fraction = jnp.minimum(distance / CUTOFF_RADIUS, 1.0)
    cutoff = (1.0 - fraction * fraction) * (1.0 - fraction * fraction)
    basis_count = w_two_in.shape[0] - 2 * emb_center.shape[0]
    centers = jnp.arange(basis_count, dtype=jnp.float32) * (CUTOFF_RADIUS / (basis_count - 1))
    sharpness = ((basis_count - 1) / CUTOFF_RADIUS) ** 2
    spread = distance[None] - centers[:, None, None]
    radial = jnp.exp(-sharpness * spread * spread).astype(jnp.bfloat16)
    features = jnp.concatenate([jnp.broadcast_to(emb_center[:, None, :], emb_nbr.shape), emb_nbr, radial], 0).reshape(-1, edge_count)
    hidden_one = jax.nn.silu(jnp.dot(w_two_in.T, features, preferred_element_type=jnp.float32)).astype(jnp.bfloat16)
    latent_zero = jnp.dot(w_two_out.T, hidden_one, preferred_element_type=jnp.float32) * cutoff.reshape(1, edge_count)
    latent_bf = latent_zero.astype(jnp.bfloat16)
    amplitude = jnp.dot(w_env.T, latent_bf, preferred_element_type=jnp.float32).reshape(-1, slot_count, atom_width) * live_mask[None]
    harmonic = jnp.concatenate([jnp.ones_like(distance)[None], direction], 0)
    product = amplitude[:, None] * harmonic[None]
    environ = lax.optimization_barrier(jnp.sum(product, axis=2)) / jnp.float32(slot_count)
    scalars = lax.optimization_barrier(jnp.sum(product * environ[:, :, None, :], axis=1)).astype(jnp.bfloat16)
    joined = jnp.concatenate([latent_bf, scalars.reshape(-1, edge_count)], 0)
    hidden_two = jax.nn.silu(jnp.dot(w_lat_in.T, joined, preferred_element_type=jnp.float32)).astype(jnp.bfloat16)
    latent_one = latent_zero + jnp.dot(w_lat_out.T, hidden_two, preferred_element_type=jnp.float32)
    pair_energy = lax.optimization_barrier(jnp.sum(readout[:, None] * latent_one, axis=0)).reshape(slot_count, atom_width)
    return pair_energy * cutoff * live_mask

def device_terms(center, halo_pos, emb_center, halo_emb, neighbour_index, count_row, weights):
    slot_count, atom_count = neighbour_index.shape
    flat_index = neighbour_index.reshape(-1).astype(jnp.int32)
    nbr_pos = jnp.take(halo_pos, flat_index, axis=1).reshape(3, slot_count, atom_count)
    emb_nbr = jnp.take(halo_emb, flat_index, axis=1).reshape(-1, slot_count, atom_count)
    live_mask = (jnp.arange(slot_count, dtype=jnp.int32)[:, None] < count_row[None, :]).astype(jnp.float32)

    def energy_sum(center_arg, nbr_arg):
        pair_energy = local_energy(center_arg, nbr_arg, emb_center, emb_nbr, live_mask, *weights)
        return (jnp.sum(pair_energy), pair_energy)
    result, pullback, pair_energy = jax.vjp(energy_sum, center, nbr_pos, has_aux=True)
    grad_center, grad_nbr = pullback(jnp.ones_like(result))
    relative = nbr_pos - center[:, None, :]
    virial_sum = -lax.optimization_barrier(jnp.sum(relative[:, None] * grad_nbr[None], axis=(2, 3)))
    ghalo = jnp.zeros((3, 9 * atom_count), jnp.float32).at[:, flat_index].add(grad_nbr.reshape(3, -1))
    ghalo = ghalo.reshape(3, 3, 3, atom_count).at[:, 1, 1, :].add(grad_center)
    return (ghalo, lax.optimization_barrier(jnp.sum(pair_energy, axis=0)), virial_sum)

def reference(positions, species, neighbours, counts, species_table, w_two_in, w_two_out, w_env, w_lat_in, w_lat_out, readout):
    weights = (w_two_in, w_two_out, w_env, w_lat_in, w_lat_out, readout)
    space_count = positions.shape[1]
    depth_count = positions.shape[2]
    atom_count = positions.shape[3]
    emb_all = jnp.transpose(species_table[species], (3, 0, 1, 2))
    padded_pos = jnp.pad(positions, ((0, 0), (1, 1), (1, 1), (0, 0)))
    padded_emb = jnp.pad(emb_all, ((0, 0), (1, 1), (1, 1), (0, 0)))
    emb_width = emb_all.shape[0]

    def one_device(device):
        space_pos = (device // depth_count).astype(jnp.int32)
        depth_pos = (device % depth_count).astype(jnp.int32)
        zero = jnp.zeros((), jnp.int32)
        halo_pos = lax.dynamic_slice(padded_pos, (zero, space_pos, depth_pos, zero), (3, 3, 3, atom_count)).reshape(3, 9 * atom_count)
        halo_emb = lax.dynamic_slice(padded_emb, (zero, space_pos, depth_pos, zero), (emb_width, 3, 3, atom_count)).reshape(emb_width, 9 * atom_count)
        center = lax.dynamic_slice(positions, (zero, space_pos, depth_pos, zero), (3, 1, 1, atom_count)).reshape(3, atom_count)
        emb_center = lax.dynamic_slice(emb_all, (zero, space_pos, depth_pos, zero), (emb_width, 1, 1, atom_count)).reshape(emb_width, atom_count)
        slot_count = neighbours.shape[0]
        neighbour_index = lax.dynamic_slice(neighbours, (zero, space_pos, depth_pos, zero), (slot_count, 1, 1, atom_count)).reshape(slot_count, atom_count)
        count_row = lax.dynamic_slice(counts, (space_pos, depth_pos, zero), (1, 1, atom_count)).reshape(atom_count)
        return device_terms(center, halo_pos, emb_center, halo_emb, neighbour_index, count_row, weights)
    ghalo, energies, virials = lax.map(one_device, jnp.arange(space_count * depth_count, dtype=jnp.int32))
    grad_grid = ghalo.reshape(space_count, depth_count, 3, 3, 3, atom_count)
    accumulated = jnp.zeros((3, space_count + 2, depth_count + 2, atom_count), jnp.float32)
    for row_offset in range(3):
        for col_offset in range(3):
            moved = jnp.transpose(grad_grid[:, :, :, row_offset, col_offset, :], (2, 0, 1, 3))
            accumulated = accumulated.at[:, row_offset:row_offset + space_count, col_offset:col_offset + depth_count, :].add(moved)
    forces = -accumulated[:, 1:-1, 1:-1, :]
    atom_energy = energies.reshape(space_count, depth_count, atom_count)
    virial = lax.optimization_barrier(jnp.sum(virials, axis=0))
    return (forces, atom_energy, virial)
```

```python
import functools

import jax
import jax.numpy as jnp
from jax import lax
from jax.experimental import pallas as pl
from jax.experimental.pallas import tpu as pltpu
from jax.sharding import PartitionSpec as P

CUTOFF_RADIUS = 5.0
SOFT_CORE = 0.25
SIDE_LENGTH = 32.0
SPREAD = 36.0
GAP = 48
SPAN = 144
LANES = 256


def pieces(value, count):
    parts = []
    rest = value
    for _ in range(count):
        part = rest.astype(jnp.bfloat16)
        parts.append(part)
        rest = rest - part.astype(jnp.float32)
    return parts


def matmul(left, right):
    return jnp.dot(left, right, preferred_element_type=jnp.float32)


def matmul_nt(left, right):
    return lax.dot_general(
        left, right, (((1,), (1,)), ((), ())), preferred_element_type=jnp.float32
    )


def edge_kernel(
    tile,
    members,
    place_ref,
    halo_ref,
    center_ref,
    index_ref,
    count_ref,
    emb_ref,
    w_two_in_ref,
    w_two_out_ref,
    w_env_ref,
    w_lat_in_ref,
    w_lat_out_ref,
    readout_ref,
    ghalo_ref,
    gcenter_ref,
    energy_ref,
    virial_ref,
    table,
    first_w,
    two_out_t,
    env_t,
    lat_in_t,
    lat_back,
    energy_w,
    radial_w,
    readout_col,
    picked,
    low_hot,
    radial_s,
    slope_s,
    slope_one,
    raw_s,
    latent_s,
    amp_s,
    mix_s,
    glat_s,
    harm_s,
    envs,
    genvs,
    rows_s,
    virial_s,
):
    slots, atoms = index_ref.shape
    tiles = atoms // tile
    rows = halo_ref.shape[1]
    f32, bf16 = jnp.float32, jnp.bfloat16
    base_space = place_ref[0]
    base_depth = place_ref[1]

    w_one = w_two_in_ref[...]
    emb = emb_ref[...]
    center_part = matmul(emb, w_one[0:64])
    nbr_part = matmul(emb, w_one[64:128])
    species_part = 0.5 * jnp.concatenate([center_part, nbr_part], 0)
    radial_half = 0.5 * w_one[128:136].astype(f32)
    split = [part.astype(f32) for part in pieces(species_part, 3)]
    first_w[...] = jnp.concatenate([radial_half] + split, 0).T.astype(bf16)
    radial_w[...] = jnp.concatenate([radial_half, jnp.zeros_like(radial_half)], 0).astype(bf16)
    two_out_t[...] = w_two_out_ref[...].astype(f32).T.astype(bf16)
    env_t[...] = w_env_ref[...].astype(f32).T.astype(bf16)
    lat_in = w_lat_in_ref[...].astype(f32)
    lat_in_t[...] = (0.5 * lat_in).T.astype(bf16)
    readout_row = readout_ref[...]
    last_row = lax.dot_general(
        jnp.broadcast_to(readout_row, (8, readout_row.shape[1])),
        w_lat_out_ref[...].astype(f32),
        (((1,), (1,)), ((), ())),
        precision=lax.Precision.HIGHEST,
        preferred_element_type=f32,
    )
    lat_back[...] = (0.5 * lat_in * last_row[0:1]).astype(bf16)
    parts = [part.astype(f32)[0:1] for part in pieces(last_row, 3)]
    energy_w[...] = jnp.concatenate(
        parts + [jnp.zeros((13, last_row.shape[1]), f32)], 0
    ).astype(bf16)
    readout_col[...] = jnp.broadcast_to(readout_row, (8, readout_row.shape[1])).T

    row_id = lax.broadcasted_iota(jnp.int32, (rows, LANES), 0)
    space_of = (row_id // GAP - 1 + base_space).astype(f32)
    depth_of = (lax.rem(row_id, GAP) // 16 - 1 + base_depth).astype(f32)
    half = SIDE_LENGTH / 2
    local = [
        halo_ref[0] - (SIDE_LENGTH * space_of + half),
        halo_ref[1] - half + SPREAD * (halo_ref[3] - 1.5),
        halo_ref[2] - (SIDE_LENGTH * depth_of + half),
    ]
    for axis in range(3):
        high, low = pieces(local[axis], 2)
        table[axis, :, 0:LANES] = high
        table[axis, :, LANES : 2 * LANES] = low

    ghalo_ref[...] = jnp.zeros_like(ghalo_ref)
    picked[...] = jnp.zeros_like(picked)
    rows_s[...] = jnp.zeros_like(rows_s)
    virial_s[...] = jnp.zeros_like(virial_s)

    def one_tile(step, carry):
        member = step // (tiles // members)
        table_row = pl.multiple_of(member * GAP, 16)
        lanes = pl.ds(pl.multiple_of(step * tile, tile), tile)
        count_row = count_ref[:, lanes]
        depth = jnp.max(count_row.astype(f32)).astype(jnp.int32)
        center_x = center_ref[0:1, lanes] - (
            SIDE_LENGTH * (base_space + member).astype(f32) + half
        )
        center_y = center_ref[1:2, lanes] - half
        center_z = center_ref[2:3, lanes] - (SIDE_LENGTH * base_depth.astype(f32) + half)
        center_species = center_ref[3:4, lanes]

        def gather(slot, carry):
            entry = index_ref[pl.ds(slot, 1), lanes]
            low_part = lax.bitwise_and(entry, LANES - 1)
            high_part = lax.shift_right_logical(entry, 8)
            hot = (
                lax.broadcasted_iota(jnp.int32, (LANES, tile), 0) == low_part
            ).astype(f32).astype(bf16)
            low_hot[slot] = hot
            both = jnp.concatenate([hot, hot], 0)
            mask = lax.broadcasted_iota(jnp.int32, (SPAN, tile), 0) == high_part
            for axis in range(3):
                found = matmul(table[axis, pl.ds(table_row, SPAN), :], both)
                picked[axis, pl.ds(slot, 1), :] = jnp.sum(
                    jnp.where(mask, found, 0.0), axis=0, keepdims=True
                )
            return carry

        lax.fori_loop(0, depth, gather, 0)

        entries = index_ref[:, lanes]
        block_space = entries // 12288
        block_depth = lax.rem(entries // 4096, 3)
        coded = picked[1] + (1.5 * SPREAD + SPREAD / 2)
        nbr_species = jnp.floor(coded * (1.0 / SPREAD))
        nbr_y = picked[1] - SPREAD * (nbr_species - 1.5)
        rel = [
            picked[0] + SIDE_LENGTH * (block_space - 1).astype(f32) - center_x,
            nbr_y - center_y,
            picked[2] + SIDE_LENGTH * (block_depth - 1).astype(f32) - center_z,
        ]
        squared = rel[0] * rel[0] + rel[1] * rel[1] + rel[2] * rel[2]
        inverse = lax.rsqrt(squared + SOFT_CORE)
        distance = (squared + SOFT_CORE) * inverse
        direction = [part * inverse for part in rel]
        fraction = jnp.minimum(distance / CUTOFF_RADIUS, 1.0)
        shell = 1.0 - fraction * fraction
        cutoff = shell * shell
        live = (
            lax.broadcasted_iota(jnp.int32, (slots, tile), 0) < count_row
        ).astype(f32)
        for axis in range(3):
            harm_s[axis] = direction[axis]
        harm_s[3] = cutoff
        harm_s[4] = live
        harm_s[5] = nbr_species
        harm_s[6] = distance
        for part in range(4):
            envs[part] = jnp.zeros(envs.shape[1:], f32)
            genvs[part] = jnp.zeros(genvs.shape[1:], f32)

        basis_id = lax.broadcasted_iota(jnp.int32, (8, tile), 0).astype(f32)
        spots = basis_id * (CUTOFF_RADIUS / 7)
        sharpness = (7 / CUTOFF_RADIUS) ** 2
        hot_row = lax.broadcasted_iota(jnp.int32, (8, tile), 0).astype(f32)

        def first(slot, carry):
            one = pl.ds(slot, 1)
            spread = harm_s[6, one, :] - spots
            radial = jnp.exp(-sharpness * spread * spread)
            radial_s[slot] = radial * (-2.0 * sharpness * spread)
            species_hot = jnp.where(
                hot_row < 4.0,
                (hot_row == center_species).astype(f32),
                (hot_row - 4.0 == harm_s[5, one, :]).astype(f32),
            )
            features = jnp.concatenate([radial, species_hot, species_hot, species_hot], 0)
            pre = matmul(first_w[...], features.astype(bf16))
            bent = jnp.tanh(pre)
            mixed = pre * bent
            hidden = (pre + mixed).astype(bf16)
            slope_one[slot] = ((1.0 + bent) * (1.0 + (pre - mixed))).astype(bf16)
            raw = matmul(two_out_t[...], hidden)
            raw_s[slot] = raw
            latent = raw * harm_s[3, one, :]
            latent_b = latent.astype(bf16)
            latent_s[slot] = latent_b
            amp = matmul(env_t[...], latent_b) * harm_s[4, one, :]
            amp_s[slot] = amp
            envs[0] += amp
            for axis in range(3):
                envs[1 + axis] += amp * harm_s[axis, one, :]
            return carry

        lax.fori_loop(0, depth, first, 0)
        for part in range(4):
            envs[part] = envs[part] * (1.0 / slots)

        def second(slot, carry):
            one = pl.ds(slot, 1)
            amp = amp_s[slot]
            ways = [harm_s[axis, one, :] for axis in range(3)]
            mix = envs[0] + envs[1] * ways[0] + envs[2] * ways[1] + envs[3] * ways[2]
            scalars = (amp * mix).astype(bf16)
            joined = jnp.concatenate([latent_s[slot], scalars], 0)
            pre = matmul(lat_in_t[...], joined)
            bent = jnp.tanh(pre)
            mixed = pre * bent
            hidden = (pre + mixed).astype(bf16)
            slope = ((1.0 + bent) * (1.0 + (pre - mixed))).astype(bf16)
            rest = jnp.sum(matmul(energy_w[...], hidden), axis=0, keepdims=True)
            cutoff_row = harm_s[3, one, :]
            weight = cutoff_row * harm_s[4, one, :]
            line = jnp.sum(readout_col[:, 0:1] * raw_s[slot], axis=0, keepdims=True)
            rows_s[0, one, :] = line * cutoff_row + rest
            back = matmul(lat_back[...], slope) * weight
            glat_s[slot] = back[0:64]
            gscal = back[64:96]
            mix_s[slot] = gscal * mix
            gprod = gscal * amp
            genvs[0] += gprod
            for axis in range(3):
                genvs[1 + axis] += gprod * ways[axis]
                rows_s[1 + axis, one, :] = jnp.sum(gprod * envs[1 + axis], axis=0, keepdims=True)
            return carry

        lax.fori_loop(0, depth, second, 0)
        for part in range(4):
            genvs[part] = genvs[part] * (1.0 / slots)

        def third(slot, carry):
            one = pl.ds(slot, 1)
            amp = amp_s[slot]
            ways = [harm_s[axis, one, :] for axis in range(3)]
            live_row = harm_s[4, one, :]
            cutoff_row = harm_s[3, one, :]
            gamp = (
                mix_s[slot]
                + genvs[0]
                + genvs[1] * ways[0]
                + genvs[2] * ways[1]
                + genvs[3] * ways[2]
            ) * live_row
            for axis in range(3):
                rows_s[1 + axis, one, :] += jnp.sum(amp * genvs[1 + axis], axis=0, keepdims=True)
            glat = (
                glat_s[slot]
                + matmul(w_env_ref[...], gamp.astype(bf16))
                + readout_col[:, 0:1] * (cutoff_row * live_row)
            )
            rows_s[4, one, :] = jnp.sum(glat * raw_s[slot], axis=0, keepdims=True)
            ghidden = matmul(w_two_out_ref[...], (glat * cutoff_row).astype(bf16))
            gpre = (ghidden * slope_one[slot].astype(f32)).astype(bf16)
            gradial = matmul(radial_w[...], gpre)[0:8]
            rows_s[5, one, :] = jnp.sum(gradial * radial_s[slot], axis=0, keepdims=True)
            return carry

        lax.fori_loop(0, depth, third, 0)

        total = rows_s[0]
        energy_ref[:, lanes] = jnp.sum(
            jnp.where(live > 0.0, total * cutoff, 0.0), axis=0, keepdims=True
        )
        gcut = rows_s[4] + total * live
        gdist = rows_s[5] - gcut * shell * fraction * (4.0 / CUTOFF_RADIUS)
        gdir = [rows_s[1 + axis] for axis in range(3)]
        along = gdir[0] * direction[0] + gdir[1] * direction[1] + gdir[2] * direction[2]
        push = gdist - along * inverse
        grel = [
            jnp.where(live > 0.0, gdir[axis] * inverse + direction[axis] * push, 0.0)
            for axis in range(3)
        ]
        for axis in range(3):
            gcenter_ref[axis : axis + 1, lanes] = -jnp.sum(grel[axis], axis=0, keepdims=True)
            picked[axis] = grel[axis]
            for other in range(3):
                virial_s[3 * axis + other] += rel[axis] * grel[other]

        def scatter(slot, carry):
            one = pl.ds(slot, 1)
            entry = index_ref[one, lanes]
            high_part = lax.shift_right_logical(entry, 8)
            mask = lax.broadcasted_iota(jnp.int32, (SPAN, tile), 0) == high_part
            hot = low_hot[slot]
            for axis in range(3):
                spread = jnp.where(mask, picked[axis, one, :], 0.0).astype(bf16)
                ghalo_ref[axis, pl.ds(table_row, SPAN), :] += matmul_nt(spread, hot)
            return carry

        lax.fori_loop(0, depth, scatter, 0)
        return carry

    lax.fori_loop(0, tiles, one_tile, 0)
    for entry in range(9):
        folded = jnp.sum(virial_s[entry], axis=0, keepdims=True)
        part = folded[:, 0:128]
        for chunk in range(1, tile // 128):
            part = part + folded[:, 128 * chunk : 128 * (chunk + 1)]
        virial_ref[entry : entry + 1, :] = -part
    virial_ref[9:16, :] = jnp.zeros((7, 128), f32)


def edge_call(place, halo, center, index, count, weights, tile, members):
    slots, atoms = index.shape
    rows = halo.shape[1]
    f32, bf16 = jnp.float32, jnp.bfloat16
    vmem = pl.BlockSpec(memory_space=pltpu.VMEM)
    shapes = (
        jax.ShapeDtypeStruct((3, rows, LANES), f32),
        jax.ShapeDtypeStruct((3, atoms), f32),
        jax.ShapeDtypeStruct((1, atoms), f32),
        jax.ShapeDtypeStruct((16, 128), f32),
    )
    scratch = [
        pltpu.VMEM((3, rows, 2 * LANES), bf16),
        pltpu.VMEM((256, 32), bf16),
        pltpu.VMEM((64, 256), bf16),
        pltpu.VMEM((32, 64), bf16),
        pltpu.VMEM((256, 96), bf16),
        pltpu.VMEM((96, 256), bf16),
        pltpu.VMEM((16, 256), bf16),
        pltpu.VMEM((16, 256), bf16),
        pltpu.VMEM((64, 8), f32),
        pltpu.VMEM((3, slots, tile), f32),
        pltpu.VMEM((slots, LANES, tile), bf16),
        pltpu.VMEM((slots, 8, tile), f32),
        pltpu.VMEM((8, 8, tile), f32),
        pltpu.VMEM((slots, 256, tile), bf16),
        pltpu.VMEM((slots, 64, tile), f32),
        pltpu.VMEM((slots, 64, tile), bf16),
        pltpu.VMEM((slots, 32, tile), f32),
        pltpu.VMEM((slots, 32, tile), f32),
        pltpu.VMEM((slots, 64, tile), f32),
        pltpu.VMEM((8, slots, tile), f32),
        pltpu.VMEM((4, 32, tile), f32),
        pltpu.VMEM((4, 32, tile), f32),
        pltpu.VMEM((6, slots, tile), f32),
        pltpu.VMEM((9, slots, tile), f32),
    ]
    return pl.pallas_call(
        functools.partial(edge_kernel, tile, members),
        out_shape=shapes,
        in_specs=[pl.BlockSpec(memory_space=pltpu.SMEM)] + [vmem] * 11,
        out_specs=(vmem,) * 4,
        scratch_shapes=scratch,
        compiler_params=pltpu.CompilerParams(vmem_limit_bytes=48 * 1024 * 1024),
    )(place, halo, center, index, count, *weights)


def with_halo(block, sides, width):
    for axis, dim in sides:
        count = lax.axis_size(axis)
        forward = [(i, i + 1) for i in range(count - 1)]
        backward = [(target, source) for source, target in forward]
        low = lax.ppermute(
            lax.slice_in_dim(block, block.shape[dim] - width, None, axis=dim), axis, forward
        )
        high = lax.ppermute(lax.slice_in_dim(block, 0, width, axis=dim), axis, backward)
        block = jnp.concatenate([low, block, high], axis=dim)
    return block


def passed_along(block, axis, distance):
    devices = range(lax.axis_size(axis))
    route = [(i - distance, i) for i in devices if i - distance in devices]
    return lax.ppermute(block, axis, route)


def per_device(
    positions,
    species,
    neighbours,
    counts,
    species_table,
    w_two_in,
    w_two_out,
    w_env,
    w_lat_in,
    w_lat_out,
    readout,
):
    atom_count = positions.shape[-1]
    slot_count = neighbours.shape[0]
    species_value = species.astype(jnp.float32)
    packed = jnp.concatenate([positions, species_value[None]], 0)
    halo = with_halo(packed, (("space", 1), ("depth", 2)), 1)
    halo = halo.reshape(4, 9 * atom_count // LANES, LANES)
    place = jnp.stack([lax.axis_index("space"), lax.axis_index("depth")]).astype(jnp.int32)
    weights = (
        species_table,
        w_two_in,
        w_two_out,
        w_env,
        w_lat_in,
        w_lat_out,
        readout.reshape(1, -1),
    )
    ghalo, gcenter, energies, virial_part = edge_call(
        place,
        halo,
        packed.reshape(4, atom_count),
        neighbours.reshape(slot_count, atom_count),
        counts.reshape(1, atom_count),
        weights,
        1024,
        1,
    )
    virial_total = lax.psum(jnp.sum(virial_part[0:9], axis=1), ("space", "depth")).reshape(3, 3)
    grad_grid = ghalo.reshape(3, 3, 3, atom_count)
    summed = grad_grid[:, 1, 1] + gcenter
    for step_space in (-1, 0, 1):
        for step_depth in (-1, 0, 1):
            if step_space == 0 and step_depth == 0:
                continue
            moved = grad_grid[:, 1 + step_space, 1 + step_depth]
            if step_space != 0:
                moved = passed_along(moved, "space", step_space)
            if step_depth != 0:
                moved = passed_along(moved, "depth", step_depth)
            summed = summed + moved
    forces = (-summed).reshape(3, 1, 1, atom_count)
    atom_energy = energies.reshape(1, 1, atom_count)
    return (forces, atom_energy, virial_total)


def solution(mesh):
    placed = (
        P(None, "space", "depth", None),
        P("space", "depth", None),
        P(None, "space", "depth", None),
        P("space", "depth", None),
        P(),
        P(),
        P(),
        P(),
        P(),
        P(),
        P(),
    )
    return jax.shard_map(
        per_device,
        mesh=mesh,
        in_specs=placed,
        out_specs=(P(None, "space", "depth", None), P("space", "depth", None), P()),
        check_vma=False,
    )
```

```python
import functools

import jax
import jax.numpy as jnp
from jax import lax
from jax.experimental import pallas as pl
from jax.experimental.pallas import tpu as pltpu
from jax.sharding import PartitionSpec as P

CUTOFF_RADIUS = 5.0
SOFT_CORE = 0.25

GROUP = 4
TILE = 1024
SIDE_LENGTH = 32.0
SPREAD = 36.0
GAP = 48
SPAN = 144
LANES = 256


def pieces(value, count):
    parts = []
    rest = value
    for _ in range(count):
        part = rest.astype(jnp.bfloat16)
        parts.append(part)
        rest = rest - part.astype(jnp.float32)
    return parts


def matmul(left, right):
    return jnp.dot(left, right, preferred_element_type=jnp.float32)


def matmul_nt(left, right):
    return lax.dot_general(
        left, right, (((1,), (1,)), ((), ())), preferred_element_type=jnp.float32
    )


def edge_kernel(
    tile,
    members,
    place_ref,
    halo_ref,
    center_ref,
    index_ref,
    emb_ref,
    w_two_in_ref,
    w_two_out_ref,
    w_env_ref,
    w_lat_in_ref,
    w_lat_out_ref,
    readout_ref,
    ghalo_ref,
    back_ref,
    virial_ref,
    table,
    first_w,
    two_out_t,
    env_t,
    lat_in_t,
    lat_back,
    energy_w,
    radial_w,
    readout_col,
    picked,
    low_hot,
    radial_s,
    slope_s,
    slope_one,
    raw_s,
    latent_s,
    amp_s,
    mix_s,
    glat_s,
    harm_s,
    envs,
    genvs,
    rows_s,
    virial_s,
):
    slots, atoms = index_ref.shape
    tiles = atoms // tile
    rows = halo_ref.shape[1]
    f32, bf16 = jnp.float32, jnp.bfloat16
    base_space = place_ref[0]
    base_depth = place_ref[1]

    w_one = w_two_in_ref[...]
    emb = emb_ref[...]
    center_part = matmul(emb, w_one[0:64])
    nbr_part = matmul(emb, w_one[64:128])
    species_part = 0.5 * jnp.concatenate([center_part, nbr_part], 0)
    radial_half = 0.5 * w_one[128:136].astype(f32)
    split = [part.astype(f32) for part in pieces(species_part, 3)]
    first_w[...] = jnp.concatenate([radial_half] + split, 0).T.astype(bf16)
    radial_w[...] = jnp.concatenate([radial_half, jnp.zeros_like(radial_half)], 0).astype(bf16)
    two_out_t[...] = w_two_out_ref[...].astype(f32).T.astype(bf16)
    env_t[...] = w_env_ref[...].astype(f32).T.astype(bf16)
    lat_in = w_lat_in_ref[...].astype(f32)
    lat_in_t[...] = (0.5 * lat_in).T.astype(bf16)
    readout_row = readout_ref[...]
    last_row = lax.dot_general(
        jnp.broadcast_to(readout_row, (8, readout_row.shape[1])),
        w_lat_out_ref[...].astype(f32),
        (((1,), (1,)), ((), ())),
        precision=lax.Precision.HIGHEST,
        preferred_element_type=f32,
    )
    lat_back[...] = (0.5 * lat_in * last_row[0:1]).astype(bf16)
    parts = [part.astype(f32)[0:1] for part in pieces(last_row, 3)]
    energy_w[...] = jnp.concatenate(
        parts + [jnp.zeros((13, last_row.shape[1]), f32)], 0
    ).astype(bf16)
    readout_col[...] = jnp.broadcast_to(readout_row, (8, readout_row.shape[1])).T

    row_id = lax.broadcasted_iota(jnp.int32, (rows, LANES), 0)
    space_of = (row_id // GAP - 1 + base_space).astype(f32)
    depth_of = (lax.rem(row_id, GAP) // 16 - 1 + base_depth).astype(f32)
    half = SIDE_LENGTH / 2
    local = [
        halo_ref[0] - (SIDE_LENGTH * space_of + half),
        halo_ref[1] - half + SPREAD * (halo_ref[3] - 1.5),
        halo_ref[2] - (SIDE_LENGTH * depth_of + half),
    ]
    for axis in range(3):
        high, low = pieces(local[axis], 2)
        table[axis, :, 0:LANES] = high
        table[axis, :, LANES : 2 * LANES] = low

    ghalo_ref[...] = jnp.zeros_like(ghalo_ref)
    back_ref[...] = jnp.zeros_like(back_ref)
    picked[...] = jnp.zeros_like(picked)
    rows_s[...] = jnp.zeros_like(rows_s)
    virial_s[...] = jnp.zeros_like(virial_s)

    def one_tile(step, carry):
        member = step // (tiles // members)
        table_row = pl.multiple_of(member * GAP, 16)
        lanes = pl.ds(pl.multiple_of(step * tile, tile), tile)
        count_row = center_ref[4:5, lanes]
        depth = jnp.max(count_row).astype(jnp.int32)
        count_row = count_row.astype(jnp.int32)
        center_x = center_ref[0:1, lanes] - (
            SIDE_LENGTH * (base_space + member).astype(f32) + half
        )
        center_y = center_ref[1:2, lanes] - half
        center_z = center_ref[2:3, lanes] - (SIDE_LENGTH * base_depth.astype(f32) + half)
        center_species = center_ref[3:4, lanes]

        def gather(slot, carry):
            entry = index_ref[pl.ds(slot, 1), lanes]
            low_part = lax.bitwise_and(entry, LANES - 1)
            high_part = lax.shift_right_logical(entry, 8)
            hot = (
                lax.broadcasted_iota(jnp.int32, (LANES, tile), 0) == low_part
            ).astype(f32).astype(bf16)
            low_hot[slot] = hot
            both = jnp.concatenate([hot, hot], 0)
            mask = lax.broadcasted_iota(jnp.int32, (SPAN, tile), 0) == high_part
            for axis in range(3):
                found = matmul(table[axis, pl.ds(table_row, SPAN), :], both)
                picked[axis, pl.ds(slot, 1), :] = jnp.sum(
                    jnp.where(mask, found, 0.0), axis=0, keepdims=True
                )
            return carry

        lax.fori_loop(0, depth, gather, 0)

        entries = index_ref[:, lanes]
        block_space = entries // 12288
        block_depth = lax.rem(entries // 4096, 3)
        coded = picked[1] + (1.5 * SPREAD + SPREAD / 2)
        nbr_species = jnp.floor(coded * (1.0 / SPREAD))
        nbr_y = picked[1] - SPREAD * (nbr_species - 1.5)
        rel = [
            picked[0] + SIDE_LENGTH * (block_space - 1).astype(f32) - center_x,
            nbr_y - center_y,
            picked[2] + SIDE_LENGTH * (block_depth - 1).astype(f32) - center_z,
        ]
        squared = rel[0] * rel[0] + rel[1] * rel[1] + rel[2] * rel[2]
        inverse = lax.rsqrt(squared + SOFT_CORE)
        distance = (squared + SOFT_CORE) * inverse
        direction = [part * inverse for part in rel]
        fraction = jnp.minimum(distance / CUTOFF_RADIUS, 1.0)
        shell = 1.0 - fraction * fraction
        cutoff = shell * shell
        live = (
            lax.broadcasted_iota(jnp.int32, (slots, tile), 0) < count_row
        ).astype(f32)
        for axis in range(3):
            harm_s[axis] = direction[axis]
        harm_s[3] = cutoff
        harm_s[4] = live
        harm_s[5] = nbr_species
        harm_s[6] = distance
        for part in range(4):
            envs[part] = jnp.zeros(envs.shape[1:], f32)
            genvs[part] = jnp.zeros(genvs.shape[1:], f32)

        basis_id = lax.broadcasted_iota(jnp.int32, (8, tile), 0).astype(f32)
        spots = basis_id * (CUTOFF_RADIUS / 7)
        sharpness = (7 / CUTOFF_RADIUS) ** 2
        hot_row = lax.broadcasted_iota(jnp.int32, (8, tile), 0).astype(f32)

        def first(slot, carry):
            one = pl.ds(slot, 1)
            spread = harm_s[6, one, :] - spots
            radial = jnp.exp(-sharpness * spread * spread)
            radial_s[slot] = radial * (-2.0 * sharpness * spread)
            species_hot = jnp.where(
                hot_row < 4.0,
                (hot_row == center_species).astype(f32),
                (hot_row - 4.0 == harm_s[5, one, :]).astype(f32),
            )
            features = jnp.concatenate([radial, species_hot, species_hot, species_hot], 0)
            pre = matmul(first_w[...], features.astype(bf16))
            bent = jnp.tanh(pre)
            mixed = pre * bent
            hidden = (pre + mixed).astype(bf16)
            slope_one[slot] = ((1.0 + bent) * (1.0 + (pre - mixed))).astype(bf16)
            raw = matmul(two_out_t[...], hidden)
            raw_s[slot] = raw
            latent = raw * harm_s[3, one, :]
            latent_b = latent.astype(bf16)
            latent_s[slot] = latent_b
            amp = matmul(env_t[...], latent_b) * harm_s[4, one, :]
            amp_s[slot] = amp
            envs[0] += amp
            for axis in range(3):
                envs[1 + axis] += amp * harm_s[axis, one, :]
            return carry

        lax.fori_loop(0, depth, first, 0)
        for part in range(4):
            envs[part] = envs[part] * (1.0 / slots)

        def second(slot, carry):
            one = pl.ds(slot, 1)
            amp = amp_s[slot]
            ways = [harm_s[axis, one, :] for axis in range(3)]
            mix = envs[0] + envs[1] * ways[0] + envs[2] * ways[1] + envs[3] * ways[2]
            scalars = (amp * mix).astype(bf16)
            joined = jnp.concatenate([latent_s[slot], scalars], 0)
            pre = matmul(lat_in_t[...], joined)
            bent = jnp.tanh(pre)
            mixed = pre * bent
            hidden = (pre + mixed).astype(bf16)
            slope = ((1.0 + bent) * (1.0 + (pre - mixed))).astype(bf16)
            rest = jnp.sum(matmul(energy_w[...], hidden), axis=0, keepdims=True)
            cutoff_row = harm_s[3, one, :]
            weight = cutoff_row * harm_s[4, one, :]
            line = jnp.sum(readout_col[:, 0:1] * raw_s[slot], axis=0, keepdims=True)
            rows_s[0, one, :] = line * cutoff_row + rest
            back = matmul(lat_back[...], slope) * weight
            glat_s[slot] = back[0:64]
            gscal = back[64:96]
            mix_s[slot] = gscal * mix
            gprod = gscal * amp
            genvs[0] += gprod
            for axis in range(3):
                genvs[1 + axis] += gprod * ways[axis]
                rows_s[1 + axis, one, :] = jnp.sum(gprod * envs[1 + axis], axis=0, keepdims=True)
            return carry

        lax.fori_loop(0, depth, second, 0)
        for part in range(4):
            genvs[part] = genvs[part] * (1.0 / slots)

        def third(slot, carry):
            one = pl.ds(slot, 1)
            amp = amp_s[slot]
            ways = [harm_s[axis, one, :] for axis in range(3)]
            live_row = harm_s[4, one, :]
            cutoff_row = harm_s[3, one, :]
            gamp = (
                mix_s[slot]
                + genvs[0]
                + genvs[1] * ways[0]
                + genvs[2] * ways[1]
                + genvs[3] * ways[2]
            ) * live_row
            for axis in range(3):
                rows_s[1 + axis, one, :] += jnp.sum(amp * genvs[1 + axis], axis=0, keepdims=True)
            glat = (
                glat_s[slot]
                + matmul(w_env_ref[...], gamp.astype(bf16))
                + readout_col[:, 0:1] * (cutoff_row * live_row)
            )
            rows_s[4, one, :] = jnp.sum(glat * raw_s[slot], axis=0, keepdims=True)
            ghidden = matmul(w_two_out_ref[...], (glat * cutoff_row).astype(bf16))
            gpre = (ghidden * slope_one[slot].astype(f32)).astype(bf16)
            gradial = matmul(radial_w[...], gpre)[0:8]
            rows_s[5, one, :] = jnp.sum(gradial * radial_s[slot], axis=0, keepdims=True)
            return carry

        lax.fori_loop(0, depth, third, 0)

        total = rows_s[0]
        back_ref[3:4, lanes] = jnp.sum(
            jnp.where(live > 0.0, total * cutoff, 0.0), axis=0, keepdims=True
        )
        gcut = rows_s[4] + total * live
        gdist = rows_s[5] - gcut * shell * fraction * (4.0 / CUTOFF_RADIUS)
        gdir = [rows_s[1 + axis] for axis in range(3)]
        along = gdir[0] * direction[0] + gdir[1] * direction[1] + gdir[2] * direction[2]
        push = gdist - along * inverse
        grel = [
            jnp.where(live > 0.0, gdir[axis] * inverse + direction[axis] * push, 0.0)
            for axis in range(3)
        ]
        for axis in range(3):
            back_ref[axis : axis + 1, lanes] = -jnp.sum(grel[axis], axis=0, keepdims=True)
            picked[axis] = grel[axis]
            for other in range(3):
                virial_s[3 * axis + other] += rel[axis] * grel[other]

        def scatter(slot, carry):
            one = pl.ds(slot, 1)
            entry = index_ref[one, lanes]
            high_part = lax.shift_right_logical(entry, 8)
            mask = lax.broadcasted_iota(jnp.int32, (SPAN, tile), 0) == high_part
            hot = low_hot[slot]
            for axis in range(3):
                spread = jnp.where(mask, picked[axis, one, :], 0.0).astype(bf16)
                ghalo_ref[axis, pl.ds(table_row, SPAN), :] += matmul_nt(spread, hot)
            return carry

        lax.fori_loop(0, depth, scatter, 0)
        return carry

    lax.fori_loop(0, tiles, one_tile, 0)
    for entry in range(9):
        folded = jnp.sum(virial_s[entry], axis=0, keepdims=True)
        part = folded[:, 0:128]
        for chunk in range(1, tile // 128):
            part = part + folded[:, 128 * chunk : 128 * (chunk + 1)]
        virial_ref[entry : entry + 1, :] = -part
    virial_ref[9:16, :] = jnp.zeros((7, 128), f32)


def edge_call(place, halo, center, index, weights, tile, members):
    slots, atoms = index.shape
    rows = halo.shape[1]
    f32, bf16 = jnp.float32, jnp.bfloat16
    vmem = pl.BlockSpec(memory_space=pltpu.VMEM)
    shapes = (
        jax.ShapeDtypeStruct((3, rows, LANES), f32),
        jax.ShapeDtypeStruct((8, atoms), f32),
        jax.ShapeDtypeStruct((16, 128), f32),
    )
    scratch = [
        pltpu.VMEM((3, rows, 2 * LANES), bf16),
        pltpu.VMEM((256, 32), bf16),
        pltpu.VMEM((64, 256), bf16),
        pltpu.VMEM((32, 64), bf16),
        pltpu.VMEM((256, 96), bf16),
        pltpu.VMEM((96, 256), bf16),
        pltpu.VMEM((16, 256), bf16),
        pltpu.VMEM((16, 256), bf16),
        pltpu.VMEM((64, 8), f32),
        pltpu.VMEM((3, slots, tile), f32),
        pltpu.VMEM((slots, LANES, tile), bf16),
        pltpu.VMEM((slots, 8, tile), f32),
        pltpu.VMEM((8, 8, tile), f32),
        pltpu.VMEM((slots, 256, tile), bf16),
        pltpu.VMEM((slots, 64, tile), f32),
        pltpu.VMEM((slots, 64, tile), bf16),
        pltpu.VMEM((slots, 32, tile), f32),
        pltpu.VMEM((slots, 32, tile), f32),
        pltpu.VMEM((slots, 64, tile), f32),
        pltpu.VMEM((8, slots, tile), f32),
        pltpu.VMEM((4, 32, tile), f32),
        pltpu.VMEM((4, 32, tile), f32),
        pltpu.VMEM((6, slots, tile), f32),
        pltpu.VMEM((9, slots, tile), f32),
    ]
    return pl.pallas_call(
        functools.partial(edge_kernel, tile, members),
        out_shape=shapes,
        in_specs=[pl.BlockSpec(memory_space=pltpu.SMEM)] + [vmem] * 10,
        out_specs=(vmem,) * 3,
        scratch_shapes=scratch,
        compiler_params=pltpu.CompilerParams(vmem_limit_bytes=48 * 1024 * 1024),
    )(place, halo, center, index, *weights)


def send(source, target, send_sem, recv_sem, space, depth):
    return pltpu.make_async_remote_copy(
        src_ref=source,
        dst_ref=target,
        send_sem=send_sem,
        recv_sem=recv_sem,
        device_id=(space, depth),
        device_id_type=pl.DeviceIdType.MESH,
    )


def greet(space, depth):
    pl.semaphore_signal(
        pltpu.get_barrier_semaphore(),
        inc=1,
        device_id=(space, depth),
        device_id_type=pl.DeviceIdType.MESH,
    )


def where_am_i(group):
    spaces, depths = lax.axis_size("space"), lax.axis_size("depth")
    space, depth = lax.axis_index("space"), lax.axis_index("depth")
    spot = lax.rem(space, group)
    first = space - spot
    before = lax.rem(first - 1 + spaces, spaces)
    after = lax.rem(first + group, spaces)
    return spaces, depths, space, depth, spot, first, before, after


def collect_kernel(
    group,
    position_ref,
    species_ref,
    index_ref,
    count_ref,
    halo_ref,
    center_ref,
    index_out_ref,
    own,
    flat,
    depth_send,
    depth_recv,
    part_send,
    part_recv,
    column_send,
    column_recv,
    edge_send,
    edge_recv,
):
    spaces, depths, space, depth, spot, first, before, after = where_am_i(group)
    atoms = position_ref.shape[1]
    share = atoms // group
    up, down = lax.rem(depth + 1, depths), lax.rem(depth + depths - 1, depths)
    mates = [first + lax.rem(spot + off, group) for off in range(1, group)]
    at_start, at_end = spot == 0, spot == group - 1

    greet(space, up)
    greet(space, down)
    for mate in mates:
        greet(mate, depth)
    greet(before, depth)
    greet(after, depth)
    expected = (
        2 + (group - 1) + group * at_start.astype(jnp.int32) + group * at_end.astype(jnp.int32)
    )

    flat[0:3, :] = position_ref[...]
    flat[3:4, :] = species_ref[...].astype(jnp.float32)
    flat[4:5, :] = count_ref[...].astype(jnp.float32)
    flat[5:8, :] = jnp.zeros((3, atoms), jnp.float32)
    for part in range(4):
        for row in range(atoms // LANES):
            own[part, row : row + 1, :] = flat[part : part + 1, row * LANES : (row + 1) * LANES]
    pl.semaphore_wait(pltpu.get_barrier_semaphore(), expected)

    column = pl.multiple_of((spot + 1) * GAP, 16)
    low, middle, high = (
        halo_ref.at[:, pl.ds(pl.multiple_of(column + 16 * part, 16), 16), :] for part in range(3)
    )
    depth_copies = [
        send(own, low, depth_send.at[0], depth_recv.at[0], space, up),
        send(own, high, depth_send.at[1], depth_recv.at[1], space, down),
    ]
    for copy in depth_copies:
        copy.start()
    mine = pl.ds(pl.multiple_of(spot * share, 128), share)
    part_copies = []
    for off in range(1, group):
        theirs = pl.ds(off * share, share)
        for kind, (source, target) in enumerate(((index_ref, index_out_ref), (flat, center_ref))):
            slot = 2 * (off - 1) + kind
            copy = send(
                source.at[:, theirs],
                target.at[:, mine],
                part_send.at[slot],
                part_recv.at[slot],
                mates[off - 1],
                depth,
            )
            copy.start()
            part_copies.append(copy)
    middle[...] = own[...]
    index_out_ref[:, mine] = index_ref[:, 0:share]
    center_ref[:, mine] = flat[:, 0:share]
    for copy in depth_copies:
        copy.wait_recv()

    source = halo_ref.at[:, pl.ds(column, GAP), :]
    column_copies = []
    for off in range(1, group):
        copy = send(
            source, source, column_send.at[off - 1], column_recv.at[off - 1], mates[off - 1], depth
        )
        copy.start()
        column_copies.append(copy)

    first_column = halo_ref.at[:, 0:GAP, :]
    last_column = halo_ref.at[:, (group + 1) * GAP : (group + 2) * GAP, :]

    def edges(side):
        base, target = (lax.rem(first - group + spaces, spaces), last_column)
        if side == 1:
            base, target = (after, first_column)
        return [
            send(
                source,
                target,
                edge_send.at[group * side + member],
                edge_recv.at[side],
                base + member,
                depth,
            )
            for member in range(group)
        ]

    for side, here in enumerate((at_start, at_end)):

        @pl.when(here)
        def _(side=side):
            for copy in edges(side):
                copy.start()

    for copy in column_copies:
        copy.wait_recv()
    send(last_column, last_column, edge_send.at[0], edge_recv.at[0], after, depth).wait_recv()
    send(first_column, first_column, edge_send.at[0], edge_recv.at[1], before, depth).wait_recv()
    for copy in part_copies:
        copy.wait_recv()
    for copy in depth_copies + part_copies + column_copies:
        copy.wait_send()
    for side, here in enumerate((at_start, at_end)):

        @pl.when(here)
        def _(side=side):
            for copy in edges(side):
                copy.wait_send()


def collect_call(positions, species, index, count, group):
    slots, atoms = index.shape
    rows = (group + 2) * GAP
    f32 = jnp.float32
    vmem = pl.BlockSpec(memory_space=pltpu.VMEM)
    dma = pltpu.SemaphoreType.DMA
    return pl.pallas_call(
        functools.partial(collect_kernel, group),
        out_shape=(
            jax.ShapeDtypeStruct((4, rows, LANES), f32),
            jax.ShapeDtypeStruct((8, atoms), f32),
            jax.ShapeDtypeStruct((slots, atoms), jnp.int32),
        ),
        in_specs=[vmem] * 4,
        out_specs=(vmem,) * 3,
        scratch_shapes=[
            pltpu.VMEM((4, atoms // LANES, LANES), f32),
            pltpu.VMEM((8, atoms), f32),
            dma((2,)),
            dma((2,)),
            dma((2 * (group - 1),)),
            dma((2 * (group - 1),)),
            dma((group - 1,)),
            dma((group - 1,)),
            dma((2 * group,)),
            dma((2,)),
        ],
        compiler_params=pltpu.CompilerParams(
            collective_id=0, has_side_effects=True, vmem_limit_bytes=24 * 1024 * 1024
        ),
    )(positions, species, index, count)


def return_kernel(
    group,
    ghalo_ref,
    back_ref,
    virial_ref,
    force_ref,
    energy_ref,
    total_ref,
    columns,
    blocks,
    flat,
    summed,
    by_member,
    by_depth,
    by_group,
    column_send,
    column_recv,
    edge_send,
    edge_recv,
    part_send,
    part_recv,
    block_send,
    block_recv,
    member_send,
    member_recv,
    layer_send,
    layer_recv,
    group_send,
    group_recv,
):
    spaces, depths, space, depth, spot, first, before, after = where_am_i(group)
    atoms = back_ref.shape[1]
    share = atoms // group
    groups = spaces // group
    up, down = lax.rem(depth + 1, depths), lax.rem(depth + depths - 1, depths)
    mates = [first + lax.rem(spot + off, group) for off in range(1, group)]
    layers = [lax.rem(depth + off, depths) for off in range(1, depths)]
    peers = [lax.rem(space + off * group, spaces) for off in range(1, groups)]
    at_start, at_end = spot == 0, spot == group - 1

    for mate in mates:
        greet(mate, depth)
    for layer in layers:
        greet(space, layer)
    for peer in peers:
        greet(peer, depth)
    previous = lax.rem(first - group + spaces, spaces)
    for here, base in ((at_start, previous), (at_end, after)):

        @pl.when(here)
        def _(base=base):
            for member in range(group):
                greet(base + member, depth)

    pl.semaphore_wait(
        pltpu.get_barrier_semaphore(), (group - 1) + (depths - 1) + (groups - 1) + 2
    )

    started = []

    def go(*args):
        copy = send(*args)
        copy.start()
        started.append(copy)
        return copy

    by_member[spot] = virial_ref[...]
    mine = by_member.at[spot]
    member_copies = [
        go(mine, mine, member_send.at[off], member_recv.at[off], mate, depth)
        for off, mate in enumerate(mates)
    ]
    column_copies = []
    for off, mate in enumerate(mates):
        theirs = pl.ds(pl.multiple_of((mate - first + 1) * GAP, 16), GAP)
        column_copies.append(
            go(
                ghalo_ref.at[:, theirs, :],
                columns.at[off],
                column_send.at[off],
                column_recv.at[off],
                mate,
                depth,
            )
        )
    for side, (target, start) in enumerate(((before, 0), (after, (group + 1) * GAP))):
        go(
            ghalo_ref.at[:, start : start + GAP, :],
            columns.at[group - 1 + spot],
            edge_send.at[side],
            edge_recv.at[spot],
            target,
            depth,
        )
    part_copies = []
    for off, mate in enumerate(mates):
        theirs = pl.ds(pl.multiple_of((mate - first) * share, 128), share)
        part = (group - 1 - off) * share
        part_copies.append(
            go(
                back_ref.at[:, theirs],
                flat.at[:, part : part + share],
                part_send.at[off],
                part_recv.at[off],
                mate,
                depth,
            )
        )
    own_part = pl.ds(pl.multiple_of(spot * share, 128), share)
    flat[:, 0:share] = back_ref[:, own_part]

    for copy in member_copies:
        copy.wait_recv()
    level = by_member[0]
    for member in range(1, group):
        level = level + by_member[member]
    by_depth[depth] = level
    mine_depth = by_depth.at[depth]
    layer_copies = [
        go(mine_depth, mine_depth, layer_send.at[off], layer_recv.at[off], space, layer)
        for off, layer in enumerate(layers)
    ]
    for copy in layer_copies:
        copy.wait_recv()
    level = by_depth[0]
    for layer in range(1, depths):
        level = level + by_depth[layer]
    place = space // group
    by_group[place] = level
    mine_group = by_group.at[place]
    group_copies = [
        go(mine_group, mine_group, group_send.at[off], group_recv.at[off], peer, depth)
        for off, peer in enumerate(peers)
    ]

    for copy in column_copies:
        copy.wait_recv()
    own_column = pl.ds(pl.multiple_of((spot + 1) * GAP, 16), GAP)
    total = ghalo_ref[:, own_column, :]
    for member in range(group - 1):
        total = total + columns[member]
    summed[...] = total

    @pl.when(jnp.logical_or(at_start, at_end))
    def _():
        for member in range(group):
            slot = group - 1 + member
            send(
                columns.at[slot],
                columns.at[slot],
                edge_send.at[0],
                edge_recv.at[member],
                before,
                depth,
            ).wait_recv()
        extra = columns[group - 1]
        for member in range(1, group):
            extra = extra + columns[group - 1 + member]
        summed[...] = summed[...] + extra

    block_copies = [
        go(summed.at[:, 0:16, :], blocks.at[0], block_send.at[0], block_recv.at[0], space, down),
        go(summed.at[:, 32:48, :], blocks.at[1], block_send.at[1], block_recv.at[1], space, up),
    ]
    for copy in part_copies:
        copy.wait_recv()
    energy_ref[...] = flat[3:4, :]
    for copy in group_copies:
        copy.wait_recv()
    level = by_group[0]
    for member in range(1, groups):
        level = level + by_group[member]
    entries = jnp.sum(level, axis=1, keepdims=True)
    shape = (8, 128)
    row_id = lax.broadcasted_iota(jnp.int32, shape, 0)
    column_id = lax.broadcasted_iota(jnp.int32, shape, 1)
    table = jnp.zeros(shape, jnp.float32)
    for entry in range(9):
        here = jnp.logical_and(row_id == entry // 3, column_id == entry % 3)
        table = jnp.where(here, entries[entry : entry + 1, :], table)
    total_ref[...] = table[0:3, 0:3]
    for copy in block_copies:
        copy.wait_recv()
    blocks[0] = summed[:, 16:32, :] + blocks[0] + blocks[1]
    for part in range(3):
        for row in range(atoms // LANES):
            lanes = slice(row * LANES, (row + 1) * LANES)
            force_ref[part : part + 1, lanes] = -(
                blocks[0, part, row : row + 1, :] + flat[part : part + 1, lanes]
            )
    for copy in started:
        copy.wait_send()


def return_call(ghalo, back, virial, group):
    atoms = back.shape[1]
    f32 = jnp.float32
    depths = lax.axis_size("depth")
    groups = lax.axis_size("space") // group
    vmem = pl.BlockSpec(memory_space=pltpu.VMEM)
    dma = pltpu.SemaphoreType.DMA
    counts = [
        group - 1,
        group - 1,
        2,
        group,
        group - 1,
        group - 1,
        2,
        2,
        group - 1,
        group - 1,
        depths - 1,
        depths - 1,
        groups - 1,
        groups - 1,
    ]
    return pl.pallas_call(
        functools.partial(return_kernel, group),
        out_shape=(
            jax.ShapeDtypeStruct((3, atoms), f32),
            jax.ShapeDtypeStruct((1, atoms), f32),
            jax.ShapeDtypeStruct((3, 3), f32),
        ),
        in_specs=[vmem] * 3,
        out_specs=(vmem,) * 3,
        scratch_shapes=[
            pltpu.VMEM((2 * group - 1, 3, GAP, LANES), f32),
            pltpu.VMEM((2, 3, 16, LANES), f32),
            pltpu.VMEM((8, atoms), f32),
            pltpu.VMEM((3, GAP, LANES), f32),
            pltpu.VMEM((group, 16, 128), f32),
            pltpu.VMEM((depths, 16, 128), f32),
            pltpu.VMEM((groups, 16, 128), f32),
        ]
        + [dma((count,)) for count in counts],
        compiler_params=pltpu.CompilerParams(
            collective_id=1, has_side_effects=True, vmem_limit_bytes=24 * 1024 * 1024
        ),
    )(ghalo, back, virial)


def per_device(
    positions,
    species,
    neighbours,
    counts,
    species_table,
    w_two_in,
    w_two_out,
    w_env,
    w_lat_in,
    w_lat_out,
    readout,
):
    atom_count = positions.shape[-1]
    slot_count = neighbours.shape[0]
    halo, center, index = collect_call(
        positions.reshape(3, atom_count),
        species.reshape(1, atom_count),
        neighbours.reshape(slot_count, atom_count),
        counts.reshape(1, atom_count),
        GROUP,
    )
    space = lax.axis_index("space")
    place = jnp.stack([space // GROUP * GROUP, lax.axis_index("depth")]).astype(jnp.int32)
    weights = (
        species_table,
        w_two_in,
        w_two_out,
        w_env,
        w_lat_in,
        w_lat_out,
        readout.reshape(1, -1),
    )
    ghalo, back, virial = edge_call(place, halo, center, index, weights, TILE, GROUP)
    forces, energies, virial_total = return_call(ghalo, back, virial, GROUP)
    return (
        forces.reshape(3, 1, 1, atom_count),
        energies.reshape(1, 1, atom_count),
        virial_total,
    )


def solution(mesh):
    placed = (
        P(None, "space", "depth", None),
        P("space", "depth", None),
        P(None, "space", "depth", None),
        P("space", "depth", None),
        P(),
        P(),
        P(),
        P(),
        P(),
        P(),
        P(),
    )
    return jax.shard_map(
        per_device,
        mesh=mesh,
        in_specs=placed,
        out_specs=(P(None, "space", "depth", None), P("space", "depth", None), P()),
        check_vma=False,
    )
```

```python
import functools

import jax
import jax.numpy as jnp
from jax import lax
from jax.experimental import pallas as pl
from jax.experimental.pallas import tpu as pltpu
from jax.sharding import PartitionSpec as P

CUTOFF_RADIUS = 5.0
SOFT_CORE = 0.25

GROUP = 4
TILE = 2048
UNITS = 8
UNIT = 256
SIDE_LENGTH = 32.0
SPREAD = 36.0
GAP = 48
SPAN = 144
LANES = 256


def pieces(value, count):
    parts = []
    rest = value
    for _ in range(count):
        part = rest.astype(jnp.bfloat16)
        parts.append(part)
        rest = rest - part.astype(jnp.float32)
    return parts


def matmul(left, right):
    return jnp.dot(left, right, preferred_element_type=jnp.float32)


def matmul_nt(left, right):
    return lax.dot_general(
        left, right, (((1,), (1,)), ((), ())), preferred_element_type=jnp.float32
    )


def edge_kernel(
    units,
    tile,
    members,
    place_ref,
    halo_ref,
    center_ref,
    index_ref,
    emb_ref,
    w_two_in_ref,
    w_two_out_ref,
    w_env_ref,
    w_lat_in_ref,
    w_lat_out_ref,
    readout_ref,
    ghalo_ref,
    back_ref,
    virial_ref,
    table,
    first_w,
    two_out_t,
    two_out,
    env_t,
    env_w,
    w_lat_in,
    w_lat_out,
    readout,
    fetch,
    lat_in_t,
    lat_back,
    energy_col,
    radial_w,
    readout_col,
    picked,
    low_hot,
    radial_s,
    slope_s,
    slope_one,
    raw_s,
    latent_s,
    amp_s,
    mix_s,
    glat_s,
    harm_s,
    envs,
    genvs,
    rows_s,
    virial_s,
    unit_slot,
    unit_chunk,
):
    slots, atoms = index_ref.shape
    tiles = atoms // tile
    rows = halo_ref.shape[1]
    f32, bf16 = jnp.float32, jnp.bfloat16
    base_space = place_ref[0]
    base_depth = place_ref[1]

    fetches = [
        pltpu.make_async_copy(source, target, fetch.at[at])
        for at, (source, target) in enumerate(
            (
                (w_two_out_ref, two_out_t),
                (w_env_ref, env_t),
                (w_lat_in_ref, w_lat_in),
                (w_lat_out_ref, w_lat_out),
                (readout_ref, readout),
            )
        )
    ]
    for copy in fetches:
        copy.start()

    row_id = lax.broadcasted_iota(jnp.int32, (rows, LANES), 0)
    space_of = (row_id // GAP - 1 + base_space).astype(f32)
    depth_of = (lax.rem(row_id, GAP) // 16 - 1 + base_depth).astype(f32)
    half = SIDE_LENGTH / 2
    local = [
        halo_ref[0] - (SIDE_LENGTH * space_of + half),
        halo_ref[1] - half + SPREAD * (halo_ref[3] - 1.5),
        halo_ref[2] - (SIDE_LENGTH * depth_of + half),
    ]
    for axis in range(3):
        high, low = pieces(local[axis], 2)
        table[axis, :, 0:LANES] = high
        table[axis, :, LANES : 2 * LANES] = low

    ghalo_ref[...] = jnp.zeros_like(ghalo_ref)
    back_ref[...] = jnp.zeros_like(back_ref)
    picked[...] = jnp.zeros_like(picked)
    harm_s[...] = jnp.zeros_like(harm_s)
    rows_s[...] = jnp.zeros_like(rows_s)
    virial_s[...] = jnp.zeros_like(virial_s)

    for copy in fetches:
        copy.wait()

    w_one = w_two_in_ref[...]
    emb = emb_ref[...]
    center_part = matmul(emb, w_one[0:64])
    nbr_part = matmul(emb, w_one[64:128])
    species_part = 0.5 * jnp.concatenate([center_part, nbr_part], 0)
    radial_half = 0.5 * w_one[128:136].astype(f32)
    split = [part.astype(f32) for part in pieces(species_part, 3)]
    first_w[...] = jnp.concatenate([radial_half] + split, 0).T.astype(bf16)
    radial_w[...] = jnp.concatenate([radial_half, jnp.zeros_like(radial_half)], 0).astype(bf16)
    two_out[...] = two_out_t[...].astype(f32).T.astype(bf16)
    env_w[...] = env_t[...].astype(f32).T.astype(bf16)
    lat_in = w_lat_in[...].astype(f32)
    lat_in_t[...] = (0.5 * lat_in).T.astype(bf16)
    readout_row = readout[...]
    last_row = lax.dot_general(
        jnp.broadcast_to(readout_row, (8, readout_row.shape[1])),
        w_lat_out[...].astype(f32),
        (((1,), (0,)), ((), ())),
        precision=lax.Precision.HIGHEST,
        preferred_element_type=f32,
    )
    lat_back[...] = (0.5 * lat_in * last_row[0:1]).astype(bf16)
    energy_col[...] = last_row.T
    readout_col[...] = jnp.broadcast_to(readout_row, (8, readout_row.shape[1])).T

    chunks = tile // UNIT
    span = units * UNIT
    cuts = [slice(unit * UNIT, (unit + 1) * UNIT) for unit in range(units)]

    def one_tile(step, carry):
        lanes = pl.ds(pl.multiple_of(step * tile, tile), tile)
        count_row = center_ref[4:5, lanes]

        total = 0
        for chunk in range(chunks):
            depth = jnp.max(count_row[:, chunk * UNIT : (chunk + 1) * UNIT]).astype(jnp.int32)
            for slot in range(slots):
                unit_slot[total + slot] = slot
                unit_chunk[total + slot] = chunk
            total = total + depth
        for unit in range(units - 1):
            unit_slot[total + unit] = 0
            unit_chunk[total + unit] = chunks
        turns = (total + (units - 1)) // units

        count_row = count_row.astype(jnp.int32)
        lane_id = lax.broadcasted_iota(jnp.int32, (1, tile), 1)
        member_row = ((lane_id + step * tile) // (atoms // members)).astype(f32)
        center_x = center_ref[0:1, lanes] - (
            SIDE_LENGTH * (base_space.astype(f32) + member_row) + half
        )
        center_y = center_ref[1:2, lanes] - half
        center_z = center_ref[2:3, lanes] - (SIDE_LENGTH * base_depth.astype(f32) + half)

        def places(turn):
            found = []
            for unit in range(units):
                slot = unit_slot[turn * units + unit]
                chunk = unit_chunk[turn * units + unit]
                found.append(
                    (pl.ds(slot, 1), pl.ds(pl.multiple_of(chunk * UNIT, UNIT), UNIT))
                )
            return found

        def indices(turn):
            found = []
            for unit in range(units):
                slot = unit_slot[turn * units + unit]
                chunk = jnp.minimum(unit_chunk[turn * units + unit], chunks - 1)
                start = pl.multiple_of(step * tile + chunk * UNIT, UNIT)
                found.append(index_ref[pl.ds(slot, 1), pl.ds(start, UNIT)])
            return jnp.concatenate(found, 1)

        def table_rows(turn):
            found = []
            for unit in range(units):
                chunk = jnp.minimum(unit_chunk[turn * units + unit], chunks - 1)
                member = (step * tile + chunk * UNIT) // (atoms // members)
                found.append(pl.ds(pl.multiple_of(member * GAP, 16), SPAN))
            return found

        def gather(turn, carry):
            entry = indices(turn)
            spots_now = places(turn)
            windows = table_rows(turn)
            low_part = lax.bitwise_and(entry, LANES - 1)
            high_part = lax.shift_right_logical(entry, 8)
            hot = (
                lax.broadcasted_iota(jnp.int32, (LANES, span), 0) == low_part
            ).astype(f32).astype(bf16)
            low_hot[turn] = hot
            both = jnp.concatenate([hot, hot], 0)
            mask = lax.broadcasted_iota(jnp.int32, (SPAN, span), 0) == high_part
            for axis in range(3):
                for (slot, chunk), window, cut in zip(spots_now, windows, cuts):
                    found = matmul(table[axis, window, :], both[:, cut])
                    picked[axis, slot, chunk] = jnp.sum(
                        jnp.where(mask[:, cut], found, 0.0), axis=0, keepdims=True
                    )
            return carry

        lax.fori_loop(0, turns, gather, 0)

        entries = index_ref[:, lanes]
        block = lax.shift_right_logical(entries, 12)
        block_space = lax.shift_right_logical(block * 11, 5)
        block_depth = block - 3 * block_space
        nbr = [picked[axis, :, 0:tile] for axis in range(3)]
        nbr_species = jnp.floor((nbr[1] + 2.0 * SPREAD) * (1.0 / SPREAD))
        nbr_y = nbr[1] - SPREAD * (nbr_species - 1.5)
        rel = [
            nbr[0] + SIDE_LENGTH * (block_space - 1).astype(f32) - center_x,
            nbr_y - center_y,
            nbr[2] + SIDE_LENGTH * (block_depth - 1).astype(f32) - center_z,
        ]
        squared = rel[0] * rel[0] + rel[1] * rel[1] + rel[2] * rel[2]
        inverse = lax.rsqrt(squared + SOFT_CORE)
        distance = (squared + SOFT_CORE) * inverse
        direction = [part * inverse for part in rel]
        fraction = jnp.minimum(distance / CUTOFF_RADIUS, 1.0)
        shell = 1.0 - fraction * fraction
        cutoff = shell * shell
        live = (
            lax.broadcasted_iota(jnp.int32, (slots, tile), 0) < count_row
        ).astype(f32)
        for axis in range(3):
            harm_s[axis, :, 0:tile] = direction[axis]
        harm_s[3, :, 0:tile] = cutoff
        harm_s[4, :, 0:tile] = live
        harm_s[5, :, 0:tile] = nbr_species
        harm_s[6, :, 0:tile] = distance
        harm_s[7, 0:1, 0:tile] = center_ref[3:4, lanes]
        for part in range(4):
            envs[part] = jnp.zeros(envs.shape[1:], f32)
            genvs[part] = jnp.zeros(genvs.shape[1:], f32)

        basis_id = lax.broadcasted_iota(jnp.int32, (8, span), 0).astype(f32)
        spots = basis_id * (CUTOFF_RADIUS / 7)
        sharpness = (7 / CUTOFF_RADIUS) ** 2

        def row(found, kind):
            return jnp.concatenate([harm_s[kind, slot, chunk] for slot, chunk in found], 1)

        def per_atom(found, ref, part):
            return jnp.concatenate([ref[part, :, chunk] for slot, chunk in found], 1)

        def put_row(found, kind, value):
            for (slot, chunk), cut in zip(found, cuts):
                rows_s[kind, slot, chunk] = value[:, cut]

        def add_row(found, kind, value):
            for (slot, chunk), cut in zip(found, cuts):
                rows_s[kind, slot, chunk] += value[:, cut]

        def add_atoms(found, ref, part, value):
            for (slot, chunk), cut in zip(found, cuts):
                ref[part, :, chunk] += value[:, cut]

        def first(turn, carry):
            found = places(turn)
            spread = row(found, 6) - spots
            radial = jnp.exp(-sharpness * spread * spread)
            radial_s[turn] = radial * (-2.0 * sharpness * spread)
            center_species = jnp.concatenate(
                [harm_s[7, 0:1, chunk] for slot, chunk in found], 1
            )
            species_hot = jnp.where(
                basis_id < 4.0,
                (basis_id == center_species).astype(f32),
                (basis_id - 4.0 == row(found, 5)).astype(f32),
            )
            features = jnp.concatenate([radial, species_hot, species_hot, species_hot], 0)
            pre = matmul(first_w[...], features.astype(bf16))
            bent = jnp.tanh(pre)
            mixed = pre * bent
            hidden = (pre + mixed).astype(bf16)
            slope_one[turn] = ((1.0 + bent) * (1.0 + (pre - mixed))).astype(bf16)
            raw = matmul(two_out_t[...], hidden)
            raw_s[turn] = raw
            latent = raw * row(found, 3)
            latent_b = latent.astype(bf16)
            latent_s[turn] = latent_b
            amp = matmul(env_t[...], latent_b) * row(found, 4)
            amp_s[turn] = amp
            add_atoms(found, envs, 0, amp)
            for axis in range(3):
                add_atoms(found, envs, 1 + axis, amp * row(found, axis))
            return carry

        lax.fori_loop(0, turns, first, 0)
        for part in range(4):
            envs[part] = envs[part] * (1.0 / slots)

        def second(turn, carry):
            found = places(turn)
            amp = amp_s[turn]
            ways = [row(found, axis) for axis in range(3)]
            env = [per_atom(found, envs, part) for part in range(4)]
            mix = env[0] + env[1] * ways[0] + env[2] * ways[1] + env[3] * ways[2]
            scalars = (amp * mix).astype(bf16)
            joined = jnp.concatenate([latent_s[turn], scalars], 0)
            pre = matmul(lat_in_t[...], joined)
            bent = jnp.tanh(pre)
            mixed = pre * bent
            slope = ((1.0 + bent) * (1.0 + (pre - mixed))).astype(bf16)
            rest = jnp.sum((pre + mixed) * energy_col[:, 0:1], axis=0, keepdims=True)
            cutoff_row = row(found, 3)
            weight = cutoff_row * row(found, 4)
            line = jnp.sum(readout_col[:, 0:1] * raw_s[turn], axis=0, keepdims=True)
            put_row(found, 0, line * cutoff_row + rest)
            back = matmul(lat_back[...], slope) * weight
            glat_s[turn] = back[0:64]
            gscal = back[64:96]
            mix_s[turn] = gscal * mix
            gprod = gscal * amp
            add_atoms(found, genvs, 0, gprod)
            for axis in range(3):
                add_atoms(found, genvs, 1 + axis, gprod * ways[axis])
                put_row(
                    found, 1 + axis, jnp.sum(gprod * env[1 + axis], axis=0, keepdims=True)
                )
            return carry

        lax.fori_loop(0, turns, second, 0)
        for part in range(4):
            genvs[part] = genvs[part] * (1.0 / slots)

        def third(turn, carry):
            found = places(turn)
            amp = amp_s[turn]
            ways = [row(found, axis) for axis in range(3)]
            live_row = row(found, 4)
            cutoff_row = row(found, 3)
            genv = [per_atom(found, genvs, part) for part in range(4)]
            gamp = (
                mix_s[turn] + genv[0] + genv[1] * ways[0] + genv[2] * ways[1] + genv[3] * ways[2]
            ) * live_row
            for axis in range(3):
                add_row(found, 1 + axis, jnp.sum(amp * genv[1 + axis], axis=0, keepdims=True))
            glat = (
                glat_s[turn]
                + matmul(env_w[...], gamp.astype(bf16))
                + readout_col[:, 0:1] * (cutoff_row * live_row)
            )
            put_row(found, 4, jnp.sum(glat * raw_s[turn], axis=0, keepdims=True))
            ghidden = matmul(two_out[...], (glat * cutoff_row).astype(bf16))
            gpre = (ghidden * slope_one[turn].astype(f32)).astype(bf16)
            gradial = matmul(radial_w[...], gpre)[0:8]
            put_row(found, 5, jnp.sum(gradial * radial_s[turn], axis=0, keepdims=True))
            return carry

        lax.fori_loop(0, turns, third, 0)

        got = [rows_s[kind, :, 0:tile] for kind in range(6)]
        pair = got[0]
        back_ref[3:4, lanes] = jnp.sum(
            jnp.where(live > 0.0, pair * cutoff, 0.0), axis=0, keepdims=True
        )
        gcut = got[4] + pair * live
        gdist = got[5] - gcut * shell * fraction * (4.0 / CUTOFF_RADIUS)
        gdir = [got[1 + axis] for axis in range(3)]
        along = gdir[0] * direction[0] + gdir[1] * direction[1] + gdir[2] * direction[2]
        push = gdist - along * inverse
        grel = [
            jnp.where(live > 0.0, gdir[axis] * inverse + direction[axis] * push, 0.0)
            for axis in range(3)
        ]
        for axis in range(3):
            back_ref[axis : axis + 1, lanes] = -jnp.sum(grel[axis], axis=0, keepdims=True)
            picked[axis, :, 0:tile] = grel[axis]
            picked[axis, :, tile : tile + UNIT] = jnp.zeros((slots, UNIT), f32)
            for other in range(3):
                virial_s[3 * axis + other] += rel[axis] * grel[other]

        def scatter(turn, carry):
            found = places(turn)
            windows = table_rows(turn)
            high_part = lax.shift_right_logical(indices(turn), 8)
            mask = lax.broadcasted_iota(jnp.int32, (SPAN, span), 0) == high_part
            for axis in range(3):
                for (slot, chunk), window, cut in zip(found, windows, cuts):
                    spread = jnp.where(mask[:, cut], picked[axis, slot, chunk], 0.0).astype(bf16)
                    ghalo_ref[axis, window, :] += matmul_nt(spread, low_hot[turn, :, cut])
            return carry

        lax.fori_loop(0, turns, scatter, 0)
        return carry

    lax.fori_loop(0, tiles, one_tile, 0)
    for entry in range(9):
        folded = jnp.sum(virial_s[entry], axis=0, keepdims=True)
        part = folded[:, 0:128]
        for chunk in range(1, tile // 128):
            part = part + folded[:, 128 * chunk : 128 * (chunk + 1)]
        virial_ref[entry : entry + 1, :] = -part
    virial_ref[9:16, :] = jnp.zeros((7, 128), f32)


def edge_call(place, halo, center, index, weights, tile, members):
    slots, atoms = index.shape
    rows = halo.shape[1]
    f32, bf16 = jnp.float32, jnp.bfloat16
    vmem = pl.BlockSpec(memory_space=pltpu.VMEM)
    shapes = (
        jax.ShapeDtypeStruct((3, rows, LANES), f32),
        jax.ShapeDtypeStruct((8, atoms), f32),
        jax.ShapeDtypeStruct((16, 128), f32),
    )
    turns = slots * tile // (UNITS * UNIT)
    span = UNITS * UNIT
    wide = tile + UNIT
    scratch = [
        pltpu.VMEM((3, rows, 2 * LANES), bf16),
        pltpu.VMEM((256, 32), bf16),
        pltpu.VMEM((64, 256), bf16),
        pltpu.VMEM((256, 64), bf16),
        pltpu.VMEM((32, 64), bf16),
        pltpu.VMEM((64, 32), bf16),
        pltpu.VMEM((96, 256), bf16),
        pltpu.VMEM((64, 256), bf16),
        pltpu.VMEM((1, 64), f32),
        pltpu.SemaphoreType.DMA((5,)),
        pltpu.VMEM((256, 96), bf16),
        pltpu.VMEM((96, 256), bf16),
        pltpu.VMEM((256, 8), f32),
        pltpu.VMEM((16, 256), bf16),
        pltpu.VMEM((64, 8), f32),
        pltpu.VMEM((3, slots, wide), f32),
        pltpu.VMEM((turns, LANES, span), bf16),
        pltpu.VMEM((turns, 8, span), f32),
        pltpu.VMEM((8, 8, wide), f32),
        pltpu.VMEM((turns, 256, span), bf16),
        pltpu.VMEM((turns, 64, span), f32),
        pltpu.VMEM((turns, 64, span), bf16),
        pltpu.VMEM((turns, 32, span), f32),
        pltpu.VMEM((turns, 32, span), f32),
        pltpu.VMEM((turns, 64, span), f32),
        pltpu.VMEM((8, slots, wide), f32),
        pltpu.VMEM((4, 32, wide), f32),
        pltpu.VMEM((4, 32, wide), f32),
        pltpu.VMEM((6, slots, wide), f32),
        pltpu.VMEM((9, slots, tile), f32),
        pltpu.SMEM((slots * (tile // UNIT) + slots + UNITS,), jnp.int32),
        pltpu.SMEM((slots * (tile // UNIT) + slots + UNITS,), jnp.int32),
    ]
    return pl.pallas_call(
        functools.partial(edge_kernel, UNITS, tile, members),
        out_shape=shapes,
        in_specs=[pl.BlockSpec(memory_space=pltpu.SMEM)] + [vmem] * 5 + [pl.BlockSpec(memory_space=pltpu.HBM)] * 5,
        out_specs=(vmem,) * 3,
        scratch_shapes=scratch,
        compiler_params=pltpu.CompilerParams(vmem_limit_bytes=48 * 1024 * 1024),
    )(place, halo, center, index, *weights)


def send(source, target, send_sem, recv_sem, space, depth):
    return pltpu.make_async_remote_copy(
        src_ref=source,
        dst_ref=target,
        send_sem=send_sem,
        recv_sem=recv_sem,
        device_id=(space, depth),
        device_id_type=pl.DeviceIdType.MESH,
    )


def greet(space, depth):
    pl.semaphore_signal(
        pltpu.get_barrier_semaphore(),
        inc=1,
        device_id=(space, depth),
        device_id_type=pl.DeviceIdType.MESH,
    )


def where_am_i(group):
    spaces, depths = lax.axis_size("space"), lax.axis_size("depth")
    space, depth = lax.axis_index("space"), lax.axis_index("depth")
    spot = lax.rem(space, group)
    first = space - spot
    before = lax.rem(first - 1 + spaces, spaces)
    after = lax.rem(first + group, spaces)
    return spaces, depths, space, depth, spot, first, before, after


def collect_kernel(
    group,
    position_ref,
    species_ref,
    index_ref,
    count_ref,
    halo_ref,
    center_ref,
    index_out_ref,
    position_in,
    species_in,
    index_in,
    count_in,
    own,
    flat,
    entries,
    load,
    depth_send,
    depth_recv,
    part_send,
    part_recv,
    column_send,
    column_recv,
    edge_send,
    edge_recv,
    relay_send,
    relay_recv,
):
    loads = [
        pltpu.make_async_copy(source, target, load.at[at])
        for at, (source, target) in enumerate(
            (
                (position_ref, position_in),
                (species_ref, species_in),
                (count_ref, count_in),
                (index_ref, index_in),
            )
        )
    ]
    for copy in loads:
        copy.start()
    spaces, depths, space, depth, spot, first, before, after = where_am_i(group)
    slots, atoms = entries.shape
    share = atoms // group
    up, down = lax.rem(depth + 1, depths), lax.rem(depth + depths - 1, depths)
    mates = [first + lax.rem(spot + off, group) for off in range(1, group)]
    side = lax.rem(space, 2)
    twin = space + 1 - 2 * side
    at_start, at_end = spot == 0, spot == group - 1
    at_edge = jnp.logical_or(at_start, at_end)
    edge_from = jnp.where(side == 0, after, before)

    greet(space, up)
    greet(space, down)
    for mate in mates:
        greet(mate, depth)
    greet(edge_from, depth)
    expected = 2 + (group - 1) + (group // 2) * at_edge.astype(jnp.int32)

    for copy in loads[0:3]:
        copy.wait()
    for part in range(3):
        flat[part : part + 1, :] = position_in[part]
    flat[3:4, :] = species_in[...].astype(jnp.float32)
    flat[4:5, :] = count_in[...].astype(jnp.float32)
    flat[5:8, :] = jnp.zeros((3, atoms), jnp.float32)
    for part in range(4):
        for row in range(atoms // LANES):
            own[part, row : row + 1, :] = flat[part : part + 1, row * LANES : (row + 1) * LANES]
    pl.semaphore_wait(pltpu.get_barrier_semaphore(), expected)

    column = pl.multiple_of((spot + 1) * GAP, 16)
    low, middle, high = (
        halo_ref.at[:, pl.ds(pl.multiple_of(column + 16 * part, 16), 16), :] for part in range(3)
    )
    depth_copies = [
        send(own, low, depth_send.at[0], depth_recv.at[0], space, up),
        send(own, high, depth_send.at[1], depth_recv.at[1], space, down),
    ]
    for copy in depth_copies:
        copy.start()
    loads[3].wait()
    for slot in range(slots):
        entries[slot : slot + 1, :] = index_in[slot]
    mine = pl.ds(pl.multiple_of(spot * share, 128), share)
    part_copies = []
    for off in range(1, group):
        theirs = pl.ds(off * share, share)
        for kind, (source, target) in enumerate(((entries, index_out_ref), (flat, center_ref))):
            slot = 2 * (off - 1) + kind
            copy = send(
                source.at[:, theirs],
                target.at[:, mine],
                part_send.at[slot],
                part_recv.at[slot],
                mates[off - 1],
                depth,
            )
            copy.start()
            part_copies.append(copy)
    middle[...] = own[...]
    index_out_ref[:, mine] = entries[:, 0:share]
    center_ref[:, mine] = flat[:, 0:share]
    for copy in depth_copies:
        copy.wait_recv()

    source = halo_ref.at[:, pl.ds(column, GAP), :]
    jumps = list(range(2, group, 2))
    cross_copies = []
    for at, off in enumerate(jumps):
        copy = send(
            source, source, column_send.at[at], column_recv.at[at], mates[off - 1], depth
        )
        copy.start()
        cross_copies.append(copy)

    def edges():
        base = jnp.where(at_start, lax.rem(first - group + spaces, spaces), after)
        start = jnp.where(at_start, (group + 1) * GAP, 0)
        target = halo_ref.at[:, pl.ds(pl.multiple_of(start, 16), GAP), :]
        return [
            send(
                source, target, edge_send.at[member], edge_recv.at[0], base + 2 * member + side, depth
            )
            for member in range(group // 2)
        ]

    @pl.when(at_edge)
    def _():
        for copy in edges():
            copy.start()

    twin_copy = send(
        source, source, column_send.at[len(jumps)], column_recv.at[len(jumps)], twin, depth
    )
    twin_copy.start()

    relay_copies = []
    for at, off in enumerate(jumps):
        cross_copies[at].wait_recv()
        start = (lax.rem(spot + group - off, group) + 1) * GAP
        block = halo_ref.at[:, pl.ds(pl.multiple_of(start, 16), GAP), :]
        copy = send(block, block, relay_send.at[at], relay_recv.at[at], twin, depth)
        copy.start()
        relay_copies.append(copy)
    edge_start = jnp.where(side == 0, (group + 1) * GAP, 0)
    block = halo_ref.at[:, pl.ds(pl.multiple_of(edge_start, 16), GAP), :]
    send(block, block, edge_send.at[0], edge_recv.at[0], edge_from, depth).wait_recv()
    copy = send(
        block, block, relay_send.at[len(jumps)], relay_recv.at[len(jumps)], twin, depth
    )
    copy.start()
    relay_copies.append(copy)

    for copy in [twin_copy] + part_copies + relay_copies:
        copy.wait_recv()
    for copy in depth_copies + part_copies + cross_copies + [twin_copy] + relay_copies:
        copy.wait_send()

    @pl.when(at_edge)
    def _():
        for copy in edges():
            copy.wait_send()


def collect_call(positions, species, index, count, group):
    slots, _, atoms = index.shape
    rows = (group + 2) * GAP
    f32, i32 = jnp.float32, jnp.int32
    vmem = pl.BlockSpec(memory_space=pltpu.VMEM)
    dma = pltpu.SemaphoreType.DMA
    half = group // 2
    return pl.pallas_call(
        functools.partial(collect_kernel, group),
        out_shape=(
            jax.ShapeDtypeStruct((4, rows, LANES), f32),
            jax.ShapeDtypeStruct((8, atoms), f32),
            jax.ShapeDtypeStruct((slots, atoms), i32),
        ),
        in_specs=[pl.BlockSpec(memory_space=pltpu.HBM)] * 4,
        out_specs=(vmem,) * 3,
        scratch_shapes=[
            pltpu.VMEM((3, 1, atoms), f32),
            pltpu.VMEM((1, atoms), i32),
            pltpu.VMEM((slots, 1, atoms), i32),
            pltpu.VMEM((1, atoms), i32),
            pltpu.VMEM((4, atoms // LANES, LANES), f32),
            pltpu.VMEM((8, atoms), f32),
            pltpu.VMEM((slots, atoms), i32),
            dma((4,)),
            dma((2,)),
            dma((2,)),
            dma((2 * (group - 1),)),
            dma((2 * (group - 1),)),
            dma((half,)),
            dma((half,)),
            dma((half,)),
            dma((1,)),
            dma((half,)),
            dma((half,)),
        ],
        compiler_params=pltpu.CompilerParams(
            collective_id=0, has_side_effects=True, vmem_limit_bytes=24 * 1024 * 1024
        ),
    )(positions, species, index, count)


def return_kernel(
    group,
    ghalo_ref,
    back_ref,
    virial_ref,
    force_ref,
    energy_ref,
    total_ref,
    columns,
    halves,
    sums,
    blocks,
    flat,
    summed,
    by_member,
    by_depth,
    by_group,
    twin_send,
    twin_recv,
    column_send,
    column_recv,
    edge_send,
    edge_recv,
    part_send,
    part_recv,
    block_send,
    block_recv,
    member_send,
    member_recv,
    layer_send,
    layer_recv,
    group_send,
    group_recv,
):
    spaces, depths, space, depth, spot, first, before, after = where_am_i(group)
    atoms = back_ref.shape[1]
    share = atoms // group
    groups = spaces // group
    up, down = lax.rem(depth + 1, depths), lax.rem(depth + depths - 1, depths)
    mates = [first + lax.rem(spot + off, group) for off in range(1, group)]
    layers = [lax.rem(depth + off, depths) for off in range(1, depths)]
    peers = [lax.rem(space + off * group, spaces) for off in range(1, groups)]
    at_start, at_end = spot == 0, spot == group - 1

    for mate in mates:
        greet(mate, depth)
    for layer in layers:
        greet(space, layer)
    for peer in peers:
        greet(peer, depth)
    side = lax.rem(space, 2)
    twin = space + 1 - 2 * side
    twin_spot = spot + 1 - 2 * side
    jumps = list(range(2, group, 2))
    at_edge = jnp.logical_or(at_start, at_end)
    edge_to = jnp.where(side == 0, after, before)

    @pl.when(at_edge)
    def _():
        base = jnp.where(at_start, lax.rem(first - group + spaces, spaces), after)
        for member in range(group // 2):
            greet(base + 2 * member + side, depth)

    pl.semaphore_wait(
        pltpu.get_barrier_semaphore(), (group - 1) + (depths - 1) + (groups - 1) + 1
    )

    started = []

    def go(*args):
        copy = send(*args)
        copy.start()
        started.append(copy)
        return copy

    by_member[spot] = virial_ref[...]
    mine = by_member.at[spot]
    member_copies = [
        go(mine, mine, member_send.at[off], member_recv.at[off], mate, depth)
        for off, mate in enumerate(mates)
    ]

    def column_starts(spot_at, side_at):
        starts = [(lax.rem(spot_at + off, group) + 1) * GAP for off in jumps + [0]]
        starts.append(jnp.where(side_at == 0, (group + 1) * GAP, 0))
        return [pl.ds(pl.multiple_of(start, 16), GAP) for start in starts]

    twin_copies = [
        go(
            ghalo_ref.at[:, where, :], halves.at[at], twin_send.at[at], twin_recv.at[at], twin, depth
        )
        for at, where in enumerate(column_starts(twin_spot, 1 - side))
    ]
    part_copies = []
    for off, mate in enumerate(mates):
        theirs = pl.ds(pl.multiple_of((mate - first) * share, 128), share)
        part = (group - 1 - off) * share
        part_copies.append(
            go(
                back_ref.at[:, theirs],
                flat.at[:, part : part + share],
                part_send.at[off],
                part_recv.at[off],
                mate,
                depth,
            )
        )
    own_part = pl.ds(pl.multiple_of(spot * share, 128), share)
    flat[:, 0:share] = back_ref[:, own_part]

    column_copies = []
    kinds = column_starts(spot, side)
    order = [len(jumps) + 1] + list(range(len(jumps)))
    for at in order:
        twin_copies[at].wait_recv()
        sums[at] = ghalo_ref[:, kinds[at], :] + halves[at]
        if at == len(jumps) + 1:
            go(
                sums.at[at],
                columns.at[len(jumps) + spot // 2],
                edge_send.at[0],
                edge_recv.at[spot // 2],
                edge_to,
                depth,
            )
        else:
            column_copies.append(
                go(
                    sums.at[at],
                    columns.at[at],
                    column_send.at[at],
                    column_recv.at[at],
                    mates[jumps[at] - 1],
                    depth,
                )
            )

    for copy in member_copies:
        copy.wait_recv()
    level = by_member[0]
    for member in range(1, group):
        level = level + by_member[member]
    by_depth[depth] = level
    mine_depth = by_depth.at[depth]
    layer_copies = [
        go(mine_depth, mine_depth, layer_send.at[off], layer_recv.at[off], space, layer)
        for off, layer in enumerate(layers)
    ]
    for copy in layer_copies:
        copy.wait_recv()
    level = by_depth[0]
    for layer in range(1, depths):
        level = level + by_depth[layer]
    place = space // group
    by_group[place] = level
    mine_group = by_group.at[place]
    group_copies = [
        go(mine_group, mine_group, group_send.at[off], group_recv.at[off], peer, depth)
        for off, peer in enumerate(peers)
    ]

    twin_copies[len(jumps)].wait_recv()
    total = ghalo_ref[:, kinds[len(jumps)], :] + halves[len(jumps)]
    for at, copy in enumerate(column_copies):
        copy.wait_recv()
        total = total + columns[at]
    summed[...] = total

    @pl.when(at_edge)
    def _():
        extra = jnp.zeros((3, GAP, LANES), jnp.float32)
        for member in range(group // 2):
            slot = len(jumps) + member
            send(
                columns.at[slot],
                columns.at[slot],
                edge_send.at[0],
                edge_recv.at[member],
                edge_to,
                depth,
            ).wait_recv()
            extra = extra + columns[slot]
        summed[...] = summed[...] + extra

    block_copies = [
        go(summed.at[:, 0:16, :], blocks.at[0], block_send.at[0], block_recv.at[0], space, down),
        go(summed.at[:, 32:48, :], blocks.at[1], block_send.at[1], block_recv.at[1], space, up),
    ]
    for copy in part_copies:
        copy.wait_recv()
    energy_ref[...] = flat[3:4, :]
    for copy in group_copies:
        copy.wait_recv()
    level = by_group[0]
    for member in range(1, groups):
        level = level + by_group[member]
    entries = jnp.sum(level, axis=1, keepdims=True)
    shape = (8, 128)
    row_id = lax.broadcasted_iota(jnp.int32, shape, 0)
    column_id = lax.broadcasted_iota(jnp.int32, shape, 1)
    table = jnp.zeros(shape, jnp.float32)
    for entry in range(9):
        here = jnp.logical_and(row_id == entry // 3, column_id == entry % 3)
        table = jnp.where(here, entries[entry : entry + 1, :], table)
    total_ref[...] = table[0:3, 0:3]
    for copy in block_copies:
        copy.wait_recv()
    blocks[0] = summed[:, 16:32, :] + blocks[0] + blocks[1]
    for part in range(3):
        for row in range(atoms // LANES):
            lanes = slice(row * LANES, (row + 1) * LANES)
            force_ref[part, :, lanes] = -(
                blocks[0, part, row : row + 1, :] + flat[part : part + 1, lanes]
            )
    for copy in started:
        copy.wait_send()


def return_call(ghalo, back, virial, group):
    atoms = back.shape[1]
    f32 = jnp.float32
    depths = lax.axis_size("depth")
    groups = lax.axis_size("space") // group
    vmem = pl.BlockSpec(memory_space=pltpu.VMEM)
    dma = pltpu.SemaphoreType.DMA
    half = group // 2
    counts = [
        half + 1,
        half + 1,
        half,
        half,
        1,
        half,
        group - 1,
        group - 1,
        2,
        2,
        group - 1,
        group - 1,
        depths - 1,
        depths - 1,
        groups - 1,
        groups - 1,
    ]
    return pl.pallas_call(
        functools.partial(return_kernel, group),
        out_shape=(
            jax.ShapeDtypeStruct((3, 1, atoms), f32),
            jax.ShapeDtypeStruct((1, atoms), f32),
            jax.ShapeDtypeStruct((3, 3), f32),
        ),
        in_specs=[vmem] * 3,
        out_specs=(vmem,) * 3,
        scratch_shapes=[
            pltpu.VMEM((group - 1, 3, GAP, LANES), f32),
            pltpu.VMEM((half + 1, 3, GAP, LANES), f32),
            pltpu.VMEM((half + 1, 3, GAP, LANES), f32),
            pltpu.VMEM((2, 3, 16, LANES), f32),
            pltpu.VMEM((8, atoms), f32),
            pltpu.VMEM((3, GAP, LANES), f32),
            pltpu.VMEM((group, 16, 128), f32),
            pltpu.VMEM((depths, 16, 128), f32),
            pltpu.VMEM((groups, 16, 128), f32),
        ]
        + [dma((count,)) for count in counts],
        compiler_params=pltpu.CompilerParams(
            collective_id=1, has_side_effects=True, vmem_limit_bytes=24 * 1024 * 1024
        ),
    )(ghalo, back, virial)


def per_device(
    positions,
    species,
    neighbours,
    counts,
    species_table,
    w_two_in,
    w_two_out,
    w_env,
    w_lat_in,
    w_lat_out,
    readout,
):
    atom_count = positions.shape[-1]
    slot_count = neighbours.shape[0]
    halo, center, index = collect_call(
        positions.reshape(3, 1, atom_count),
        species.reshape(1, atom_count),
        neighbours.reshape(slot_count, 1, atom_count),
        counts.reshape(1, atom_count),
        GROUP,
    )
    space = lax.axis_index("space")
    place = jnp.stack([space // GROUP * GROUP, lax.axis_index("depth")]).astype(jnp.int32)
    weights = (
        species_table,
        w_two_in,
        w_two_out.T,
        w_env.T,
        w_lat_in,
        w_lat_out.T,
        readout.reshape(1, -1),
    )
    ghalo, back, virial = edge_call(place, halo, center, index, weights, TILE, GROUP)
    forces, energies, virial_total = return_call(ghalo, back, virial, GROUP)
    return (
        forces.reshape(3, 1, 1, atom_count),
        energies.reshape(1, 1, atom_count),
        virial_total,
    )


def solution(mesh):
    placed = (
        P(None, "space", "depth", None),
        P("space", "depth", None),
        P(None, "space", "depth", None),
        P("space", "depth", None),
        P(),
        P(),
        P(),
        P(),
        P(),
        P(),
        P(),
    )
    return jax.shard_map(
        per_device,
        mesh=mesh,
        in_specs=placed,
        out_specs=(P(None, "space", "depth", None), P("space", "depth", None), P()),
        check_vma=False,
    )
```

```python
import functools

import jax
import jax.numpy as jnp
from jax import lax
from jax.experimental import pallas as pl
from jax.experimental.pallas import tpu as pltpu
from jax.sharding import PartitionSpec as P

CUTOFF_RADIUS = 5.0
SOFT_CORE = 0.25

GROUP = 4
TILE = 1024
UNITS = 8
UNIT = 256
SIDE_LENGTH = 32.0
SPREAD = 36.0
GAP = 48
SPAN = 144
LANES = 256


def pieces(value, count):
    parts = []
    rest = value
    for _ in range(count):
        part = rest.astype(jnp.bfloat16)
        parts.append(part)
        rest = rest - part.astype(jnp.float32)
    return parts


def matmul(left, right):
    return jnp.dot(left, right, preferred_element_type=jnp.float32)


def matmul_nt(left, right):
    return lax.dot_general(
        left, right, (((1,), (1,)), ((), ())), preferred_element_type=jnp.float32
    )


def edge_kernel(
    units,
    tile,
    members,
    place_ref,
    halo_ref,
    center_ref,
    weight_ref,
    readout_ref,
    ghalo_ref,
    back_ref,
    virial_ref,
    table,
    first_w,
    two_out_t,
    two_out,
    env_t,
    env_w,
    lat_in_t,
    lat_back,
    energy_col,
    radial_w,
    readout_col,
    picked,
    low_hot,
    radial_s,
    slope_s,
    slope_one,
    raw_s,
    latent_s,
    amp_s,
    mix_s,
    glat_s,
    harm_s,
    envs,
    genvs,
    rows_s,
    virial_s,
    unit_slot,
    unit_chunk,
):
    slots, atoms = 8, center_ref.shape[1]
    tiles = atoms // tile
    rows = halo_ref.shape[1]
    f32, bf16 = jnp.float32, jnp.bfloat16
    base_space = place_ref[0]
    base_depth = place_ref[1]

    row_id = lax.broadcasted_iota(jnp.int32, (rows, LANES), 0)
    space_of = (row_id // GAP - 1 + base_space).astype(f32)
    depth_of = (lax.rem(row_id, GAP) // 16 - 1 + base_depth).astype(f32)
    half = SIDE_LENGTH / 2
    local = [
        halo_ref[0] - (SIDE_LENGTH * space_of + half),
        halo_ref[1] - half + SPREAD * (halo_ref[3] - 1.5),
        halo_ref[2] - (SIDE_LENGTH * depth_of + half),
    ]
    for axis in range(3):
        high, low = pieces(local[axis], 2)
        table[axis, :, 0:LANES] = high
        table[axis, :, LANES : 2 * LANES] = low

    ghalo_ref[...] = jnp.zeros_like(ghalo_ref)
    back_ref[...] = jnp.zeros_like(back_ref)
    picked[...] = jnp.zeros_like(picked)
    harm_s[...] = jnp.zeros_like(harm_s)
    rows_s[...] = jnp.zeros_like(rows_s)
    virial_s[...] = jnp.zeros_like(virial_s)

    w_one = weight_ref[0:136]
    lat_in = weight_ref[136:232].astype(f32)
    two_out_now = weight_ref[232:296].astype(f32)
    lat_out_now = weight_ref[296:360].astype(f32)
    env_now = weight_ref[360:392].astype(f32)[:, 0:64]
    emb = weight_ref[392:396].astype(f32)[:, 0:64].astype(bf16)
    center_part = matmul(emb, w_one[0:64])
    nbr_part = matmul(emb, w_one[64:128])
    species_part = 0.5 * jnp.concatenate([center_part, nbr_part], 0)
    radial_half = 0.5 * w_one[128:136].astype(f32)
    split = [part.astype(f32) for part in pieces(species_part, 3)]
    first_w[...] = jnp.concatenate([radial_half] + split, 0).T.astype(bf16)
    radial_w[...] = jnp.concatenate([radial_half, jnp.zeros_like(radial_half)], 0).astype(bf16)
    two_out_t[...] = two_out_now.astype(bf16)
    two_out[...] = two_out_now.T.astype(bf16)
    env_t[...] = env_now.astype(bf16)
    env_w[...] = env_now.T.astype(bf16)
    lat_in_t[...] = (0.5 * lat_in).T.astype(bf16)
    readout_row = readout_ref[...]
    last_row = lax.dot_general(
        jnp.broadcast_to(readout_row, (8, readout_row.shape[1])),
        lat_out_now,
        (((1,), (0,)), ((), ())),
        precision=lax.Precision.HIGHEST,
        preferred_element_type=f32,
    )
    lat_back[...] = (0.5 * lat_in * last_row[0:1]).astype(bf16)
    energy_col[...] = last_row.T
    readout_col[...] = jnp.broadcast_to(readout_row, (8, readout_row.shape[1])).T

    chunks = tile // UNIT
    span = units * UNIT
    cuts = [slice(unit * UNIT, (unit + 1) * UNIT) for unit in range(units)]

    def one_tile(step, carry):
        lanes = pl.ds(pl.multiple_of(step * tile, tile), tile)
        count_row = center_ref[4:5, lanes]

        total = 0
        for chunk in range(chunks):
            depth = jnp.max(count_row[:, chunk * UNIT : (chunk + 1) * UNIT]).astype(jnp.int32)
            for slot in range(slots):
                unit_slot[total + slot] = slot
                unit_chunk[total + slot] = chunk
            total = total + depth
        for unit in range(units - 1):
            unit_slot[total + unit] = 0
            unit_chunk[total + unit] = chunks
        turns = (total + (units - 1)) // units

        count_row = count_row.astype(jnp.int32)
        center_x = center_ref[0:1, lanes] - (
            SIDE_LENGTH * (base_space + step // (tiles // members)).astype(f32) + half
        )
        center_y = center_ref[1:2, lanes] - half
        center_z = center_ref[2:3, lanes] - (SIDE_LENGTH * base_depth.astype(f32) + half)

        member = step // (tiles // members)
        window = pl.ds(pl.multiple_of(member * GAP, 16), SPAN)

        def places(turn):
            found = []
            for unit in range(units):
                slot = unit_slot[turn * units + unit]
                chunk = unit_chunk[turn * units + unit]
                found.append(
                    (pl.ds(slot, 1), pl.ds(pl.multiple_of(chunk * UNIT, UNIT), UNIT))
                )
            return found

        def indices(turn):
            found = []
            for unit in range(units):
                slot = unit_slot[turn * units + unit]
                chunk = jnp.minimum(unit_chunk[turn * units + unit], chunks - 1)
                start = pl.multiple_of(step * tile + chunk * UNIT, UNIT)
                found.append(center_ref[pl.ds(slot + 8, 1), pl.ds(start, UNIT)])
            return jnp.concatenate(found, 1).astype(jnp.int32)

        def gather(turn, carry):
            entry = indices(turn)
            spots_now = places(turn)
            low_part = lax.bitwise_and(entry, LANES - 1)
            high_part = lax.shift_right_logical(entry, 8)
            hot = (
                lax.broadcasted_iota(jnp.int32, (LANES, span), 0) == low_part
            ).astype(f32).astype(bf16)
            low_hot[turn] = hot
            both = jnp.concatenate([hot, hot], 0)
            left = jnp.concatenate([table[axis, window, :] for axis in range(3)], 0)
            mask = lax.broadcasted_iota(jnp.int32, (SPAN, span), 0) == high_part
            for (slot, chunk), cut in zip(spots_now, cuts):
                found = matmul(left, both[:, cut])
                for axis in range(3):
                    picked[axis, slot, chunk] = jnp.sum(
                        jnp.where(mask[:, cut], found[axis * SPAN : (axis + 1) * SPAN], 0.0),
                        axis=0,
                        keepdims=True,
                    )
            return carry

        lax.fori_loop(0, turns, gather, 0)

        entries = center_ref[8:16, lanes].astype(jnp.int32)
        block = lax.shift_right_logical(entries, 12)
        block_space = lax.shift_right_logical(block * 11, 5)
        block_depth = block - 3 * block_space
        nbr = [picked[axis, :, 0:tile] for axis in range(3)]
        nbr_species = jnp.floor((nbr[1] + 2.0 * SPREAD) * (1.0 / SPREAD))
        nbr_y = nbr[1] - SPREAD * (nbr_species - 1.5)
        rel = [
            nbr[0] + SIDE_LENGTH * (block_space - 1).astype(f32) - center_x,
            nbr_y - center_y,
            nbr[2] + SIDE_LENGTH * (block_depth - 1).astype(f32) - center_z,
        ]
        squared = rel[0] * rel[0] + rel[1] * rel[1] + rel[2] * rel[2]
        inverse = lax.rsqrt(squared + SOFT_CORE)
        distance = (squared + SOFT_CORE) * inverse
        direction = [part * inverse for part in rel]
        fraction = jnp.minimum(distance / CUTOFF_RADIUS, 1.0)
        shell = 1.0 - fraction * fraction
        cutoff = shell * shell
        live = (
            lax.broadcasted_iota(jnp.int32, (slots, tile), 0) < count_row
        ).astype(f32)
        for axis in range(3):
            harm_s[axis, :, 0:tile] = direction[axis]
        harm_s[3, :, 0:tile] = cutoff
        harm_s[4, :, 0:tile] = live
        harm_s[5, :, 0:tile] = nbr_species
        harm_s[6, :, 0:tile] = distance
        harm_s[7, 0:1, 0:tile] = center_ref[3:4, lanes]
        for part in range(4):
            envs[part] = jnp.zeros(envs.shape[1:], f32)
            genvs[part] = jnp.zeros(genvs.shape[1:], f32)

        basis_id = lax.broadcasted_iota(jnp.int32, (8, span), 0).astype(f32)
        spots = basis_id * (CUTOFF_RADIUS / 7)
        sharpness = (7 / CUTOFF_RADIUS) ** 2

        def row(found, kind):
            return jnp.concatenate([harm_s[kind, slot, chunk] for slot, chunk in found], 1)

        def per_atom(found, ref, part):
            return jnp.concatenate([ref[part, :, chunk] for slot, chunk in found], 1)

        def put_row(found, kind, value):
            for (slot, chunk), cut in zip(found, cuts):
                rows_s[kind, slot, chunk] = value[:, cut]

        def add_row(found, kind, value):
            for (slot, chunk), cut in zip(found, cuts):
                rows_s[kind, slot, chunk] += value[:, cut]

        def add_atoms(found, ref, part, value):
            for (slot, chunk), cut in zip(found, cuts):
                ref[part, :, chunk] += value[:, cut]

        def first(turn, carry):
            found = places(turn)
            spread = row(found, 6) - spots
            radial = jnp.exp(-sharpness * spread * spread)
            radial_s[turn] = radial * (-2.0 * sharpness * spread)
            center_species = jnp.concatenate(
                [harm_s[7, 0:1, chunk] for slot, chunk in found], 1
            )
            species_hot = jnp.where(
                basis_id < 4.0,
                (basis_id == center_species).astype(f32),
                (basis_id - 4.0 == row(found, 5)).astype(f32),
            )
            features = jnp.concatenate([radial, species_hot, species_hot, species_hot], 0)
            pre = matmul(first_w[...], features.astype(bf16))
            bent = jnp.tanh(pre)
            mixed = pre * bent
            hidden = (pre + mixed).astype(bf16)
            slope_one[turn] = ((1.0 + bent) * (1.0 + (pre - mixed))).astype(bf16)
            raw = matmul(two_out_t[...], hidden)
            raw_s[turn] = raw
            latent = raw * row(found, 3)
            latent_b = latent.astype(bf16)
            latent_s[turn] = latent_b
            amp = matmul(env_t[...], latent_b) * row(found, 4)
            amp_s[turn] = amp
            add_atoms(found, envs, 0, amp)
            for axis in range(3):
                add_atoms(found, envs, 1 + axis, amp * row(found, axis))
            return carry

        lax.fori_loop(0, turns, first, 0)
        for part in range(4):
            envs[part] = envs[part] * (1.0 / slots)

        def second(turn, carry):
            found = places(turn)
            amp = amp_s[turn]
            ways = [row(found, axis) for axis in range(3)]
            env = [per_atom(found, envs, part) for part in range(4)]
            mix = env[0] + env[1] * ways[0] + env[2] * ways[1] + env[3] * ways[2]
            scalars = (amp * mix).astype(bf16)
            joined = jnp.concatenate([latent_s[turn], scalars], 0)
            pre = matmul(lat_in_t[...], joined)
            bent = jnp.tanh(pre)
            mixed = pre * bent
            slope = ((1.0 + bent) * (1.0 + (pre - mixed))).astype(bf16)
            rest = jnp.sum((pre + mixed) * energy_col[:, 0:1], axis=0, keepdims=True)
            cutoff_row = row(found, 3)
            weight = cutoff_row * row(found, 4)
            line = jnp.sum(readout_col[:, 0:1] * raw_s[turn], axis=0, keepdims=True)
            put_row(found, 0, line * cutoff_row + rest)
            back = matmul(lat_back[...], slope) * weight
            glat_s[turn] = back[0:64]
            gscal = back[64:96]
            mix_s[turn] = gscal * mix
            gprod = gscal * amp
            add_atoms(found, genvs, 0, gprod)
            for axis in range(3):
                add_atoms(found, genvs, 1 + axis, gprod * ways[axis])
                put_row(
                    found, 1 + axis, jnp.sum(gprod * env[1 + axis], axis=0, keepdims=True)
                )
            return carry

        lax.fori_loop(0, turns, second, 0)
        for part in range(4):
            genvs[part] = genvs[part] * (1.0 / slots)

        def third(turn, carry):
            found = places(turn)
            amp = amp_s[turn]
            ways = [row(found, axis) for axis in range(3)]
            live_row = row(found, 4)
            cutoff_row = row(found, 3)
            genv = [per_atom(found, genvs, part) for part in range(4)]
            gamp = (
                mix_s[turn] + genv[0] + genv[1] * ways[0] + genv[2] * ways[1] + genv[3] * ways[2]
            ) * live_row
            for axis in range(3):
                add_row(found, 1 + axis, jnp.sum(amp * genv[1 + axis], axis=0, keepdims=True))
            glat = (
                glat_s[turn]
                + matmul(env_w[...], gamp.astype(bf16))
                + readout_col[:, 0:1] * (cutoff_row * live_row)
            )
            put_row(found, 4, jnp.sum(glat * raw_s[turn], axis=0, keepdims=True))
            ghidden = matmul(two_out[...], (glat * cutoff_row).astype(bf16))
            gpre = (ghidden * slope_one[turn].astype(f32)).astype(bf16)
            gradial = matmul(radial_w[...], gpre)[0:8]
            put_row(found, 5, jnp.sum(gradial * radial_s[turn], axis=0, keepdims=True))
            return carry

        lax.fori_loop(0, turns, third, 0)

        got = [rows_s[kind, :, 0:tile] for kind in range(6)]
        pair = got[0]
        back_ref[3:4, lanes] = jnp.sum(
            jnp.where(live > 0.0, pair * cutoff, 0.0), axis=0, keepdims=True
        )
        gcut = got[4] + pair * live
        gdist = got[5] - gcut * shell * fraction * (4.0 / CUTOFF_RADIUS)
        gdir = [got[1 + axis] for axis in range(3)]
        along = gdir[0] * direction[0] + gdir[1] * direction[1] + gdir[2] * direction[2]
        push = gdist - along * inverse
        grel = [
            jnp.where(live > 0.0, gdir[axis] * inverse + direction[axis] * push, 0.0)
            for axis in range(3)
        ]
        for axis in range(3):
            back_ref[axis : axis + 1, lanes] = -jnp.sum(grel[axis], axis=0, keepdims=True)
            picked[axis, :, 0:tile] = grel[axis]
            picked[axis, :, tile : tile + UNIT] = jnp.zeros((slots, UNIT), f32)
            for other in range(3):
                virial_s[3 * axis + other] += rel[axis] * grel[other]

        def scatter(turn, carry):
            found = places(turn)
            high_part = lax.shift_right_logical(indices(turn), 8)
            mask = lax.broadcasted_iota(jnp.int32, (SPAN, span), 0) == high_part
            grads = [
                jnp.concatenate([picked[axis, slot, chunk] for slot, chunk in found], 1)
                for axis in range(3)
            ]
            spread = jnp.concatenate(
                [jnp.where(mask, grad, 0.0).astype(bf16) for grad in grads], 0
            )
            added = matmul_nt(spread, low_hot[turn])
            for axis in range(3):
                ghalo_ref[axis, window, :] += added[axis * SPAN : (axis + 1) * SPAN]
            return carry

        lax.fori_loop(0, turns, scatter, 0)
        return carry

    lax.fori_loop(0, tiles, one_tile, 0)
    for entry in range(9):
        folded = jnp.sum(virial_s[entry], axis=0, keepdims=True)
        part = folded[:, 0:128]
        for chunk in range(1, tile // 128):
            part = part + folded[:, 128 * chunk : 128 * (chunk + 1)]
        virial_ref[entry : entry + 1, :] = -part
    virial_ref[9:16, :] = jnp.zeros((7, 128), f32)


def edge_call(place, halo, center, weights, readout, tile, members):
    slots, atoms = 8, center.shape[1]
    rows = halo.shape[1]
    f32, bf16 = jnp.float32, jnp.bfloat16
    vmem = pl.BlockSpec(memory_space=pltpu.VMEM)
    shapes = (
        jax.ShapeDtypeStruct((3, rows, LANES), f32),
        jax.ShapeDtypeStruct((8, atoms), f32),
        jax.ShapeDtypeStruct((16, 128), f32),
    )
    turns = slots * tile // (UNITS * UNIT)
    span = UNITS * UNIT
    wide = tile + UNIT
    scratch = [
        pltpu.VMEM((3, rows, 2 * LANES), bf16),
        pltpu.VMEM((256, 32), bf16),
        pltpu.VMEM((64, 256), bf16),
        pltpu.VMEM((256, 64), bf16),
        pltpu.VMEM((32, 64), bf16),
        pltpu.VMEM((64, 32), bf16),
        pltpu.VMEM((256, 96), bf16),
        pltpu.VMEM((96, 256), bf16),
        pltpu.VMEM((256, 8), f32),
        pltpu.VMEM((16, 256), bf16),
        pltpu.VMEM((64, 8), f32),
        pltpu.VMEM((3, slots, wide), f32),
        pltpu.VMEM((turns, LANES, span), bf16),
        pltpu.VMEM((turns, 8, span), f32),
        pltpu.VMEM((8, 8, wide), f32),
        pltpu.VMEM((turns, 256, span), bf16),
        pltpu.VMEM((turns, 64, span), f32),
        pltpu.VMEM((turns, 64, span), bf16),
        pltpu.VMEM((turns, 32, span), f32),
        pltpu.VMEM((turns, 32, span), f32),
        pltpu.VMEM((turns, 64, span), f32),
        pltpu.VMEM((8, slots, wide), f32),
        pltpu.VMEM((4, 32, wide), f32),
        pltpu.VMEM((4, 32, wide), f32),
        pltpu.VMEM((6, slots, wide), f32),
        pltpu.VMEM((9, slots, tile), f32),
        pltpu.SMEM((slots * (tile // UNIT) + slots + UNITS,), jnp.int32),
        pltpu.SMEM((slots * (tile // UNIT) + slots + UNITS,), jnp.int32),
    ]
    return pl.pallas_call(
        functools.partial(edge_kernel, UNITS, tile, members),
        out_shape=shapes,
        in_specs=[pl.BlockSpec(memory_space=pltpu.SMEM)] + [vmem] * 4,
        out_specs=(vmem,) * 3,
        scratch_shapes=scratch,
        compiler_params=pltpu.CompilerParams(vmem_limit_bytes=48 * 1024 * 1024),
    )(place, halo, center, weights, readout)


def pack_weights(species_table, w_two_in, w_two_out, w_env, w_lat_in, w_lat_out):
    def wide(part):
        return jnp.pad(part, ((0, 0), (0, w_two_in.shape[1] - part.shape[1])))

    table = jnp.pad(species_table, ((0, 4), (0, 0)))
    return jnp.concatenate(
        [w_two_in, w_lat_in, w_two_out.T, w_lat_out.T, wide(w_env.T), wide(table)], 0
    )


def pack_atoms(positions, species, neighbours, counts):
    atoms = positions.shape[-1]
    f32 = jnp.float32
    return jnp.concatenate(
        [
            positions.reshape(3, atoms),
            species.reshape(1, atoms).astype(f32),
            counts.reshape(1, atoms).astype(f32),
            jnp.zeros((3, atoms), f32),
            neighbours.reshape(-1, atoms).astype(f32),
        ],
        0,
    )


def send(source, target, send_sem, recv_sem, space, depth):
    return pltpu.make_async_remote_copy(
        src_ref=source,
        dst_ref=target,
        send_sem=send_sem,
        recv_sem=recv_sem,
        device_id=(space, depth),
        device_id_type=pl.DeviceIdType.MESH,
    )


def greet(space, depth):
    pl.semaphore_signal(
        pltpu.get_barrier_semaphore(),
        inc=1,
        device_id=(space, depth),
        device_id_type=pl.DeviceIdType.MESH,
    )


def where_am_i(group):
    spaces, depths = lax.axis_size("space"), lax.axis_size("depth")
    space, depth = lax.axis_index("space"), lax.axis_index("depth")
    spot = lax.rem(space, group)
    first = space - spot
    before = lax.rem(first - 1 + spaces, spaces)
    after = lax.rem(first + group, spaces)
    return spaces, depths, space, depth, spot, first, before, after


def collect_kernel(
    group,
    packed_ref,
    halo_ref,
    center_ref,
    own,
    depth_send,
    depth_recv,
    part_send,
    part_recv,
    column_send,
    column_recv,
    edge_send,
    edge_recv,
    relay_send,
    relay_recv,
):
    spaces, depths, space, depth, spot, first, before, after = where_am_i(group)
    atoms = packed_ref.shape[1]
    share = atoms // group
    up, down = lax.rem(depth + 1, depths), lax.rem(depth + depths - 1, depths)
    mates = [first + lax.rem(spot + off, group) for off in range(1, group)]
    side = lax.rem(space, 2)
    twin = space + 1 - 2 * side
    at_start, at_end = spot == 0, spot == group - 1
    at_edge = jnp.logical_or(at_start, at_end)
    edge_from = jnp.where(side == 0, after, before)

    greet(space, up)
    greet(space, down)
    for mate in mates:
        greet(mate, depth)
    greet(edge_from, depth)
    expected = 2 + (group - 1) + (group // 2) * at_edge.astype(jnp.int32)

    def piece(start, part):
        return halo_ref.at[:, pl.ds(pl.multiple_of(start + 16 * part, 16), 16), :]

    column = (spot + 1) * GAP
    for part in range(4):
        for row in range(atoms // LANES):
            own[part, row : row + 1, :] = packed_ref[
                part : part + 1, row * LANES : (row + 1) * LANES
            ]
    piece(column, 1)[...] = own[...]
    pl.semaphore_wait(pltpu.get_barrier_semaphore(), expected)

    jumps = list(range(2, group, 2))
    half = group // 2
    depth_copies = [
        send(own, piece(column, 0), depth_send.at[0], depth_recv.at[0], space, up),
        send(own, piece(column, 2), depth_send.at[1], depth_recv.at[1], space, down),
    ]
    for copy in depth_copies:
        copy.start()

    def edges(part):
        base = jnp.where(at_start, lax.rem(first - group + spaces, spaces), after)
        start = jnp.where(at_start, (group + 1) * GAP, 0)
        return [
            send(
                piece(column, part),
                piece(start, part),
                edge_send.at[3 * member + part],
                edge_recv.at[part],
                base + 2 * member + side,
                depth,
            )
            for member in range(half)
        ]

    direct = {}
    for part in (1, 0, 2):
        if part != 1:
            depth_copies[part // 2].wait_recv()
        block = piece(column, part)

        @pl.when(at_edge)
        def _(part=part):
            for copy in edges(part):
                copy.start()

        for at, off in enumerate(jumps + [0]):
            slot = 3 * at + part
            target = mates[off - 1] if off else twin
            copy = send(block, block, column_send.at[slot], column_recv.at[slot], target, depth)
            copy.start()
            direct[at, part] = copy
        if part == 1:
            mine = pl.ds(pl.multiple_of(spot * share, 128), share)
            part_copies = []
            for off in range(1, group):
                copy = send(
                    packed_ref.at[:, off * share : (off + 1) * share],
                    center_ref.at[:, mine],
                    part_send.at[off - 1],
                    part_recv.at[off - 1],
                    mates[off - 1],
                    depth,
                )
                copy.start()
                part_copies.append(copy)
            center_ref[:, mine] = packed_ref[:, 0:share]

    relays = []
    edge_start = jnp.where(side == 0, (group + 1) * GAP, 0)
    for part in (1, 0, 2):
        for at, off in enumerate(jumps + [0]):
            if off:
                direct[at, part].wait_recv()
                block = piece((lax.rem(spot + group - off, group) + 1) * GAP, part)
            else:
                block = piece(edge_start, part)
                send(
                    block, block, edge_send.at[part], edge_recv.at[part], edge_from, depth
                ).wait_recv()
            slot = 3 * at + part
            copy = send(block, block, relay_send.at[slot], relay_recv.at[slot], twin, depth)
            copy.start()
            relays.append(copy)

    for part in range(3):
        direct[len(jumps), part].wait_recv()
    for copy in part_copies + relays:
        copy.wait_recv()
    for copy in depth_copies + part_copies + list(direct.values()) + relays:
        copy.wait_send()

    @pl.when(at_edge)
    def _():
        for part in range(3):
            for copy in edges(part):
                copy.wait_send()


def collect_call(packed, group):
    kinds, atoms = packed.shape
    rows = (group + 2) * GAP
    f32 = jnp.float32
    vmem = pl.BlockSpec(memory_space=pltpu.VMEM)
    dma = pltpu.SemaphoreType.DMA
    half = group // 2
    return pl.pallas_call(
        functools.partial(collect_kernel, group),
        out_shape=(
            jax.ShapeDtypeStruct((4, rows, LANES), f32),
            jax.ShapeDtypeStruct((kinds, atoms), f32),
        ),
        in_specs=[vmem],
        out_specs=(vmem,) * 2,
        scratch_shapes=[
            pltpu.VMEM((4, atoms // LANES, LANES), f32),
            dma((2,)),
            dma((2,)),
            dma((group - 1,)),
            dma((group - 1,)),
            dma((3 * half,)),
            dma((3 * half,)),
            dma((3 * half,)),
            dma((3,)),
            dma((3 * half,)),
            dma((3 * half,)),
        ],
        compiler_params=pltpu.CompilerParams(
            collective_id=0, has_side_effects=True, vmem_limit_bytes=24 * 1024 * 1024
        ),
    )(packed)


def return_kernel(
    group,
    ghalo_ref,
    back_ref,
    virial_ref,
    force_ref,
    energy_ref,
    total_ref,
    columns,
    halves,
    sums,
    blocks,
    flat,
    summed,
    by_member,
    by_depth,
    by_group,
    twin_send,
    twin_recv,
    column_send,
    column_recv,
    edge_send,
    edge_recv,
    part_send,
    part_recv,
    block_send,
    block_recv,
    member_send,
    member_recv,
    layer_send,
    layer_recv,
    group_send,
    group_recv,
):
    spaces, depths, space, depth, spot, first, before, after = where_am_i(group)
    atoms = back_ref.shape[1]
    share = atoms // group
    groups = spaces // group
    up, down = lax.rem(depth + 1, depths), lax.rem(depth + depths - 1, depths)
    mates = [first + lax.rem(spot + off, group) for off in range(1, group)]
    layers = [lax.rem(depth + off, depths) for off in range(1, depths)]
    peers = [lax.rem(space + off * group, spaces) for off in range(1, groups)]
    at_start, at_end = spot == 0, spot == group - 1

    for mate in mates:
        greet(mate, depth)
    for layer in layers:
        greet(space, layer)
    for peer in peers:
        greet(peer, depth)
    side = lax.rem(space, 2)
    twin = space + 1 - 2 * side
    twin_spot = spot + 1 - 2 * side
    jumps = list(range(2, group, 2))
    at_edge = jnp.logical_or(at_start, at_end)
    edge_to = jnp.where(side == 0, after, before)

    @pl.when(at_edge)
    def _():
        base = jnp.where(at_start, lax.rem(first - group + spaces, spaces), after)
        for member in range(group // 2):
            greet(base + 2 * member + side, depth)

    pl.semaphore_wait(
        pltpu.get_barrier_semaphore(), (group - 1) + (depths - 1) + (groups - 1) + 1
    )

    started = []

    def go(*args):
        copy = send(*args)
        copy.start()
        started.append(copy)
        return copy

    by_member[spot] = virial_ref[...]
    mine = by_member.at[spot]
    member_copies = [
        go(mine, mine, member_send.at[off], member_recv.at[off], mate, depth)
        for off, mate in enumerate(mates)
    ]

    def column_starts(spot_at, side_at):
        starts = [(lax.rem(spot_at + off, group) + 1) * GAP for off in jumps + [0]]
        return starts + [jnp.where(side_at == 0, (group + 1) * GAP, 0)]

    def rows_at(start, part):
        return pl.ds(pl.multiple_of(start + 16 * part, 16), 16)

    layer_order = (0, 2, 1)
    own_kind, edge_kind = len(jumps), len(jumps) + 1
    kind_order = [edge_kind] + list(range(len(jumps) + 1))
    theirs = column_starts(twin_spot, 1 - side)
    kinds = column_starts(spot, side)
    halfway = {}
    for part in layer_order:
        for kind in kind_order:
            slot = 3 * kind + part
            halfway[kind, part] = go(
                ghalo_ref.at[:, rows_at(theirs[kind], part), :],
                halves.at[kind, :, 16 * part : 16 * part + 16, :],
                twin_send.at[slot],
                twin_recv.at[slot],
                twin,
                depth,
            )
    part_copies = []
    for off, mate in enumerate(mates):
        theirs = pl.ds(pl.multiple_of((mate - first) * share, 128), share)
        part = (group - 1 - off) * share
        part_copies.append(
            go(
                back_ref.at[:, theirs],
                flat.at[:, part : part + share],
                part_send.at[off],
                part_recv.at[off],
                mate,
                depth,
            )
        )
    own_part = pl.ds(pl.multiple_of(spot * share, 128), share)
    flat[:, 0:share] = back_ref[:, own_part]

    crossing = {}
    for part in layer_order:
        rows = slice(16 * part, 16 * part + 16)
        for kind in kind_order[:-1]:
            halfway[kind, part].wait_recv()
            sums[kind, :, rows, :] = (
                ghalo_ref[:, rows_at(kinds[kind], part), :] + halves[kind, :, rows, :]
            )
            if kind == edge_kind:
                slot = len(jumps) + spot // 2
                go(
                    sums.at[kind, :, rows, :],
                    columns.at[slot, :, rows, :],
                    edge_send.at[part],
                    edge_recv.at[3 * (spot // 2) + part],
                    edge_to,
                    depth,
                )
            else:
                crossing[kind, part] = go(
                    sums.at[kind, :, rows, :],
                    columns.at[kind, :, rows, :],
                    column_send.at[3 * kind + part],
                    column_recv.at[3 * kind + part],
                    mates[jumps[kind] - 1],
                    depth,
                )

    for copy in member_copies:
        copy.wait_recv()
    level = by_member[0]
    for member in range(1, group):
        level = level + by_member[member]
    by_depth[depth] = level
    mine_depth = by_depth.at[depth]
    layer_copies = [
        go(mine_depth, mine_depth, layer_send.at[off], layer_recv.at[off], space, layer)
        for off, layer in enumerate(layers)
    ]
    for copy in layer_copies:
        copy.wait_recv()
    level = by_depth[0]
    for layer in range(1, depths):
        level = level + by_depth[layer]
    place = space // group
    by_group[place] = level
    mine_group = by_group.at[place]
    group_copies = [
        go(mine_group, mine_group, group_send.at[off], group_recv.at[off], peer, depth)
        for off, peer in enumerate(peers)
    ]

    block_copies = []
    for part in layer_order:
        rows = slice(16 * part, 16 * part + 16)
        halfway[own_kind, part].wait_recv()
        total = ghalo_ref[:, rows_at(kinds[own_kind], part), :] + halves[own_kind, :, rows, :]
        for kind in range(len(jumps)):
            crossing[kind, part].wait_recv()
            total = total + columns[kind, :, rows, :]
        summed[:, rows, :] = total

        @pl.when(at_edge)
        def _(part=part, rows=rows):
            extra = jnp.zeros((3, 16, LANES), jnp.float32)
            for member in range(group // 2):
                block = columns.at[len(jumps) + member, :, rows, :]
                send(
                    block,
                    block,
                    edge_send.at[part],
                    edge_recv.at[3 * member + part],
                    edge_to,
                    depth,
                ).wait_recv()
                extra = extra + block[...]
            summed[:, rows, :] = summed[:, rows, :] + extra

        if part != 1:
            at, layer = part // 2, (down, up)[part // 2]
            block_copies.append(
                go(
                    summed.at[:, rows, :],
                    blocks.at[at],
                    block_send.at[at],
                    block_recv.at[at],
                    space,
                    layer,
                )
            )

    for copy in part_copies:
        copy.wait_recv()
    energy_ref[...] = flat[3:4, :]
    for copy in group_copies:
        copy.wait_recv()
    level = by_group[0]
    for member in range(1, groups):
        level = level + by_group[member]
    entries = jnp.sum(level, axis=1, keepdims=True)
    shape = (8, 128)
    row_id = lax.broadcasted_iota(jnp.int32, shape, 0)
    column_id = lax.broadcasted_iota(jnp.int32, shape, 1)
    table = jnp.zeros(shape, jnp.float32)
    for entry in range(9):
        here = jnp.logical_and(row_id == entry // 3, column_id == entry % 3)
        table = jnp.where(here, entries[entry : entry + 1, :], table)
    total_ref[...] = table[0:3, 0:3]
    for copy in block_copies:
        copy.wait_recv()
    blocks[0] = summed[:, 16:32, :] + blocks[0] + blocks[1]
    for part in range(3):
        for row in range(atoms // LANES):
            lanes = slice(row * LANES, (row + 1) * LANES)
            force_ref[part, :, lanes] = -(
                blocks[0, part, row : row + 1, :] + flat[part : part + 1, lanes]
            )
    for copy in started:
        copy.wait_send()


def return_call(ghalo, back, virial, group):
    atoms = back.shape[1]
    f32 = jnp.float32
    depths = lax.axis_size("depth")
    groups = lax.axis_size("space") // group
    vmem = pl.BlockSpec(memory_space=pltpu.VMEM)
    dma = pltpu.SemaphoreType.DMA
    half = group // 2
    counts = [
        3 * (half + 1),
        3 * (half + 1),
        3 * half,
        3 * half,
        3,
        3 * half,
        group - 1,
        group - 1,
        2,
        2,
        group - 1,
        group - 1,
        depths - 1,
        depths - 1,
        groups - 1,
        groups - 1,
    ]
    return pl.pallas_call(
        functools.partial(return_kernel, group),
        out_shape=(
            jax.ShapeDtypeStruct((3, 1, atoms), f32),
            jax.ShapeDtypeStruct((1, atoms), f32),
            jax.ShapeDtypeStruct((3, 3), f32),
        ),
        in_specs=[vmem] * 3,
        out_specs=(vmem,) * 3,
        scratch_shapes=[
            pltpu.VMEM((group - 1, 3, GAP, LANES), f32),
            pltpu.VMEM((half + 1, 3, GAP, LANES), f32),
            pltpu.VMEM((half + 1, 3, GAP, LANES), f32),
            pltpu.VMEM((2, 3, 16, LANES), f32),
            pltpu.VMEM((8, atoms), f32),
            pltpu.VMEM((3, GAP, LANES), f32),
            pltpu.VMEM((group, 16, 128), f32),
            pltpu.VMEM((depths, 16, 128), f32),
            pltpu.VMEM((groups, 16, 128), f32),
        ]
        + [dma((count,)) for count in counts],
        compiler_params=pltpu.CompilerParams(
            collective_id=1, has_side_effects=True, vmem_limit_bytes=24 * 1024 * 1024
        ),
    )(ghalo, back, virial)


def per_device(
    positions,
    species,
    neighbours,
    counts,
    species_table,
    w_two_in,
    w_two_out,
    w_env,
    w_lat_in,
    w_lat_out,
    readout,
):
    atom_count = positions.shape[-1]
    weights = pack_weights(species_table, w_two_in, w_two_out, w_env, w_lat_in, w_lat_out)
    halo, center = collect_call(pack_atoms(positions, species, neighbours, counts), GROUP)
    space = lax.axis_index("space")
    place = jnp.stack([space // GROUP * GROUP, lax.axis_index("depth")]).astype(jnp.int32)
    ghalo, back, virial = edge_call(
        place, halo, center, weights, readout.reshape(1, -1), TILE, GROUP
    )
    forces, energies, virial_total = return_call(ghalo, back, virial, GROUP)
    return (
        forces.reshape(3, 1, 1, atom_count),
        energies.reshape(1, 1, atom_count),
        virial_total,
    )


def solution(mesh):
    placed = (
        P(None, "space", "depth", None),
        P("space", "depth", None),
        P(None, "space", "depth", None),
        P("space", "depth", None),
        P(),
        P(),
        P(),
        P(),
        P(),
        P(),
        P(),
    )
    return jax.shard_map(
        per_device,
        mesh=mesh,
        in_specs=placed,
        out_specs=(P(None, "space", "depth", None), P("space", "depth", None), P()),
        check_vma=False,
    )
```

```python
import functools

import jax
import jax.numpy as jnp
from jax import lax
from jax.experimental import pallas as pl
from jax.experimental.pallas import tpu as pltpu
from jax.sharding import PartitionSpec as P

CUTOFF_RADIUS = 5.0
SOFT_CORE = 0.25

GROUP = 4
TILE = 1024
UNITS = 8
UNIT = 256
SIDE_LENGTH = 32.0
SPREAD = 36.0
GAP = 48
SPAN = 144
LANES = 256


def pieces(value, count):
    parts = []
    rest = value
    for _ in range(count):
        part = rest.astype(jnp.bfloat16)
        parts.append(part)
        rest = rest - part.astype(jnp.float32)
    return parts


def matmul(left, right):
    return jnp.dot(left, right, preferred_element_type=jnp.float32)


def matmul_nt(left, right):
    return lax.dot_general(
        left, right, (((1,), (1,)), ((), ())), preferred_element_type=jnp.float32
    )


def edge_kernel(
    units,
    tile,
    members,
    place_ref,
    halo_ref,
    center_ref,
    weight_ref,
    readout_ref,
    ghalo_ref,
    back_ref,
    virial_ref,
    table,
    first_w,
    two_out_t,
    two_out,
    lat_in_t,
    lat_back,
    energy_col,
    radial_w,
    readout_col,
    near,
    entry_s,
    low_hot,
    radial_s,
    slope_one,
    raw_s,
    latent_s,
    amp_s,
    mix_s,
    glat_s,
    rows_s,
    rows_back,
    envs,
    genvs,
    virial_s,
    unit_slot,
    unit_chunk,
):
    slots, atoms = 8, center_ref.shape[1]
    tiles = atoms // tile
    rows = halo_ref.shape[1]
    f32, bf16 = jnp.float32, jnp.bfloat16
    base_space = place_ref[0]
    base_depth = place_ref[1]

    row_id = lax.broadcasted_iota(jnp.int32, (rows, LANES), 0)
    space_of = (row_id // GAP - 1 + base_space).astype(f32)
    depth_of = (lax.rem(row_id, GAP) // 16 - 1 + base_depth).astype(f32)
    half = SIDE_LENGTH / 2
    local = [
        halo_ref[0] - (SIDE_LENGTH * space_of + half),
        halo_ref[1] - half + SPREAD * (halo_ref[3] - 1.5),
        halo_ref[2] - (SIDE_LENGTH * depth_of + half),
    ]
    for axis in range(3):
        high, low = pieces(local[axis], 2)
        table[axis, :, 0:LANES] = high
        table[axis, :, LANES : 2 * LANES] = low

    ghalo_ref[...] = jnp.zeros_like(ghalo_ref)
    back_ref[...] = jnp.zeros_like(back_ref)
    virial_s[...] = jnp.zeros_like(virial_s)

    w_one = weight_ref[0:136]
    lat_in = weight_ref[136:232].astype(f32)
    two_out_now = weight_ref[232:296].astype(f32)
    lat_out_now = weight_ref[296:360].astype(f32)
    env_now = weight_ref[360:392].astype(f32)[:, 0:64]
    emb = weight_ref[392:396].astype(f32)[:, 0:64].astype(bf16)
    center_part = matmul(emb, w_one[0:64])
    nbr_part = matmul(emb, w_one[64:128])
    species_part = 0.5 * jnp.concatenate([center_part, nbr_part], 0)
    radial_half = 0.5 * w_one[128:136].astype(f32)
    split = [part.astype(f32) for part in pieces(species_part, 3)]
    first_w[...] = jnp.concatenate([radial_half] + split, 0).T.astype(bf16)
    radial_w[...] = jnp.concatenate([radial_half, jnp.zeros_like(radial_half)], 0).astype(bf16)
    amp_high, amp_low = pieces(matmul(env_now.astype(bf16), two_out_now.astype(bf16)), 2)
    latent_rows = jnp.concatenate(
        [two_out_now, amp_high.astype(f32), amp_low.astype(f32)], 0
    )
    readout_row = readout_ref[...]
    wide_row = jnp.broadcast_to(readout_row, (8, readout_row.shape[1]))
    line_row = jnp.dot(
        wide_row, two_out_now, precision=lax.Precision.HIGHEST, preferred_element_type=f32
    )
    line_rows = [part.astype(f32)[0:1] for part in pieces(line_row, 3)]
    two_out_t[0:128] = latent_rows.astype(bf16)
    two_out_t[128:144] = jnp.concatenate(
        line_rows + [jnp.zeros((13, two_out_now.shape[1]), f32)], 0
    ).astype(bf16)
    two_out[...] = latent_rows.T.astype(bf16)
    lat_in_t[...] = (0.5 * lat_in).T.astype(bf16)
    last_row = lax.dot_general(
        jnp.broadcast_to(readout_row, (8, readout_row.shape[1])),
        lat_out_now,
        (((1,), (0,)), ((), ())),
        precision=lax.Precision.HIGHEST,
        preferred_element_type=f32,
    )
    lat_back[...] = (0.5 * lat_in * last_row[0:1]).astype(bf16)
    energy_col[...] = last_row.T
    readout_col[...] = jnp.broadcast_to(readout_row, (8, readout_row.shape[1])).T

    chunks = tile // UNIT
    span = units * UNIT
    cuts = [slice(unit * UNIT, (unit + 1) * UNIT) for unit in range(units)]
    sharpness = (7 / CUTOFF_RADIUS) ** 2

    def one_tile(step, carry):
        lanes = pl.ds(pl.multiple_of(step * tile, tile), tile)
        count_row = center_ref[4:5, lanes]

        total = 0
        for chunk in range(chunks):
            depth = jnp.max(count_row[:, chunk * UNIT : (chunk + 1) * UNIT]).astype(jnp.int32)
            for slot in range(slots):
                unit_slot[total + slot] = slot
                unit_chunk[total + slot] = chunk
            total = total + depth
        for unit in range(units - 1):
            unit_slot[total + unit] = slots
            unit_chunk[total + unit] = 0
        turns = (total + (units - 1)) // units

        member = step // (tiles // members)
        window = pl.ds(pl.multiple_of(member * GAP, 16), SPAN)
        origin_x = SIDE_LENGTH * (base_space + member).astype(f32) + half
        origin_z = SIDE_LENGTH * base_depth.astype(f32) + half
        for part in range(4):
            envs[part] = jnp.zeros(envs.shape[1:], f32)
            genvs[part] = jnp.zeros(genvs.shape[1:], f32)

        def places(turn):
            found = []
            for unit in range(units):
                slot = unit_slot[turn * units + unit]
                chunk = unit_chunk[turn * units + unit]
                inner = pl.ds(pl.multiple_of(chunk * UNIT, UNIT), UNIT)
                outer = pl.ds(pl.multiple_of(step * tile + chunk * UNIT, UNIT), UNIT)
                found.append((slot, inner, outer))
            return found

        def row(turn, kind):
            return jnp.concatenate(
                [rows_s[turn, kind, unit : unit + 1, :] for unit in range(units)], 1
            )

        def per_atom(found, ref, part):
            return jnp.concatenate([ref[part, :, inner] for _, inner, _ in found], 1)

        def put_row(ref, kind, value):
            for unit, cut in enumerate(cuts):
                ref[kind, unit : unit + 1, :] = value[:, cut]

        def add_row(ref, kind, value):
            for unit, cut in enumerate(cuts):
                ref[kind, unit : unit + 1, :] += value[:, cut]

        def add_atoms(found, ref, part, value):
            for (_, inner, _), cut in zip(found, cuts):
                ref[part, :, inner] += value[:, cut]

        def entry_row(turn):
            return jnp.concatenate(
                [entry_s[turn, unit : unit + 1, :] for unit in range(units)], 1
            )

        def first(turn, carry):
            found = places(turn)
            for unit, (slot, _, outer) in enumerate(found):
                one = slice(unit, unit + 1)
                entry = center_ref[pl.ds(jnp.minimum(slot, slots - 1) + 8, 1), outer]
                entry_s[turn, one, :] = entry.astype(jnp.int32)
                for kind in range(4):
                    near[3 + kind, one, :] = center_ref[kind : kind + 1, outer]
                near[7, one, :] = center_ref[4:5, outer] - slot.astype(f32)
            entry = entry_row(turn)
            low_part = lax.bitwise_and(entry, LANES - 1)
            high_part = lax.shift_right_logical(entry, 8)
            hot = (
                lax.broadcasted_iota(jnp.int32, (LANES, span), 0) == low_part
            ).astype(f32).astype(bf16)
            low_hot[turn] = hot
            both = jnp.concatenate([hot, hot], 0)
            left = jnp.concatenate([table[axis, window, :] for axis in range(3)], 0)
            mask = lax.broadcasted_iota(jnp.int32, (SPAN, span), 0) == high_part
            for unit, cut in enumerate(cuts):
                seen = matmul(left, both[:, cut])
                for axis in range(3):
                    near[axis, unit : unit + 1, :] = jnp.sum(
                        jnp.where(mask[:, cut], seen[axis * SPAN : (axis + 1) * SPAN], 0.0),
                        axis=0,
                        keepdims=True,
                    )

            block = lax.shift_right_logical(entry_s[turn], 12)
            block_space = lax.shift_right_logical(block * 11, 5)
            block_depth = block - 3 * block_space
            nbr_species = jnp.floor((near[1] + 2.0 * SPREAD) * (1.0 / SPREAD))
            rel = [
                near[0] + SIDE_LENGTH * (block_space - 1).astype(f32) - (near[3] - origin_x),
                near[1] - SPREAD * (nbr_species - 1.5) - (near[4] - half),
                near[2] + SIDE_LENGTH * (block_depth - 1).astype(f32) - (near[5] - origin_z),
            ]
            squared = rel[0] * rel[0] + rel[1] * rel[1] + rel[2] * rel[2] + SOFT_CORE
            inverse = lax.rsqrt(squared)
            distance = squared * inverse
            fraction = jnp.minimum(distance * (1.0 / CUTOFF_RADIUS), 1.0)
            shell = 1.0 - fraction * fraction
            for axis in range(3):
                rows_s[turn, axis] = rel[axis] * inverse
            rows_s[turn, 3] = shell * shell
            rows_s[turn, 4] = jnp.where(near[7] > 0.0, 1.0, 0.0)
            rows_s[turn, 5] = nbr_species
            rows_s[turn, 6] = distance
            rows_s[turn, 7] = inverse
            rows_s[turn, 8] = shell * fraction * (4.0 / CUTOFF_RADIUS)
            rows_s[turn, 9] = near[6]

            basis_id = lax.broadcasted_iota(jnp.int32, (8, span), 0).astype(f32)
            spread = row(turn, 6) - basis_id * (CUTOFF_RADIUS / 7)
            radial = jnp.exp(-sharpness * spread * spread)
            radial_s[turn] = radial * (-2.0 * sharpness * spread)
            species_hot = jnp.where(
                basis_id < 4.0,
                (basis_id == row(turn, 9)).astype(f32),
                (basis_id - 4.0 == row(turn, 5)).astype(f32),
            )
            features = jnp.concatenate([radial, species_hot, species_hot, species_hot], 0)
            pre = matmul(first_w[...], features.astype(bf16))
            bent = jnp.tanh(pre)
            mixed = pre * bent
            hidden = (pre + mixed).astype(bf16)
            slope_one[turn] = ((1.0 + bent) * (1.0 + (pre - mixed))).astype(bf16)
            latents = matmul(two_out_t[...], hidden)
            raw = latents[0:64]
            raw_s[turn] = raw
            latent_s[turn] = (raw * row(turn, 3)).astype(bf16)
            amp = latents[64:96] + latents[96:128]
            line = jnp.sum(latents[128:136], axis=0, keepdims=True)
            put_row(rows_back.at[turn], 0, line * row(turn, 3))
            amp_s[turn] = amp
            amp = amp * (row(turn, 3) * row(turn, 4))
            add_atoms(found, envs, 0, amp)
            for axis in range(3):
                add_atoms(found, envs, 1 + axis, amp * row(turn, axis))
            return carry

        lax.fori_loop(0, turns, first, 0)
        for part in range(4):
            envs[part] = envs[part] * (1.0 / slots)

        def second(turn, carry):
            found = places(turn)
            cutoff_row = row(turn, 3)
            weight = cutoff_row * row(turn, 4)
            amp = amp_s[turn] * weight
            ways = [row(turn, axis) for axis in range(3)]
            env = [per_atom(found, envs, part) for part in range(4)]
            mix = env[0] + env[1] * ways[0] + env[2] * ways[1] + env[3] * ways[2]
            scalars = (amp * mix).astype(bf16)
            joined = jnp.concatenate([latent_s[turn], scalars], 0)
            pre = matmul(lat_in_t[...], joined)
            bent = jnp.tanh(pre)
            mixed = pre * bent
            slope = ((1.0 + bent) * (1.0 + (pre - mixed))).astype(bf16)
            rest = jnp.sum((pre + mixed) * energy_col[:, 0:1], axis=0, keepdims=True)
            back_rows = rows_back.at[turn]
            add_row(back_rows, 0, rest)
            back = matmul(lat_back[...], slope) * weight
            glat_s[turn] = back[0:64]
            gscal = back[64:96]
            mix_s[turn] = gscal * mix
            gprod = gscal * amp
            add_atoms(found, genvs, 0, gprod)
            for axis in range(3):
                add_atoms(found, genvs, 1 + axis, gprod * ways[axis])
                put_row(
                    back_rows, 1 + axis, jnp.sum(gprod * env[1 + axis], axis=0, keepdims=True)
                )
            return carry

        lax.fori_loop(0, turns, second, 0)
        for part in range(4):
            genvs[part] = genvs[part] * (1.0 / slots)

        def third(turn, carry):
            found = places(turn)
            ways = [row(turn, axis) for axis in range(3)]
            live_row = row(turn, 4)
            cutoff_row = row(turn, 3)
            weight = cutoff_row * live_row
            amp_raw = amp_s[turn]
            amp = amp_raw * weight
            genv = [per_atom(found, genvs, part) for part in range(4)]
            gamp = (
                mix_s[turn] + genv[0] + genv[1] * ways[0] + genv[2] * ways[1] + genv[3] * ways[2]
            ) * live_row
            for axis in range(3):
                put_row(near, axis, jnp.sum(amp * genv[1 + axis], axis=0, keepdims=True))
            glat = glat_s[turn] + readout_col[:, 0:1] * weight
            put_row(
                near,
                3,
                jnp.sum(glat * raw_s[turn], axis=0, keepdims=True)
                + jnp.sum(gamp * amp_raw, axis=0, keepdims=True),
            )
            gamp_b = (gamp * cutoff_row).astype(bf16)
            glatents = jnp.concatenate([(glat * cutoff_row).astype(bf16), gamp_b, gamp_b], 0)
            ghidden = matmul(two_out[...], glatents)
            gpre = (ghidden * slope_one[turn].astype(f32)).astype(bf16)
            gradial = matmul(radial_w[...], gpre)[0:8]
            put_row(near, 4, jnp.sum(gradial * radial_s[turn], axis=0, keepdims=True))

            pair = rows_back[turn, 0]
            direction = [rows_s[turn, axis] for axis in range(3)]
            live, inverse = rows_s[turn, 4], rows_s[turn, 7]
            gdir = [near[axis] + rows_back[turn, 1 + axis] for axis in range(3)]
            gcut = near[3] + pair * live
            gdist = near[4] - gcut * rows_s[turn, 8]
            along = gdir[0] * direction[0] + gdir[1] * direction[1] + gdir[2] * direction[2]
            push = gdist - along * inverse
            grel = [
                (gdir[axis] * inverse + direction[axis] * push) * live for axis in range(3)
            ]
            energy = pair * rows_s[turn, 3] * live
            distance = rows_s[turn, 6]
            for axis in range(3):
                near[5 + axis] = grel[axis]
                rel = direction[axis] * distance
                for other in range(3):
                    virial_s[3 * axis + other] += rel * grel[other]
            for unit, (_, _, outer) in enumerate(found):
                for axis in range(3):
                    back_ref[axis : axis + 1, outer] -= grel[axis][unit : unit + 1]
                back_ref[3:4, outer] += energy[unit : unit + 1]

            high_part = lax.shift_right_logical(entry_row(turn), 8)
            mask = lax.broadcasted_iota(jnp.int32, (SPAN, span), 0) == high_part
            grads = [
                jnp.concatenate([near[5 + axis, unit : unit + 1, :] for unit in range(units)], 1)
                for axis in range(3)
            ]
            spread = jnp.concatenate(
                [jnp.where(mask, grad, 0.0).astype(bf16) for grad in grads], 0
            )
            added = matmul_nt(spread, low_hot[turn])
            for axis in range(3):
                ghalo_ref[axis, window, :] += added[axis * SPAN : (axis + 1) * SPAN]
            return carry

        lax.fori_loop(0, turns, third, 0)
        return carry

    lax.fori_loop(0, tiles, one_tile, 0)
    for entry in range(9):
        folded = jnp.sum(virial_s[entry], axis=0, keepdims=True)
        part = folded[:, 0:128]
        for chunk in range(1, UNIT // 128):
            part = part + folded[:, 128 * chunk : 128 * (chunk + 1)]
        virial_ref[entry : entry + 1, :] = -part
    virial_ref[9:16, :] = jnp.zeros((7, 128), f32)


def edge_call(place, halo, center, weights, readout, tile, members):
    slots, atoms = 8, center.shape[1]
    rows = halo.shape[1]
    f32, bf16 = jnp.float32, jnp.bfloat16
    vmem = pl.BlockSpec(memory_space=pltpu.VMEM)
    shapes = (
        jax.ShapeDtypeStruct((3, rows, LANES), f32),
        jax.ShapeDtypeStruct((8, atoms), f32),
        jax.ShapeDtypeStruct((16, 128), f32),
    )
    turns = slots * tile // (UNITS * UNIT)
    span = UNITS * UNIT
    scratch = [
        pltpu.VMEM((3, rows, 2 * LANES), bf16),
        pltpu.VMEM((256, 32), bf16),
        pltpu.VMEM((144, 256), bf16),
        pltpu.VMEM((256, 128), bf16),
        pltpu.VMEM((256, 96), bf16),
        pltpu.VMEM((96, 256), bf16),
        pltpu.VMEM((256, 8), f32),
        pltpu.VMEM((16, 256), bf16),
        pltpu.VMEM((64, 8), f32),
        pltpu.VMEM((8, UNITS, UNIT), f32),
        pltpu.VMEM((turns, UNITS, UNIT), jnp.int32),
        pltpu.VMEM((turns, LANES, span), bf16),
        pltpu.VMEM((turns, 8, span), f32),
        pltpu.VMEM((turns, 256, span), bf16),
        pltpu.VMEM((turns, 64, span), f32),
        pltpu.VMEM((turns, 64, span), bf16),
        pltpu.VMEM((turns, 32, span), f32),
        pltpu.VMEM((turns, 32, span), f32),
        pltpu.VMEM((turns, 64, span), f32),
        pltpu.VMEM((turns, 10, UNITS, UNIT), f32),
        pltpu.VMEM((turns, 4, UNITS, UNIT), f32),
        pltpu.VMEM((4, 32, tile), f32),
        pltpu.VMEM((4, 32, tile), f32),
        pltpu.VMEM((9, UNITS, UNIT), f32),
        pltpu.SMEM((slots * (tile // UNIT) + slots + UNITS,), jnp.int32),
        pltpu.SMEM((slots * (tile // UNIT) + slots + UNITS,), jnp.int32),
    ]
    return pl.pallas_call(
        functools.partial(edge_kernel, UNITS, tile, members),
        out_shape=shapes,
        in_specs=[pl.BlockSpec(memory_space=pltpu.SMEM)] + [vmem] * 4,
        out_specs=(vmem,) * 3,
        scratch_shapes=scratch,
        compiler_params=pltpu.CompilerParams(vmem_limit_bytes=48 * 1024 * 1024),
    )(place, halo, center, weights, readout)


def pack_weights(species_table, w_two_in, w_two_out, w_env, w_lat_in, w_lat_out):
    def wide(part):
        return jnp.pad(part, ((0, 0), (0, w_two_in.shape[1] - part.shape[1])))

    table = jnp.pad(species_table, ((0, 4), (0, 0)))
    return jnp.concatenate(
        [w_two_in, w_lat_in, w_two_out.T, w_lat_out.T, wide(w_env.T), wide(table)], 0
    )


def send(source, target, send_sem, recv_sem, space, depth):
    return pltpu.make_async_remote_copy(
        src_ref=source,
        dst_ref=target,
        send_sem=send_sem,
        recv_sem=recv_sem,
        device_id=(space, depth),
        device_id_type=pl.DeviceIdType.MESH,
    )


def greet(space, depth):
    pl.semaphore_signal(
        pltpu.get_barrier_semaphore(),
        inc=1,
        device_id=(space, depth),
        device_id_type=pl.DeviceIdType.MESH,
    )


def where_am_i(group):
    spaces, depths = lax.axis_size("space"), lax.axis_size("depth")
    space, depth = lax.axis_index("space"), lax.axis_index("depth")
    spot = lax.rem(space, group)
    first = space - spot
    before = lax.rem(first - 1 + spaces, spaces)
    after = lax.rem(first + group, spaces)
    return spaces, depths, space, depth, spot, first, before, after


def collect_kernel(
    group,
    position_ref,
    species_ref,
    index_ref,
    count_ref,
    halo_ref,
    center_ref,
    packed_ref,
    position_in,
    species_in,
    index_in,
    count_in,
    load,
    own,
    depth_send,
    depth_recv,
    part_send,
    part_recv,
    column_send,
    column_recv,
    edge_send,
    edge_recv,
    relay_send,
    relay_recv,
):
    spaces, depths, space, depth, spot, first, before, after = where_am_i(group)
    loads = [
        pltpu.make_async_copy(source, target, load.at[at])
        for at, (source, target) in enumerate(
            (
                (position_ref, position_in),
                (species_ref, species_in),
                (count_ref, count_in),
                (index_ref, index_in),
            )
        )
    ]
    for copy in loads:
        copy.start()
    slots, atoms = index_ref.shape[0], packed_ref.shape[1]
    share = atoms // group
    up, down = lax.rem(depth + 1, depths), lax.rem(depth + depths - 1, depths)
    mates = [first + lax.rem(spot + off, group) for off in range(1, group)]
    side = lax.rem(space, 2)
    twin = space + 1 - 2 * side
    at_start, at_end = spot == 0, spot == group - 1
    at_edge = jnp.logical_or(at_start, at_end)
    edge_from = jnp.where(side == 0, after, before)

    greet(space, up)
    greet(space, down)
    for mate in mates:
        greet(mate, depth)
    greet(edge_from, depth)
    expected = 2 + (group - 1) + (group // 2) * at_edge.astype(jnp.int32)

    def piece(start, part):
        return halo_ref.at[:, pl.ds(pl.multiple_of(start + 16 * part, 16), 16), :]

    column = (spot + 1) * GAP
    for copy in loads:
        copy.wait()
    for part in range(3):
        packed_ref[part : part + 1, :] = position_in[part]
    packed_ref[3:4, :] = species_in[...].astype(jnp.float32)
    packed_ref[4:5, :] = count_in[...].astype(jnp.float32)
    packed_ref[5:8, :] = jnp.zeros((3, atoms), jnp.float32)
    for slot in range(slots):
        packed_ref[8 + slot : 9 + slot, :] = index_in[slot].astype(jnp.float32)
    for part in range(4):
        for row in range(atoms // LANES):
            own[part, row : row + 1, :] = packed_ref[
                part : part + 1, row * LANES : (row + 1) * LANES
            ]
    piece(column, 1)[...] = own[...]
    pl.semaphore_wait(pltpu.get_barrier_semaphore(), expected)

    jumps = list(range(2, group, 2))
    half = group // 2
    depth_copies = [
        send(own, piece(column, 0), depth_send.at[0], depth_recv.at[0], space, up),
        send(own, piece(column, 2), depth_send.at[1], depth_recv.at[1], space, down),
    ]
    for copy in depth_copies:
        copy.start()

    def edges(part):
        base = jnp.where(at_start, lax.rem(first - group + spaces, spaces), after)
        start = jnp.where(at_start, (group + 1) * GAP, 0)
        return [
            send(
                piece(column, part),
                piece(start, part),
                edge_send.at[3 * member + part],
                edge_recv.at[part],
                base + 2 * member + side,
                depth,
            )
            for member in range(half)
        ]

    direct = {}
    for part in (1, 0, 2):
        if part != 1:
            depth_copies[part // 2].wait_recv()
        block = piece(column, part)

        @pl.when(at_edge)
        def _(part=part):
            for copy in edges(part):
                copy.start()

        for at, off in enumerate(jumps + [0]):
            slot = 3 * at + part
            target = mates[off - 1] if off else twin
            copy = send(block, block, column_send.at[slot], column_recv.at[slot], target, depth)
            copy.start()
            direct[at, part] = copy
        if part == 1:
            mine = pl.ds(pl.multiple_of(spot * share, 128), share)
            part_copies = []
            for off in range(1, group):
                copy = send(
                    packed_ref.at[:, off * share : (off + 1) * share],
                    center_ref.at[:, mine],
                    part_send.at[off - 1],
                    part_recv.at[off - 1],
                    mates[off - 1],
                    depth,
                )
                copy.start()
                part_copies.append(copy)
            center_ref[:, mine] = packed_ref[:, 0:share]

    relays = []
    edge_start = jnp.where(side == 0, (group + 1) * GAP, 0)
    for part in (1, 0, 2):
        for at, off in enumerate(jumps + [0]):
            if off:
                direct[at, part].wait_recv()
                block = piece((lax.rem(spot + group - off, group) + 1) * GAP, part)
            else:
                block = piece(edge_start, part)
                send(
                    block, block, edge_send.at[part], edge_recv.at[part], edge_from, depth
                ).wait_recv()
            slot = 3 * at + part
            copy = send(block, block, relay_send.at[slot], relay_recv.at[slot], twin, depth)
            copy.start()
            relays.append(copy)

    for part in range(3):
        direct[len(jumps), part].wait_recv()
    for copy in part_copies + relays:
        copy.wait_recv()
    for copy in depth_copies + part_copies + list(direct.values()) + relays:
        copy.wait_send()

    @pl.when(at_edge)
    def _():
        for part in range(3):
            for copy in edges(part):
                copy.wait_send()


def collect_call(positions, species, index, count, group):
    slots, _, atoms = index.shape
    kinds = 8 + slots
    rows = (group + 2) * GAP
    f32 = jnp.float32
    vmem = pl.BlockSpec(memory_space=pltpu.VMEM)
    dma = pltpu.SemaphoreType.DMA
    half = group // 2
    return pl.pallas_call(
        functools.partial(collect_kernel, group),
        out_shape=(
            jax.ShapeDtypeStruct((4, rows, LANES), f32),
            jax.ShapeDtypeStruct((kinds, atoms), f32),
        ),
        in_specs=[pl.BlockSpec(memory_space=pltpu.HBM)] * 4,
        out_specs=(vmem,) * 2,
        scratch_shapes=[
            pltpu.VMEM((kinds, atoms), f32),
            pltpu.VMEM((3, 1, atoms), f32),
            pltpu.VMEM((1, atoms), jnp.int32),
            pltpu.VMEM((slots, 1, atoms), jnp.int32),
            pltpu.VMEM((1, atoms), jnp.int32),
            dma((4,)),
            pltpu.VMEM((4, atoms // LANES, LANES), f32),
            dma((2,)),
            dma((2,)),
            dma((group - 1,)),
            dma((group - 1,)),
            dma((3 * half,)),
            dma((3 * half,)),
            dma((3 * half,)),
            dma((3,)),
            dma((3 * half,)),
            dma((3 * half,)),
        ],
        compiler_params=pltpu.CompilerParams(
            collective_id=0, has_side_effects=True, vmem_limit_bytes=24 * 1024 * 1024
        ),
    )(positions, species, index, count)


def return_kernel(
    group,
    ghalo_ref,
    back_ref,
    virial_ref,
    force_ref,
    energy_ref,
    total_ref,
    columns,
    halves,
    sums,
    blocks,
    flat,
    summed,
    by_member,
    by_depth,
    by_group,
    twin_send,
    twin_recv,
    column_send,
    column_recv,
    edge_send,
    edge_recv,
    part_send,
    part_recv,
    block_send,
    block_recv,
    member_send,
    member_recv,
    layer_send,
    layer_recv,
    group_send,
    group_recv,
):
    spaces, depths, space, depth, spot, first, before, after = where_am_i(group)
    atoms = back_ref.shape[1]
    share = atoms // group
    groups = spaces // group
    up, down = lax.rem(depth + 1, depths), lax.rem(depth + depths - 1, depths)
    mates = [first + lax.rem(spot + off, group) for off in range(1, group)]
    layers = [lax.rem(depth + off, depths) for off in range(1, depths)]
    peers = [lax.rem(space + off * group, spaces) for off in range(1, groups)]
    at_start, at_end = spot == 0, spot == group - 1

    for mate in mates:
        greet(mate, depth)
    for layer in layers:
        greet(space, layer)
    for peer in peers:
        greet(peer, depth)
    side = lax.rem(space, 2)
    twin = space + 1 - 2 * side
    twin_spot = spot + 1 - 2 * side
    jumps = list(range(2, group, 2))
    at_edge = jnp.logical_or(at_start, at_end)
    edge_to = jnp.where(side == 0, after, before)

    @pl.when(at_edge)
    def _():
        base = jnp.where(at_start, lax.rem(first - group + spaces, spaces), after)
        for member in range(group // 2):
            greet(base + 2 * member + side, depth)

    pl.semaphore_wait(
        pltpu.get_barrier_semaphore(), (group - 1) + (depths - 1) + (groups - 1) + 1
    )

    started = []

    def go(*args):
        copy = send(*args)
        copy.start()
        started.append(copy)
        return copy

    by_member[spot] = virial_ref[...]
    mine = by_member.at[spot]
    member_copies = [
        go(mine, mine, member_send.at[off], member_recv.at[off], mate, depth)
        for off, mate in enumerate(mates)
    ]

    def column_starts(spot_at, side_at):
        starts = [(lax.rem(spot_at + off, group) + 1) * GAP for off in jumps + [0]]
        return starts + [jnp.where(side_at == 0, (group + 1) * GAP, 0)]

    def rows_at(start, part):
        return pl.ds(pl.multiple_of(start + 16 * part, 16), 16)

    layer_order = (0, 2, 1)
    own_kind, edge_kind = len(jumps), len(jumps) + 1
    kind_order = [edge_kind] + list(range(len(jumps) + 1))
    theirs = column_starts(twin_spot, 1 - side)
    kinds = column_starts(spot, side)
    halfway = {}
    for part in layer_order:
        for kind in kind_order:
            slot = 3 * kind + part
            halfway[kind, part] = go(
                ghalo_ref.at[:, rows_at(theirs[kind], part), :],
                halves.at[kind, :, 16 * part : 16 * part + 16, :],
                twin_send.at[slot],
                twin_recv.at[slot],
                twin,
                depth,
            )
    part_copies = []
    for off, mate in enumerate(mates):
        theirs = pl.ds(pl.multiple_of((mate - first) * share, 128), share)
        part = (group - 1 - off) * share
        part_copies.append(
            go(
                back_ref.at[:, theirs],
                flat.at[:, part : part + share],
                part_send.at[off],
                part_recv.at[off],
                mate,
                depth,
            )
        )
    own_part = pl.ds(pl.multiple_of(spot * share, 128), share)
    flat[:, 0:share] = back_ref[:, own_part]

    crossing = {}
    for part in layer_order:
        rows = slice(16 * part, 16 * part + 16)
        for kind in kind_order[:-1]:
            halfway[kind, part].wait_recv()
            sums[kind, :, rows, :] = (
                ghalo_ref[:, rows_at(kinds[kind], part), :] + halves[kind, :, rows, :]
            )
            if kind == edge_kind:
                slot = len(jumps) + spot // 2
                go(
                    sums.at[kind, :, rows, :],
                    columns.at[slot, :, rows, :],
                    edge_send.at[part],
                    edge_recv.at[3 * (spot // 2) + part],
                    edge_to,
                    depth,
                )
            else:
                crossing[kind, part] = go(
                    sums.at[kind, :, rows, :],
                    columns.at[kind, :, rows, :],
                    column_send.at[3 * kind + part],
                    column_recv.at[3 * kind + part],
                    mates[jumps[kind] - 1],
                    depth,
                )

    for copy in member_copies:
        copy.wait_recv()
    level = by_member[0]
    for member in range(1, group):
        level = level + by_member[member]
    by_depth[depth] = level
    mine_depth = by_depth.at[depth]
    layer_copies = [
        go(mine_depth, mine_depth, layer_send.at[off], layer_recv.at[off], space, layer)
        for off, layer in enumerate(layers)
    ]
    for copy in layer_copies:
        copy.wait_recv()
    level = by_depth[0]
    for layer in range(1, depths):
        level = level + by_depth[layer]
    place = space // group
    by_group[place] = level
    mine_group = by_group.at[place]
    group_copies = [
        go(mine_group, mine_group, group_send.at[off], group_recv.at[off], peer, depth)
        for off, peer in enumerate(peers)
    ]

    block_copies = []
    for part in layer_order:
        rows = slice(16 * part, 16 * part + 16)
        halfway[own_kind, part].wait_recv()
        total = ghalo_ref[:, rows_at(kinds[own_kind], part), :] + halves[own_kind, :, rows, :]
        for kind in range(len(jumps)):
            crossing[kind, part].wait_recv()
            total = total + columns[kind, :, rows, :]
        summed[:, rows, :] = total

        @pl.when(at_edge)
        def _(part=part, rows=rows):
            extra = jnp.zeros((3, 16, LANES), jnp.float32)
            for member in range(group // 2):
                block = columns.at[len(jumps) + member, :, rows, :]
                send(
                    block,
                    block,
                    edge_send.at[part],
                    edge_recv.at[3 * member + part],
                    edge_to,
                    depth,
                ).wait_recv()
                extra = extra + block[...]
            summed[:, rows, :] = summed[:, rows, :] + extra

        if part != 1:
            at, layer = part // 2, (down, up)[part // 2]
            block_copies.append(
                go(
                    summed.at[:, rows, :],
                    blocks.at[at],
                    block_send.at[at],
                    block_recv.at[at],
                    space,
                    layer,
                )
            )

    for copy in part_copies:
        copy.wait_recv()
    energy_ref[...] = flat[3:4, :]
    for copy in group_copies:
        copy.wait_recv()
    level = by_group[0]
    for member in range(1, groups):
        level = level + by_group[member]
    entries = jnp.sum(level, axis=1, keepdims=True)
    shape = (8, 128)
    row_id = lax.broadcasted_iota(jnp.int32, shape, 0)
    column_id = lax.broadcasted_iota(jnp.int32, shape, 1)
    table = jnp.zeros(shape, jnp.float32)
    for entry in range(9):
        here = jnp.logical_and(row_id == entry // 3, column_id == entry % 3)
        table = jnp.where(here, entries[entry : entry + 1, :], table)
    total_ref[...] = table[0:3, 0:3]
    for copy in block_copies:
        copy.wait_recv()
    blocks[0] = summed[:, 16:32, :] + blocks[0] + blocks[1]
    for part in range(3):
        for row in range(atoms // LANES):
            lanes = slice(row * LANES, (row + 1) * LANES)
            force_ref[part, :, lanes] = -(
                blocks[0, part, row : row + 1, :] + flat[part : part + 1, lanes]
            )
    for copy in started:
        copy.wait_send()


def return_call(ghalo, back, virial, group):
    atoms = back.shape[1]
    f32 = jnp.float32
    depths = lax.axis_size("depth")
    groups = lax.axis_size("space") // group
    vmem = pl.BlockSpec(memory_space=pltpu.VMEM)
    dma = pltpu.SemaphoreType.DMA
    half = group // 2
    counts = [
        3 * (half + 1),
        3 * (half + 1),
        3 * half,
        3 * half,
        3,
        3 * half,
        group - 1,
        group - 1,
        2,
        2,
        group - 1,
        group - 1,
        depths - 1,
        depths - 1,
        groups - 1,
        groups - 1,
    ]
    return pl.pallas_call(
        functools.partial(return_kernel, group),
        out_shape=(
            jax.ShapeDtypeStruct((3, 1, atoms), f32),
            jax.ShapeDtypeStruct((1, atoms), f32),
            jax.ShapeDtypeStruct((3, 3), f32),
        ),
        in_specs=[vmem] * 3,
        out_specs=(vmem,) * 3,
        scratch_shapes=[
            pltpu.VMEM((group - 1, 3, GAP, LANES), f32),
            pltpu.VMEM((half + 1, 3, GAP, LANES), f32),
            pltpu.VMEM((half + 1, 3, GAP, LANES), f32),
            pltpu.VMEM((2, 3, 16, LANES), f32),
            pltpu.VMEM((8, atoms), f32),
            pltpu.VMEM((3, GAP, LANES), f32),
            pltpu.VMEM((group, 16, 128), f32),
            pltpu.VMEM((depths, 16, 128), f32),
            pltpu.VMEM((groups, 16, 128), f32),
        ]
        + [dma((count,)) for count in counts],
        compiler_params=pltpu.CompilerParams(
            collective_id=1, has_side_effects=True, vmem_limit_bytes=24 * 1024 * 1024
        ),
    )(ghalo, back, virial)


def per_device(
    positions,
    species,
    neighbours,
    counts,
    species_table,
    w_two_in,
    w_two_out,
    w_env,
    w_lat_in,
    w_lat_out,
    readout,
):
    atom_count = positions.shape[-1]
    weights = pack_weights(species_table, w_two_in, w_two_out, w_env, w_lat_in, w_lat_out)
    halo, center = collect_call(
        pltpu.with_memory_space_constraint(positions.reshape(3, 1, atom_count), pltpu.HBM),
        pltpu.with_memory_space_constraint(species.reshape(1, atom_count), pltpu.HBM),
        pltpu.with_memory_space_constraint(neighbours.reshape(-1, 1, atom_count), pltpu.HBM),
        pltpu.with_memory_space_constraint(counts.reshape(1, atom_count), pltpu.HBM),
        GROUP,
    )
    space = lax.axis_index("space")
    place = jnp.stack([space // GROUP * GROUP, lax.axis_index("depth")]).astype(jnp.int32)
    ghalo, back, virial = edge_call(
        place, halo, center, weights, readout.reshape(1, -1), TILE, GROUP
    )
    forces, energies, virial_total = return_call(ghalo, back, virial, GROUP)
    return (
        forces.reshape(3, 1, 1, atom_count),
        energies.reshape(1, 1, atom_count),
        virial_total,
    )


def solution(mesh):
    placed = (
        P(None, "space", "depth", None),
        P("space", "depth", None),
        P(None, "space", "depth", None),
        P("space", "depth", None),
        P(),
        P(),
        P(),
        P(),
        P(),
        P(),
        P(),
    )
    return jax.shard_map(
        per_device,
        mesh=mesh,
        in_specs=placed,
        out_specs=(P(None, "space", "depth", None), P("space", "depth", None), P()),
        check_vma=False,
    )
```

```python
import functools

import jax
import jax.numpy as jnp
from jax import lax
from jax.experimental import pallas as pl
from jax.experimental.pallas import tpu as pltpu
from jax.sharding import PartitionSpec as P

CUTOFF_RADIUS = 5.0
SOFT_CORE = 0.25

GROUP = 4
TILE = 1024
UNITS = 8
UNIT = 256
SIDE_LENGTH = 32.0
SPREAD = 36.0
GAP = 48
SPAN = 144
LANES = 256


def pieces(value, count):
    parts = []
    rest = value
    for _ in range(count):
        part = rest.astype(jnp.bfloat16)
        parts.append(part)
        rest = rest - part.astype(jnp.float32)
    return parts


def matmul(left, right):
    return jnp.dot(left, right, preferred_element_type=jnp.float32)


def matmul_nt(left, right):
    return lax.dot_general(
        left, right, (((1,), (1,)), ((), ())), preferred_element_type=jnp.float32
    )


def edge_kernel(
    units,
    tile,
    members,
    place_ref,
    halo_ref,
    center_ref,
    emb_ref,
    w_two_in_ref,
    w_two_out_ref,
    w_env_ref,
    w_lat_in_ref,
    w_lat_out_ref,
    readout_ref,
    ghalo_ref,
    back_ref,
    virial_ref,
    emb_in,
    two_in_in,
    two_out_in,
    env_in,
    lat_in_in,
    lat_out_in,
    readout_in,
    fetch,
    table,
    first_w,
    two_out_t,
    two_out,
    lat_in_t,
    lat_back,
    energy_col,
    radial_w,
    readout_col,
    near,
    entry_s,
    low_hot,
    radial_s,
    slope_one,
    raw_s,
    latent_s,
    amp_s,
    mix_s,
    glat_s,
    rows_s,
    rows_back,
    envs,
    genvs,
    virial_s,
    unit_slot,
    unit_chunk,
):
    slots, atoms = 8, center_ref.shape[1]
    tiles = atoms // tile
    rows = halo_ref.shape[1]
    f32, bf16 = jnp.float32, jnp.bfloat16
    base_space = place_ref[0]
    base_depth = place_ref[1]

    fetches = [
        pltpu.make_async_copy(source, target, fetch.at[at])
        for at, (source, target) in enumerate(
            (
                (emb_ref, emb_in),
                (w_two_in_ref, two_in_in),
                (w_two_out_ref, two_out_in),
                (w_env_ref, env_in),
                (w_lat_in_ref, lat_in_in),
                (w_lat_out_ref, lat_out_in),
                (readout_ref, readout_in),
            )
        )
    ]
    for copy in fetches:
        copy.start()

    row_id = lax.broadcasted_iota(jnp.int32, (rows, LANES), 0)
    space_of = (row_id // GAP - 1 + base_space).astype(f32)
    depth_of = (lax.rem(row_id, GAP) // 16 - 1 + base_depth).astype(f32)
    half = SIDE_LENGTH / 2
    local = [
        halo_ref[0] - (SIDE_LENGTH * space_of + half),
        halo_ref[1] - half + SPREAD * (halo_ref[3] - 1.5),
        halo_ref[2] - (SIDE_LENGTH * depth_of + half),
    ]
    for axis in range(3):
        high, low = pieces(local[axis], 2)
        table[axis, :, 0:LANES] = high
        table[axis, :, LANES : 2 * LANES] = low

    ghalo_ref[...] = jnp.zeros_like(ghalo_ref)
    back_ref[...] = jnp.zeros_like(back_ref)
    virial_s[...] = jnp.zeros_like(virial_s)

    for copy in fetches:
        copy.wait()
    w_one = two_in_in[...]
    lat_in = lat_in_in[...].astype(f32)
    two_out_now = two_out_in[...].astype(f32)
    lat_out_now = lat_out_in[...].astype(f32)
    env_now = env_in[...].astype(f32)
    emb = emb_in[...]
    center_part = matmul(emb, w_one[0:64])
    nbr_part = matmul(emb, w_one[64:128])
    species_part = 0.5 * jnp.concatenate([center_part, nbr_part], 0)
    radial_half = 0.5 * w_one[128:136].astype(f32)
    split = [part.astype(f32) for part in pieces(species_part, 3)]
    first_w[...] = jnp.concatenate([radial_half] + split, 0).T.astype(bf16)
    radial_w[...] = jnp.concatenate([radial_half, jnp.zeros_like(radial_half)], 0).astype(bf16)
    amp_high, amp_low = pieces(matmul(env_now.astype(bf16), two_out_now.astype(bf16)), 2)
    latent_rows = jnp.concatenate(
        [two_out_now, amp_high.astype(f32), amp_low.astype(f32)], 0
    )
    readout_row = readout_in[...]
    wide_row = jnp.broadcast_to(readout_row, (8, readout_row.shape[1]))
    line_row = jnp.dot(
        wide_row, two_out_now, precision=lax.Precision.HIGHEST, preferred_element_type=f32
    )
    line_rows = [part.astype(f32)[0:1] for part in pieces(line_row, 3)]
    two_out_t[0:128] = latent_rows.astype(bf16)
    two_out_t[128:144] = jnp.concatenate(
        line_rows + [jnp.zeros((13, two_out_now.shape[1]), f32)], 0
    ).astype(bf16)
    two_out[...] = latent_rows.T.astype(bf16)
    lat_in_t[...] = (0.5 * lat_in).T.astype(bf16)
    last_row = lax.dot_general(
        jnp.broadcast_to(readout_row, (8, readout_row.shape[1])),
        lat_out_now,
        (((1,), (0,)), ((), ())),
        precision=lax.Precision.HIGHEST,
        preferred_element_type=f32,
    )
    lat_back[...] = (0.5 * lat_in * last_row[0:1]).astype(bf16)
    energy_col[...] = last_row.T
    readout_col[...] = jnp.broadcast_to(readout_row, (8, readout_row.shape[1])).T

    chunks = tile // UNIT
    span = units * UNIT
    cuts = [slice(unit * UNIT, (unit + 1) * UNIT) for unit in range(units)]
    sharpness = (7 / CUTOFF_RADIUS) ** 2

    def one_tile(step, carry):
        lanes = pl.ds(pl.multiple_of(step * tile, tile), tile)
        count_row = center_ref[4:5, lanes]

        total = 0
        for chunk in range(chunks):
            depth = jnp.max(count_row[:, chunk * UNIT : (chunk + 1) * UNIT]).astype(jnp.int32)
            for slot in range(slots):
                unit_slot[total + slot] = slot
                unit_chunk[total + slot] = chunk
            total = total + depth
        for unit in range(units - 1):
            unit_slot[total + unit] = slots
            unit_chunk[total + unit] = 0
        turns = (total + (units - 1)) // units

        member = step // (tiles // members)
        window = pl.ds(pl.multiple_of(member * GAP, 16), SPAN)
        origin_x = SIDE_LENGTH * (base_space + member).astype(f32) + half
        origin_z = SIDE_LENGTH * base_depth.astype(f32) + half
        for part in range(4):
            envs[part] = jnp.zeros(envs.shape[1:], f32)
            genvs[part] = jnp.zeros(genvs.shape[1:], f32)

        def places(turn):
            found = []
            for unit in range(units):
                slot = unit_slot[turn * units + unit]
                chunk = unit_chunk[turn * units + unit]
                inner = pl.ds(pl.multiple_of(chunk * UNIT, UNIT), UNIT)
                outer = pl.ds(pl.multiple_of(step * tile + chunk * UNIT, UNIT), UNIT)
                found.append((slot, inner, outer))
            return found

        def row(turn, kind):
            return jnp.concatenate(
                [rows_s[turn, kind, unit : unit + 1, :] for unit in range(units)], 1
            )

        def per_atom(found, ref, part):
            return jnp.concatenate([ref[part, :, inner] for _, inner, _ in found], 1)

        def put_row(ref, kind, value):
            for unit, cut in enumerate(cuts):
                ref[kind, unit : unit + 1, :] = value[:, cut]

        def add_row(ref, kind, value):
            for unit, cut in enumerate(cuts):
                ref[kind, unit : unit + 1, :] += value[:, cut]

        def add_atoms(found, ref, part, value):
            for (_, inner, _), cut in zip(found, cuts):
                ref[part, :, inner] += value[:, cut]

        def entry_row(turn):
            return jnp.concatenate(
                [entry_s[turn, unit : unit + 1, :] for unit in range(units)], 1
            )

        def first(turn, carry):
            found = places(turn)
            for unit, (slot, _, outer) in enumerate(found):
                one = slice(unit, unit + 1)
                entry = center_ref[pl.ds(jnp.minimum(slot, slots - 1) + 8, 1), outer]
                entry_s[turn, one, :] = entry.astype(jnp.int32)
                for kind in range(4):
                    near[3 + kind, one, :] = center_ref[kind : kind + 1, outer]
                near[7, one, :] = center_ref[4:5, outer] - slot.astype(f32)
            entry = entry_row(turn)
            low_part = lax.bitwise_and(entry, LANES - 1)
            high_part = lax.shift_right_logical(entry, 8)
            hot = (
                lax.broadcasted_iota(jnp.int32, (LANES, span), 0) == low_part
            ).astype(f32).astype(bf16)
            low_hot[turn] = hot
            both = jnp.concatenate([hot, hot], 0)
            left = jnp.concatenate([table[axis, window, :] for axis in range(3)], 0)
            mask = lax.broadcasted_iota(jnp.int32, (SPAN, span), 0) == high_part
            for unit, cut in enumerate(cuts):
                seen = matmul(left, both[:, cut])
                for axis in range(3):
                    near[axis, unit : unit + 1, :] = jnp.sum(
                        jnp.where(mask[:, cut], seen[axis * SPAN : (axis + 1) * SPAN], 0.0),
                        axis=0,
                        keepdims=True,
                    )

            block = lax.shift_right_logical(entry_s[turn], 12)
            block_space = lax.shift_right_logical(block * 11, 5)
            block_depth = block - 3 * block_space
            nbr_species = jnp.floor((near[1] + 2.0 * SPREAD) * (1.0 / SPREAD))
            rel = [
                near[0] + SIDE_LENGTH * (block_space - 1).astype(f32) - (near[3] - origin_x),
                near[1] - SPREAD * (nbr_species - 1.5) - (near[4] - half),
                near[2] + SIDE_LENGTH * (block_depth - 1).astype(f32) - (near[5] - origin_z),
            ]
            squared = rel[0] * rel[0] + rel[1] * rel[1] + rel[2] * rel[2] + SOFT_CORE
            inverse = lax.rsqrt(squared)
            distance = squared * inverse
            fraction = jnp.minimum(distance * (1.0 / CUTOFF_RADIUS), 1.0)
            shell = 1.0 - fraction * fraction
            for axis in range(3):
                rows_s[turn, axis] = rel[axis] * inverse
            rows_s[turn, 3] = shell * shell
            rows_s[turn, 4] = jnp.where(near[7] > 0.0, 1.0, 0.0)
            rows_s[turn, 5] = nbr_species
            rows_s[turn, 6] = distance
            rows_s[turn, 7] = inverse
            rows_s[turn, 8] = shell * fraction * (4.0 / CUTOFF_RADIUS)
            rows_s[turn, 9] = near[6]

            basis_id = lax.broadcasted_iota(jnp.int32, (8, span), 0).astype(f32)
            spread = row(turn, 6) - basis_id * (CUTOFF_RADIUS / 7)
            radial = jnp.exp(-sharpness * spread * spread)
            radial_s[turn] = radial * (-2.0 * sharpness * spread)
            species_hot = jnp.where(
                basis_id < 4.0,
                (basis_id == row(turn, 9)).astype(f32),
                (basis_id - 4.0 == row(turn, 5)).astype(f32),
            )
            features = jnp.concatenate([radial, species_hot, species_hot, species_hot], 0)
            pre = matmul(first_w[...], features.astype(bf16))
            bent = jnp.tanh(pre)
            mixed = pre * bent
            hidden = (pre + mixed).astype(bf16)
            slope_one[turn] = ((1.0 + bent) * (1.0 + (pre - mixed))).astype(bf16)
            latents = matmul(two_out_t[...], hidden)
            raw = latents[0:64]
            raw_s[turn] = raw
            latent_s[turn] = (raw * row(turn, 3)).astype(bf16)
            amp = latents[64:96] + latents[96:128]
            line = jnp.sum(latents[128:136], axis=0, keepdims=True)
            put_row(rows_back.at[turn], 0, line * row(turn, 3))
            amp_s[turn] = amp
            amp = amp * (row(turn, 3) * row(turn, 4))
            add_atoms(found, envs, 0, amp)
            for axis in range(3):
                add_atoms(found, envs, 1 + axis, amp * row(turn, axis))
            return carry

        lax.fori_loop(0, turns, first, 0)
        for part in range(4):
            envs[part] = envs[part] * (1.0 / slots)

        def second(turn, carry):
            found = places(turn)
            cutoff_row = row(turn, 3)
            weight = cutoff_row * row(turn, 4)
            amp = amp_s[turn] * weight
            ways = [row(turn, axis) for axis in range(3)]
            env = [per_atom(found, envs, part) for part in range(4)]
            mix = env[0] + env[1] * ways[0] + env[2] * ways[1] + env[3] * ways[2]
            scalars = (amp * mix).astype(bf16)
            joined = jnp.concatenate([latent_s[turn], scalars], 0)
            pre = matmul(lat_in_t[...], joined)
            bent = jnp.tanh(pre)
            mixed = pre * bent
            slope = ((1.0 + bent) * (1.0 + (pre - mixed))).astype(bf16)
            rest = jnp.sum((pre + mixed) * energy_col[:, 0:1], axis=0, keepdims=True)
            back_rows = rows_back.at[turn]
            add_row(back_rows, 0, rest)
            back = matmul(lat_back[...], slope) * weight
            glat_s[turn] = back[0:64]
            gscal = back[64:96]
            mix_s[turn] = gscal * mix
            gprod = gscal * amp
            add_atoms(found, genvs, 0, gprod)
            for axis in range(3):
                add_atoms(found, genvs, 1 + axis, gprod * ways[axis])
                put_row(
                    back_rows, 1 + axis, jnp.sum(gprod * env[1 + axis], axis=0, keepdims=True)
                )
            return carry

        lax.fori_loop(0, turns, second, 0)
        for part in range(4):
            genvs[part] = genvs[part] * (1.0 / slots)

        def third(turn, carry):
            found = places(turn)
            ways = [row(turn, axis) for axis in range(3)]
            live_row = row(turn, 4)
            cutoff_row = row(turn, 3)
            weight = cutoff_row * live_row
            amp_raw = amp_s[turn]
            amp = amp_raw * weight
            genv = [per_atom(found, genvs, part) for part in range(4)]
            gamp = (
                mix_s[turn] + genv[0] + genv[1] * ways[0] + genv[2] * ways[1] + genv[3] * ways[2]
            ) * live_row
            for axis in range(3):
                put_row(near, axis, jnp.sum(amp * genv[1 + axis], axis=0, keepdims=True))
            glat = glat_s[turn] + readout_col[:, 0:1] * weight
            put_row(
                near,
                3,
                jnp.sum(glat * raw_s[turn], axis=0, keepdims=True)
                + jnp.sum(gamp * amp_raw, axis=0, keepdims=True),
            )
            gamp_b = (gamp * cutoff_row).astype(bf16)
            glatents = jnp.concatenate([(glat * cutoff_row).astype(bf16), gamp_b, gamp_b], 0)
            ghidden = matmul(two_out[...], glatents)
            gpre = (ghidden * slope_one[turn].astype(f32)).astype(bf16)
            gradial = matmul(radial_w[...], gpre)[0:8]
            put_row(near, 4, jnp.sum(gradial * radial_s[turn], axis=0, keepdims=True))

            pair = rows_back[turn, 0]
            direction = [rows_s[turn, axis] for axis in range(3)]
            live, inverse = rows_s[turn, 4], rows_s[turn, 7]
            gdir = [near[axis] + rows_back[turn, 1 + axis] for axis in range(3)]
            gcut = near[3] + pair * live
            gdist = near[4] - gcut * rows_s[turn, 8]
            along = gdir[0] * direction[0] + gdir[1] * direction[1] + gdir[2] * direction[2]
            push = gdist - along * inverse
            grel = [
                (gdir[axis] * inverse + direction[axis] * push) * live for axis in range(3)
            ]
            energy = pair * rows_s[turn, 3] * live
            distance = rows_s[turn, 6]
            for axis in range(3):
                near[5 + axis] = grel[axis]
                rel = direction[axis] * distance
                for other in range(3):
                    virial_s[3 * axis + other] += rel * grel[other]
            for unit, (_, _, outer) in enumerate(found):
                for axis in range(3):
                    back_ref[axis : axis + 1, outer] -= grel[axis][unit : unit + 1]
                back_ref[3:4, outer] += energy[unit : unit + 1]

            high_part = lax.shift_right_logical(entry_row(turn), 8)
            mask = lax.broadcasted_iota(jnp.int32, (SPAN, span), 0) == high_part
            grads = [
                jnp.concatenate([near[5 + axis, unit : unit + 1, :] for unit in range(units)], 1)
                for axis in range(3)
            ]
            spread = jnp.concatenate(
                [jnp.where(mask, grad, 0.0).astype(bf16) for grad in grads], 0
            )
            added = matmul_nt(spread, low_hot[turn])
            for axis in range(3):
                ghalo_ref[axis, window, :] += added[axis * SPAN : (axis + 1) * SPAN]
            return carry

        lax.fori_loop(0, turns, third, 0)
        return carry

    lax.fori_loop(0, tiles, one_tile, 0)
    for entry in range(9):
        folded = jnp.sum(virial_s[entry], axis=0, keepdims=True)
        part = folded[:, 0:128]
        for chunk in range(1, UNIT // 128):
            part = part + folded[:, 128 * chunk : 128 * (chunk + 1)]
        virial_ref[entry : entry + 1, :] = -part
    virial_ref[9:16, :] = jnp.zeros((7, 128), f32)


def edge_call(place, halo, center, weights, tile, members):
    slots, atoms = 8, center.shape[1]
    rows = halo.shape[1]
    f32, bf16 = jnp.float32, jnp.bfloat16
    vmem = pl.BlockSpec(memory_space=pltpu.VMEM)
    shapes = (
        jax.ShapeDtypeStruct((3, rows, LANES), f32),
        jax.ShapeDtypeStruct((8, atoms), f32),
        jax.ShapeDtypeStruct((16, 128), f32),
    )
    turns = slots * tile // (UNITS * UNIT)
    span = UNITS * UNIT
    scratch = [pltpu.VMEM(part.shape, part.dtype) for part in weights]
    scratch += [
        pltpu.SemaphoreType.DMA((len(weights),)),
        pltpu.VMEM((3, rows, 2 * LANES), bf16),
        pltpu.VMEM((256, 32), bf16),
        pltpu.VMEM((144, 256), bf16),
        pltpu.VMEM((256, 128), bf16),
        pltpu.VMEM((256, 96), bf16),
        pltpu.VMEM((96, 256), bf16),
        pltpu.VMEM((256, 8), f32),
        pltpu.VMEM((16, 256), bf16),
        pltpu.VMEM((64, 8), f32),
        pltpu.VMEM((8, UNITS, UNIT), f32),
        pltpu.VMEM((turns, UNITS, UNIT), jnp.int32),
        pltpu.VMEM((turns, LANES, span), bf16),
        pltpu.VMEM((turns, 8, span), f32),
        pltpu.VMEM((turns, 256, span), bf16),
        pltpu.VMEM((turns, 64, span), f32),
        pltpu.VMEM((turns, 64, span), bf16),
        pltpu.VMEM((turns, 32, span), f32),
        pltpu.VMEM((turns, 32, span), f32),
        pltpu.VMEM((turns, 64, span), f32),
        pltpu.VMEM((turns, 10, UNITS, UNIT), f32),
        pltpu.VMEM((turns, 4, UNITS, UNIT), f32),
        pltpu.VMEM((4, 32, tile), f32),
        pltpu.VMEM((4, 32, tile), f32),
        pltpu.VMEM((9, UNITS, UNIT), f32),
        pltpu.SMEM((slots * (tile // UNIT) + slots + UNITS,), jnp.int32),
        pltpu.SMEM((slots * (tile // UNIT) + slots + UNITS,), jnp.int32),
    ]
    return pl.pallas_call(
        functools.partial(edge_kernel, UNITS, tile, members),
        out_shape=shapes,
        in_specs=[pl.BlockSpec(memory_space=pltpu.SMEM)] + [vmem] * 2
        + [pl.BlockSpec(memory_space=pltpu.HBM)] * len(weights),
        out_specs=(vmem,) * 3,
        scratch_shapes=scratch,
        compiler_params=pltpu.CompilerParams(vmem_limit_bytes=48 * 1024 * 1024),
    )(place, halo, center, *weights)


def send(source, target, send_sem, recv_sem, space, depth):
    return pltpu.make_async_remote_copy(
        src_ref=source,
        dst_ref=target,
        send_sem=send_sem,
        recv_sem=recv_sem,
        device_id=(space, depth),
        device_id_type=pl.DeviceIdType.MESH,
    )


def greet(space, depth):
    pl.semaphore_signal(
        pltpu.get_barrier_semaphore(),
        inc=1,
        device_id=(space, depth),
        device_id_type=pl.DeviceIdType.MESH,
    )


def where_am_i(group):
    spaces, depths = lax.axis_size("space"), lax.axis_size("depth")
    space, depth = lax.axis_index("space"), lax.axis_index("depth")
    spot = lax.rem(space, group)
    first = space - spot
    before = lax.rem(first - 1 + spaces, spaces)
    after = lax.rem(first + group, spaces)
    return spaces, depths, space, depth, spot, first, before, after


def collect_kernel(
    group,
    position_ref,
    species_ref,
    index_ref,
    count_ref,
    halo_ref,
    center_ref,
    packed_ref,
    position_in,
    species_in,
    index_in,
    count_in,
    load,
    own,
    depth_send,
    depth_recv,
    part_send,
    part_recv,
    column_send,
    column_recv,
    edge_send,
    edge_recv,
    relay_send,
    relay_recv,
):
    spaces, depths, space, depth, spot, first, before, after = where_am_i(group)
    loads = [
        pltpu.make_async_copy(source, target, load.at[at])
        for at, (source, target) in enumerate(
            (
                (position_ref, position_in),
                (species_ref, species_in),
                (count_ref, count_in),
                (index_ref, index_in),
            )
        )
    ]
    for copy in loads:
        copy.start()
    slots, atoms = index_ref.shape[0], packed_ref.shape[1]
    share = atoms // group
    up, down = lax.rem(depth + 1, depths), lax.rem(depth + depths - 1, depths)
    mates = [first + lax.rem(spot + off, group) for off in range(1, group)]
    side = lax.rem(space, 2)
    twin = space + 1 - 2 * side
    at_start, at_end = spot == 0, spot == group - 1
    at_edge = jnp.logical_or(at_start, at_end)
    edge_from = jnp.where(side == 0, after, before)

    greet(space, up)
    greet(space, down)
    for mate in mates:
        greet(mate, depth)
    greet(edge_from, depth)
    expected = 2 + (group - 1) + (group // 2) * at_edge.astype(jnp.int32)

    def piece(start, part):
        return halo_ref.at[:, pl.ds(pl.multiple_of(start + 16 * part, 16), 16), :]

    column = (spot + 1) * GAP
    for copy in loads:
        copy.wait()
    for part in range(3):
        packed_ref[part : part + 1, :] = position_in[part]
    packed_ref[3:4, :] = species_in[...].astype(jnp.float32)
    packed_ref[4:5, :] = count_in[...].astype(jnp.float32)
    packed_ref[5:8, :] = jnp.zeros((3, atoms), jnp.float32)
    for slot in range(slots):
        packed_ref[8 + slot : 9 + slot, :] = index_in[slot].astype(jnp.float32)
    for part in range(4):
        for row in range(atoms // LANES):
            own[part, row : row + 1, :] = packed_ref[
                part : part + 1, row * LANES : (row + 1) * LANES
            ]
    piece(column, 1)[...] = own[...]
    pl.semaphore_wait(pltpu.get_barrier_semaphore(), expected)

    jumps = list(range(2, group, 2))
    half = group // 2
    depth_copies = [
        send(own, piece(column, 0), depth_send.at[0], depth_recv.at[0], space, up),
        send(own, piece(column, 2), depth_send.at[1], depth_recv.at[1], space, down),
    ]
    for copy in depth_copies:
        copy.start()

    def edges(part):
        base = jnp.where(at_start, lax.rem(first - group + spaces, spaces), after)
        start = jnp.where(at_start, (group + 1) * GAP, 0)
        return [
            send(
                piece(column, part),
                piece(start, part),
                edge_send.at[3 * member + part],
                edge_recv.at[part],
                base + 2 * member + side,
                depth,
            )
            for member in range(half)
        ]

    direct = {}
    for part in (1, 0, 2):
        if part != 1:
            depth_copies[part // 2].wait_recv()
        block = piece(column, part)

        @pl.when(at_edge)
        def _(part=part):
            for copy in edges(part):
                copy.start()

        for at, off in enumerate(jumps + [0]):
            slot = 3 * at + part
            target = mates[off - 1] if off else twin
            copy = send(block, block, column_send.at[slot], column_recv.at[slot], target, depth)
            copy.start()
            direct[at, part] = copy
        if part == 1:
            mine = pl.ds(pl.multiple_of(spot * share, 128), share)
            part_copies = []
            for off in range(1, group):
                copy = send(
                    packed_ref.at[:, off * share : (off + 1) * share],
                    center_ref.at[:, mine],
                    part_send.at[off - 1],
                    part_recv.at[off - 1],
                    mates[off - 1],
                    depth,
                )
                copy.start()
                part_copies.append(copy)
            center_ref[:, mine] = packed_ref[:, 0:share]

    relays = []
    edge_start = jnp.where(side == 0, (group + 1) * GAP, 0)
    for part in (1, 0, 2):
        for at, off in enumerate(jumps + [0]):
            if off:
                direct[at, part].wait_recv()
                block = piece((lax.rem(spot + group - off, group) + 1) * GAP, part)
            else:
                block = piece(edge_start, part)
                send(
                    block, block, edge_send.at[part], edge_recv.at[part], edge_from, depth
                ).wait_recv()
            slot = 3 * at + part
            copy = send(block, block, relay_send.at[slot], relay_recv.at[slot], twin, depth)
            copy.start()
            relays.append(copy)

    for part in range(3):
        direct[len(jumps), part].wait_recv()
    for copy in part_copies + relays:
        copy.wait_recv()
    for copy in depth_copies + part_copies + list(direct.values()) + relays:
        copy.wait_send()

    @pl.when(at_edge)
    def _():
        for part in range(3):
            for copy in edges(part):
                copy.wait_send()


def collect_call(positions, species, index, count, group):
    slots, _, atoms = index.shape
    kinds = 8 + slots
    rows = (group + 2) * GAP
    f32 = jnp.float32
    vmem = pl.BlockSpec(memory_space=pltpu.VMEM)
    dma = pltpu.SemaphoreType.DMA
    half = group // 2
    return pl.pallas_call(
        functools.partial(collect_kernel, group),
        out_shape=(
            jax.ShapeDtypeStruct((4, rows, LANES), f32),
            jax.ShapeDtypeStruct((kinds, atoms), f32),
        ),
        in_specs=[pl.BlockSpec(memory_space=pltpu.HBM)] * 4,
        out_specs=(vmem,) * 2,
        scratch_shapes=[
            pltpu.VMEM((kinds, atoms), f32),
            pltpu.VMEM((3, 1, atoms), f32),
            pltpu.VMEM((1, atoms), jnp.int32),
            pltpu.VMEM((slots, 1, atoms), jnp.int32),
            pltpu.VMEM((1, atoms), jnp.int32),
            dma((4,)),
            pltpu.VMEM((4, atoms // LANES, LANES), f32),
            dma((2,)),
            dma((2,)),
            dma((group - 1,)),
            dma((group - 1,)),
            dma((3 * half,)),
            dma((3 * half,)),
            dma((3 * half,)),
            dma((3,)),
            dma((3 * half,)),
            dma((3 * half,)),
        ],
        compiler_params=pltpu.CompilerParams(
            collective_id=0, has_side_effects=True, vmem_limit_bytes=24 * 1024 * 1024
        ),
    )(positions, species, index, count)


def return_kernel(
    group,
    ghalo_ref,
    back_ref,
    virial_ref,
    force_ref,
    energy_ref,
    total_ref,
    columns,
    halves,
    sums,
    blocks,
    flat,
    summed,
    by_member,
    by_depth,
    by_group,
    twin_send,
    twin_recv,
    column_send,
    column_recv,
    edge_send,
    edge_recv,
    part_send,
    part_recv,
    block_send,
    block_recv,
    member_send,
    member_recv,
    layer_send,
    layer_recv,
    group_send,
    group_recv,
):
    spaces, depths, space, depth, spot, first, before, after = where_am_i(group)
    atoms = back_ref.shape[1]
    share = atoms // group
    groups = spaces // group
    up, down = lax.rem(depth + 1, depths), lax.rem(depth + depths - 1, depths)
    mates = [first + lax.rem(spot + off, group) for off in range(1, group)]
    layers = [lax.rem(depth + off, depths) for off in range(1, depths)]
    peers = [lax.rem(space + off * group, spaces) for off in range(1, groups)]
    at_start, at_end = spot == 0, spot == group - 1

    for mate in mates:
        greet(mate, depth)
    for layer in layers:
        greet(space, layer)
    for peer in peers:
        greet(peer, depth)
    side = lax.rem(space, 2)
    twin = space + 1 - 2 * side
    twin_spot = spot + 1 - 2 * side
    jumps = list(range(2, group, 2))
    at_edge = jnp.logical_or(at_start, at_end)
    edge_to = jnp.where(side == 0, after, before)

    @pl.when(at_edge)
    def _():
        base = jnp.where(at_start, lax.rem(first - group + spaces, spaces), after)
        for member in range(group // 2):
            greet(base + 2 * member + side, depth)

    pl.semaphore_wait(
        pltpu.get_barrier_semaphore(), (group - 1) + (depths - 1) + (groups - 1) + 1
    )

    started = []

    def go(*args):
        copy = send(*args)
        copy.start()
        started.append(copy)
        return copy

    by_member[spot] = virial_ref[...]
    mine = by_member.at[spot]
    member_copies = [
        go(mine, mine, member_send.at[off], member_recv.at[off], mate, depth)
        for off, mate in enumerate(mates)
    ]

    def column_starts(spot_at, side_at):
        starts = [(lax.rem(spot_at + off, group) + 1) * GAP for off in jumps + [0]]
        return starts + [jnp.where(side_at == 0, (group + 1) * GAP, 0)]

    def rows_at(start, part):
        return pl.ds(pl.multiple_of(start + 16 * part, 16), 16)

    layer_order = (0, 2, 1)
    own_kind, edge_kind = len(jumps), len(jumps) + 1
    kind_order = [edge_kind] + list(range(len(jumps) + 1))
    theirs = column_starts(twin_spot, 1 - side)
    kinds = column_starts(spot, side)
    halfway = {}
    for part in layer_order:
        for kind in kind_order:
            slot = 3 * kind + part
            halfway[kind, part] = go(
                ghalo_ref.at[:, rows_at(theirs[kind], part), :],
                halves.at[kind, :, 16 * part : 16 * part + 16, :],
                twin_send.at[slot],
                twin_recv.at[slot],
                twin,
                depth,
            )
    part_copies = []
    for off, mate in enumerate(mates):
        theirs = pl.ds(pl.multiple_of((mate - first) * share, 128), share)
        part = (group - 1 - off) * share
        part_copies.append(
            go(
                back_ref.at[:, theirs],
                flat.at[:, part : part + share],
                part_send.at[off],
                part_recv.at[off],
                mate,
                depth,
            )
        )
    own_part = pl.ds(pl.multiple_of(spot * share, 128), share)
    flat[:, 0:share] = back_ref[:, own_part]

    crossing = {}
    for part in layer_order:
        rows = slice(16 * part, 16 * part + 16)
        for kind in kind_order[:-1]:
            halfway[kind, part].wait_recv()
            sums[kind, :, rows, :] = (
                ghalo_ref[:, rows_at(kinds[kind], part), :] + halves[kind, :, rows, :]
            )
            if kind == edge_kind:
                slot = len(jumps) + spot // 2
                go(
                    sums.at[kind, :, rows, :],
                    columns.at[slot, :, rows, :],
                    edge_send.at[part],
                    edge_recv.at[3 * (spot // 2) + part],
                    edge_to,
                    depth,
                )
            else:
                crossing[kind, part] = go(
                    sums.at[kind, :, rows, :],
                    columns.at[kind, :, rows, :],
                    column_send.at[3 * kind + part],
                    column_recv.at[3 * kind + part],
                    mates[jumps[kind] - 1],
                    depth,
                )

    for copy in member_copies:
        copy.wait_recv()
    level = by_member[0]
    for member in range(1, group):
        level = level + by_member[member]
    by_depth[depth] = level
    mine_depth = by_depth.at[depth]
    layer_copies = [
        go(mine_depth, mine_depth, layer_send.at[off], layer_recv.at[off], space, layer)
        for off, layer in enumerate(layers)
    ]
    for copy in layer_copies:
        copy.wait_recv()
    level = by_depth[0]
    for layer in range(1, depths):
        level = level + by_depth[layer]
    place = space // group
    by_group[place] = level
    mine_group = by_group.at[place]
    group_copies = [
        go(mine_group, mine_group, group_send.at[off], group_recv.at[off], peer, depth)
        for off, peer in enumerate(peers)
    ]

    block_copies = []
    for part in layer_order:
        rows = slice(16 * part, 16 * part + 16)
        halfway[own_kind, part].wait_recv()
        total = ghalo_ref[:, rows_at(kinds[own_kind], part), :] + halves[own_kind, :, rows, :]
        for kind in range(len(jumps)):
            crossing[kind, part].wait_recv()
            total = total + columns[kind, :, rows, :]
        summed[:, rows, :] = total

        @pl.when(at_edge)
        def _(part=part, rows=rows):
            extra = jnp.zeros((3, 16, LANES), jnp.float32)
            for member in range(group // 2):
                block = columns.at[len(jumps) + member, :, rows, :]
                send(
                    block,
                    block,
                    edge_send.at[part],
                    edge_recv.at[3 * member + part],
                    edge_to,
                    depth,
                ).wait_recv()
                extra = extra + block[...]
            summed[:, rows, :] = summed[:, rows, :] + extra

        if part != 1:
            at, layer = part // 2, (down, up)[part // 2]
            block_copies.append(
                go(
                    summed.at[:, rows, :],
                    blocks.at[at],
                    block_send.at[at],
                    block_recv.at[at],
                    space,
                    layer,
                )
            )

    for copy in part_copies:
        copy.wait_recv()
    energy_ref[...] = flat[3:4, :]
    for copy in group_copies:
        copy.wait_recv()
    level = by_group[0]
    for member in range(1, groups):
        level = level + by_group[member]
    entries = jnp.sum(level, axis=1, keepdims=True)
    shape = (8, 128)
    row_id = lax.broadcasted_iota(jnp.int32, shape, 0)
    column_id = lax.broadcasted_iota(jnp.int32, shape, 1)
    table = jnp.zeros(shape, jnp.float32)
    for entry in range(9):
        here = jnp.logical_and(row_id == entry // 3, column_id == entry % 3)
        table = jnp.where(here, entries[entry : entry + 1, :], table)
    total_ref[...] = table[0:3, 0:3]
    for copy in block_copies:
        copy.wait_recv()
    blocks[0] = summed[:, 16:32, :] + blocks[0] + blocks[1]
    for part in range(3):
        for row in range(atoms // LANES):
            lanes = slice(row * LANES, (row + 1) * LANES)
            force_ref[part, :, lanes] = -(
                blocks[0, part, row : row + 1, :] + flat[part : part + 1, lanes]
            )
    for copy in started:
        copy.wait_send()


def return_call(ghalo, back, virial, group):
    atoms = back.shape[1]
    f32 = jnp.float32
    depths = lax.axis_size("depth")
    groups = lax.axis_size("space") // group
    vmem = pl.BlockSpec(memory_space=pltpu.VMEM)
    dma = pltpu.SemaphoreType.DMA
    half = group // 2
    counts = [
        3 * (half + 1),
        3 * (half + 1),
        3 * half,
        3 * half,
        3,
        3 * half,
        group - 1,
        group - 1,
        2,
        2,
        group - 1,
        group - 1,
        depths - 1,
        depths - 1,
        groups - 1,
        groups - 1,
    ]
    return pl.pallas_call(
        functools.partial(return_kernel, group),
        out_shape=(
            jax.ShapeDtypeStruct((3, 1, atoms), f32),
            jax.ShapeDtypeStruct((1, atoms), f32),
            jax.ShapeDtypeStruct((3, 3), f32),
        ),
        in_specs=[vmem] * 3,
        out_specs=(vmem,) * 3,
        scratch_shapes=[
            pltpu.VMEM((group - 1, 3, GAP, LANES), f32),
            pltpu.VMEM((half + 1, 3, GAP, LANES), f32),
            pltpu.VMEM((half + 1, 3, GAP, LANES), f32),
            pltpu.VMEM((2, 3, 16, LANES), f32),
            pltpu.VMEM((8, atoms), f32),
            pltpu.VMEM((3, GAP, LANES), f32),
            pltpu.VMEM((group, 16, 128), f32),
            pltpu.VMEM((depths, 16, 128), f32),
            pltpu.VMEM((groups, 16, 128), f32),
        ]
        + [dma((count,)) for count in counts],
        compiler_params=pltpu.CompilerParams(
            collective_id=1, has_side_effects=True, vmem_limit_bytes=24 * 1024 * 1024
        ),
    )(ghalo, back, virial)


def store_kernel(*refs):
    sources, targets, done = refs[0:3], refs[3:6], refs[6]
    copies = [
        pltpu.make_async_copy(source, target, done.at[at])
        for at, (source, target) in enumerate(zip(sources, targets))
    ]
    for copy in copies:
        copy.start()
    for copy in copies:
        copy.wait()


def store_call(parts):
    return pl.pallas_call(
        store_kernel,
        out_shape=tuple(jax.ShapeDtypeStruct(part.shape, part.dtype) for part in parts),
        in_specs=[pl.BlockSpec(memory_space=pltpu.VMEM)] * 3,
        out_specs=(pl.BlockSpec(memory_space=pltpu.HBM),) * 3,
        scratch_shapes=[pltpu.SemaphoreType.DMA((3,))],
    )(*parts)


def per_device(
    positions,
    species,
    neighbours,
    counts,
    species_table,
    w_two_in,
    w_two_out,
    w_env,
    w_lat_in,
    w_lat_out,
    readout,
):
    atom_count = positions.shape[-1]
    weights = [
        pltpu.with_memory_space_constraint(part, pltpu.HBM)
        for part in (
            species_table,
            w_two_in,
            w_two_out.T,
            w_env.T,
            w_lat_in,
            w_lat_out.T,
            readout.reshape(1, -1),
        )
    ]
    halo, center = collect_call(
        pltpu.with_memory_space_constraint(positions.reshape(3, 1, atom_count), pltpu.HBM),
        pltpu.with_memory_space_constraint(species.reshape(1, atom_count), pltpu.HBM),
        pltpu.with_memory_space_constraint(neighbours.reshape(-1, 1, atom_count), pltpu.HBM),
        pltpu.with_memory_space_constraint(counts.reshape(1, atom_count), pltpu.HBM),
        GROUP,
    )
    space = lax.axis_index("space")
    place = jnp.stack([space // GROUP * GROUP, lax.axis_index("depth")]).astype(jnp.int32)
    ghalo, back, virial = edge_call(
        place, halo, center, weights, TILE, GROUP
    )
    results = return_call(ghalo, back, virial, GROUP)
    forces, energies, virial_total = store_call(results)
    return (
        forces.reshape(3, 1, 1, atom_count),
        energies.reshape(1, 1, atom_count),
        virial_total,
    )


def solution(mesh):
    placed = (
        P(None, "space", "depth", None),
        P("space", "depth", None),
        P(None, "space", "depth", None),
        P("space", "depth", None),
        P(),
        P(),
        P(),
        P(),
        P(),
        P(),
        P(),
    )
    return jax.shard_map(
        per_device,
        mesh=mesh,
        in_specs=placed,
        out_specs=(P(None, "space", "depth", None), P("space", "depth", None), P()),
        check_vma=False,
    )
```

```python
import functools

import jax
import jax.numpy as jnp
from jax import lax
from jax.experimental import pallas as pl
from jax.experimental.pallas import tpu as pltpu
from jax.sharding import PartitionSpec as P

CUTOFF_RADIUS = 5.0
SOFT_CORE = 0.25

GROUP = 4
TILE = 1024
UNITS = 8
UNIT = 256
SIDE_LENGTH = 32.0
SPREAD = 36.0
GAP = 48
SPAN = 144
LANES = 256


def pieces(value, count):
    parts = []
    rest = value
    for _ in range(count):
        part = rest.astype(jnp.bfloat16)
        parts.append(part)
        rest = rest - part.astype(jnp.float32)
    return parts


def matmul(left, right):
    return jnp.dot(left, right, preferred_element_type=jnp.float32)


def matmul_nt(left, right):
    return lax.dot_general(
        left, right, (((1,), (1,)), ((), ())), preferred_element_type=jnp.float32
    )


def edge_kernel(
    units,
    tile,
    members,
    place_ref,
    halo_ref,
    center_ref,
    emb_ref,
    w_two_in_ref,
    w_two_out_ref,
    w_env_ref,
    w_lat_in_ref,
    w_lat_out_ref,
    readout_ref,
    ghalo_ref,
    back_ref,
    virial_ref,
    emb_in,
    two_in_in,
    two_out_in,
    env_in,
    lat_in_in,
    lat_out_in,
    readout_in,
    fetch,
    table,
    first_w,
    two_out_t,
    two_out,
    lat_in_t,
    lat_back,
    energy_col,
    radial_w,
    readout_col,
    near,
    entry_s,
    low_hot,
    radial_s,
    slope_one,
    raw_s,
    latent_s,
    amp_s,
    mix_s,
    glat_s,
    rows_s,
    rows_back,
    envs,
    genvs,
    virial_s,
    unit_slot,
    unit_chunk,
):
    slots, atoms = 8, center_ref.shape[1]
    tiles = atoms // tile
    rows = halo_ref.shape[1]
    f32, bf16 = jnp.float32, jnp.bfloat16
    base_space = place_ref[0]
    base_depth = place_ref[1]

    fetches = [
        pltpu.make_async_copy(source, target, fetch.at[at])
        for at, (source, target) in enumerate(
            (
                (emb_ref, emb_in),
                (w_two_in_ref, two_in_in),
                (w_two_out_ref, two_out_in),
                (w_env_ref, env_in),
                (w_lat_in_ref, lat_in_in),
                (w_lat_out_ref, lat_out_in),
                (readout_ref, readout_in),
            )
        )
    ]
    for copy in fetches:
        copy.start()

    row_id = lax.broadcasted_iota(jnp.int32, (rows, LANES), 0)
    space_of = (row_id // GAP - 1 + base_space).astype(f32)
    depth_of = (lax.rem(row_id, GAP) // 16 - 1 + base_depth).astype(f32)
    half = SIDE_LENGTH / 2
    local = [
        halo_ref[0] - (SIDE_LENGTH * space_of + half),
        halo_ref[1] - half + SPREAD * (halo_ref[3] - 1.5),
        halo_ref[2] - (SIDE_LENGTH * depth_of + half),
    ]
    for axis in range(3):
        high, low = pieces(local[axis], 2)
        table[axis, :, 0:LANES] = high
        table[axis, :, LANES : 2 * LANES] = low

    ghalo_ref[...] = jnp.zeros_like(ghalo_ref)
    back_ref[...] = jnp.zeros_like(back_ref)
    virial_s[...] = jnp.zeros_like(virial_s)

    for copy in fetches:
        copy.wait()
    w_one = two_in_in[...]
    lat_in = lat_in_in[...].astype(f32)
    two_out_now = two_out_in[...].astype(f32)
    lat_out_now = lat_out_in[...].astype(f32)
    env_now = env_in[...].astype(f32)
    emb = emb_in[...]
    center_part = matmul(emb, w_one[0:64])
    nbr_part = matmul(emb, w_one[64:128])
    species_part = 0.5 * jnp.concatenate([center_part, nbr_part], 0)
    radial_half = 0.5 * w_one[128:136].astype(f32)
    split = [part.astype(f32) for part in pieces(species_part, 3)]
    first_w[...] = jnp.concatenate([radial_half] + split, 0).T.astype(bf16)
    radial_w[...] = jnp.concatenate([radial_half, jnp.zeros_like(radial_half)], 0).astype(bf16)
    amp_high, amp_low = pieces(matmul(env_now.astype(bf16), two_out_now.astype(bf16)), 2)
    latent_rows = jnp.concatenate(
        [two_out_now, amp_high.astype(f32), amp_low.astype(f32)], 0
    )
    readout_row = readout_in[...]
    wide_row = jnp.broadcast_to(readout_row, (8, readout_row.shape[1]))
    line_row = jnp.dot(
        wide_row, two_out_now, precision=lax.Precision.HIGHEST, preferred_element_type=f32
    )
    line_rows = [part.astype(f32)[0:1] for part in pieces(line_row, 3)]
    two_out_t[0:128] = latent_rows.astype(bf16)
    two_out_t[128:144] = jnp.concatenate(
        line_rows + [jnp.zeros((13, two_out_now.shape[1]), f32)], 0
    ).astype(bf16)
    two_out[...] = latent_rows.T.astype(bf16)
    lat_in_t[...] = (0.5 * lat_in).T.astype(bf16)
    last_row = lax.dot_general(
        jnp.broadcast_to(readout_row, (8, readout_row.shape[1])),
        lat_out_now,
        (((1,), (0,)), ((), ())),
        precision=lax.Precision.HIGHEST,
        preferred_element_type=f32,
    )
    lat_back[...] = (0.5 * lat_in * last_row[0:1]).astype(bf16)
    energy_col[...] = last_row.T
    readout_col[...] = jnp.broadcast_to(readout_row, (8, readout_row.shape[1])).T

    chunks = tile // UNIT
    span = units * UNIT
    cuts = [slice(unit * UNIT, (unit + 1) * UNIT) for unit in range(units)]
    sharpness = (7 / CUTOFF_RADIUS) ** 2

    def one_tile(step, carry):
        lanes = pl.ds(pl.multiple_of(step * tile, tile), tile)
        count_row = center_ref[4:5, lanes]

        total = 0
        for chunk in range(chunks):
            depth = jnp.max(count_row[:, chunk * UNIT : (chunk + 1) * UNIT]).astype(jnp.int32)
            for slot in range(slots):
                unit_slot[total + slot] = slot
                unit_chunk[total + slot] = chunk
            total = total + depth
        for unit in range(units - 1):
            unit_slot[total + unit] = slots
            unit_chunk[total + unit] = 0
        turns = (total + (units - 1)) // units

        member = step // (tiles // members)
        window = pl.ds(pl.multiple_of(member * GAP, 16), SPAN)
        origin_x = SIDE_LENGTH * (base_space + member).astype(f32) + half
        origin_z = SIDE_LENGTH * base_depth.astype(f32) + half
        for part in range(4):
            envs[part] = jnp.zeros(envs.shape[1:], f32)
            genvs[part] = jnp.zeros(genvs.shape[1:], f32)

        def places(turn):
            found = []
            for unit in range(units):
                slot = unit_slot[turn * units + unit]
                chunk = unit_chunk[turn * units + unit]
                inner = pl.ds(pl.multiple_of(chunk * UNIT, UNIT), UNIT)
                outer = pl.ds(pl.multiple_of(step * tile + chunk * UNIT, UNIT), UNIT)
                found.append((slot, inner, outer))
            return found

        def row(turn, kind):
            return jnp.concatenate(
                [rows_s[turn, kind, unit : unit + 1, :] for unit in range(units)], 1
            )

        def per_atom(found, ref, part):
            return jnp.concatenate([ref[part, :, inner] for _, inner, _ in found], 1)

        def put_row(ref, kind, value):
            for unit, cut in enumerate(cuts):
                ref[kind, unit : unit + 1, :] = value[:, cut]

        def add_row(ref, kind, value):
            for unit, cut in enumerate(cuts):
                ref[kind, unit : unit + 1, :] += value[:, cut]

        def add_atoms(found, ref, part, value):
            for (_, inner, _), cut in zip(found, cuts):
                ref[part, :, inner] += value[:, cut]

        def entry_row(turn):
            return jnp.concatenate(
                [entry_s[turn, unit : unit + 1, :] for unit in range(units)], 1
            )

        def first(turn, carry):
            found = places(turn)
            for unit, (slot, _, outer) in enumerate(found):
                one = slice(unit, unit + 1)
                entry = center_ref[pl.ds(jnp.minimum(slot, slots - 1) + 8, 1), outer]
                entry_s[turn, one, :] = entry.astype(jnp.int32)
                for kind in range(4):
                    near[3 + kind, one, :] = center_ref[kind : kind + 1, outer]
                near[7, one, :] = center_ref[4:5, outer] - slot.astype(f32)
            entry = entry_row(turn)
            low_part = lax.bitwise_and(entry, LANES - 1)
            high_part = lax.shift_right_logical(entry, 8)
            low_id = lax.broadcasted_iota(jnp.int32, (LANES, span), 0).astype(f32).astype(bf16)
            low_row = low_part.astype(f32).astype(bf16)
            hot = jnp.where(low_id == low_row, jnp.ones((), bf16), jnp.zeros((), bf16))
            low_hot[turn] = hot
            both = jnp.concatenate([hot, hot], 0)
            left = jnp.concatenate([table[axis, window, :] for axis in range(3)], 0)
            mask = lax.broadcasted_iota(jnp.int32, (SPAN, span), 0) == high_part
            for unit, cut in enumerate(cuts):
                seen = matmul(left, both[:, cut])
                for axis in range(3):
                    near[axis, unit : unit + 1, :] = jnp.sum(
                        jnp.where(mask[:, cut], seen[axis * SPAN : (axis + 1) * SPAN], 0.0),
                        axis=0,
                        keepdims=True,
                    )

            block = lax.shift_right_logical(entry_s[turn], 12)
            block_space = lax.shift_right_logical(block * 11, 5)
            block_depth = block - 3 * block_space
            nbr_species = jnp.floor((near[1] + 2.0 * SPREAD) * (1.0 / SPREAD))
            rel = [
                near[0] + SIDE_LENGTH * (block_space - 1).astype(f32) - (near[3] - origin_x),
                near[1] - SPREAD * (nbr_species - 1.5) - (near[4] - half),
                near[2] + SIDE_LENGTH * (block_depth - 1).astype(f32) - (near[5] - origin_z),
            ]
            squared = rel[0] * rel[0] + rel[1] * rel[1] + rel[2] * rel[2] + SOFT_CORE
            inverse = lax.rsqrt(squared)
            distance = squared * inverse
            fraction = jnp.minimum(distance * (1.0 / CUTOFF_RADIUS), 1.0)
            shell = 1.0 - fraction * fraction
            for axis in range(3):
                rows_s[turn, axis] = rel[axis] * inverse
            rows_s[turn, 3] = shell * shell
            rows_s[turn, 4] = jnp.where(near[7] > 0.0, 1.0, 0.0)
            rows_s[turn, 5] = nbr_species
            rows_s[turn, 6] = distance
            rows_s[turn, 7] = inverse
            rows_s[turn, 8] = shell * fraction * (4.0 / CUTOFF_RADIUS)
            rows_s[turn, 9] = near[6]

            basis_id = lax.broadcasted_iota(jnp.int32, (8, span), 0).astype(f32)
            spread = row(turn, 6) - basis_id * (CUTOFF_RADIUS / 7)
            radial = jnp.exp(-sharpness * spread * spread)
            radial_s[turn] = radial * (-2.0 * sharpness * spread)
            species_hot = jnp.where(
                basis_id < 4.0,
                (basis_id == row(turn, 9)).astype(f32),
                (basis_id - 4.0 == row(turn, 5)).astype(f32),
            )
            features = jnp.concatenate([radial, species_hot, species_hot, species_hot], 0)
            pre = matmul(first_w[...], features.astype(bf16))
            bent = jnp.tanh(pre)
            mixed = pre * bent
            hidden = (pre + mixed).astype(bf16)
            slope_one[turn] = ((1.0 + bent) * (1.0 + (pre - mixed))).astype(bf16)
            latents = matmul(two_out_t[...], hidden)
            raw = latents[0:64]
            raw_s[turn] = raw
            latent_s[turn] = (raw * row(turn, 3)).astype(bf16)
            amp = latents[64:96] + latents[96:128]
            line = jnp.sum(latents[128:136], axis=0, keepdims=True)
            put_row(rows_back.at[turn], 0, line * row(turn, 3))
            amp_s[turn] = amp
            amp = amp * (row(turn, 3) * row(turn, 4))
            add_atoms(found, envs, 0, amp)
            for axis in range(3):
                add_atoms(found, envs, 1 + axis, amp * row(turn, axis))
            return carry

        lax.fori_loop(0, turns, first, 0)
        for part in range(4):
            envs[part] = envs[part] * (1.0 / slots)

        def second(turn, carry):
            found = places(turn)
            cutoff_row = row(turn, 3)
            weight = cutoff_row * row(turn, 4)
            amp = amp_s[turn] * weight
            ways = [row(turn, axis) for axis in range(3)]
            env = [per_atom(found, envs, part) for part in range(4)]
            mix = env[0] + env[1] * ways[0] + env[2] * ways[1] + env[3] * ways[2]
            scalars = (amp * mix).astype(bf16)
            joined = jnp.concatenate([latent_s[turn], scalars], 0)
            pre = matmul(lat_in_t[...], joined)
            bent = jnp.tanh(pre)
            mixed = pre * bent
            slope = ((1.0 + bent) * (1.0 + (pre - mixed))).astype(bf16)
            rest = jnp.sum((pre + mixed) * energy_col[:, 0:1], axis=0, keepdims=True)
            back_rows = rows_back.at[turn]
            add_row(back_rows, 0, rest)
            back = matmul(lat_back[...], slope) * weight
            glat_s[turn] = back[0:64]
            gscal = back[64:96]
            mix_s[turn] = gscal * mix
            gprod = gscal * amp
            add_atoms(found, genvs, 0, gprod)
            for axis in range(3):
                add_atoms(found, genvs, 1 + axis, gprod * ways[axis])
                put_row(
                    back_rows, 1 + axis, jnp.sum(gprod * env[1 + axis], axis=0, keepdims=True)
                )
            return carry

        lax.fori_loop(0, turns, second, 0)
        for part in range(4):
            genvs[part] = genvs[part] * (1.0 / slots)

        def third(turn, carry):
            found = places(turn)
            ways = [row(turn, axis) for axis in range(3)]
            live_row = row(turn, 4)
            cutoff_row = row(turn, 3)
            weight = cutoff_row * live_row
            amp_raw = amp_s[turn]
            amp = amp_raw * weight
            genv = [per_atom(found, genvs, part) for part in range(4)]
            gamp = (
                mix_s[turn] + genv[0] + genv[1] * ways[0] + genv[2] * ways[1] + genv[3] * ways[2]
            ) * live_row
            for axis in range(3):
                put_row(near, axis, jnp.sum(amp * genv[1 + axis], axis=0, keepdims=True))
            glat = glat_s[turn] + readout_col[:, 0:1] * weight
            put_row(
                near,
                3,
                jnp.sum(glat * raw_s[turn], axis=0, keepdims=True)
                + jnp.sum(gamp * amp_raw, axis=0, keepdims=True),
            )
            gamp_b = (gamp * cutoff_row).astype(bf16)
            glatents = jnp.concatenate([(glat * cutoff_row).astype(bf16), gamp_b, gamp_b], 0)
            ghidden = matmul(two_out[...], glatents)
            gpre = (ghidden * slope_one[turn].astype(f32)).astype(bf16)
            gradial = matmul(radial_w[...], gpre)[0:8]
            put_row(near, 4, jnp.sum(gradial * radial_s[turn], axis=0, keepdims=True))

            pair = rows_back[turn, 0]
            direction = [rows_s[turn, axis] for axis in range(3)]
            live, inverse = rows_s[turn, 4], rows_s[turn, 7]
            gdir = [near[axis] + rows_back[turn, 1 + axis] for axis in range(3)]
            gcut = near[3] + pair * live
            gdist = near[4] - gcut * rows_s[turn, 8]
            along = gdir[0] * direction[0] + gdir[1] * direction[1] + gdir[2] * direction[2]
            push = gdist - along * inverse
            grel = [
                (gdir[axis] * inverse + direction[axis] * push) * live for axis in range(3)
            ]
            energy = pair * rows_s[turn, 3] * live
            distance = rows_s[turn, 6]
            for axis in range(3):
                near[5 + axis] = grel[axis]
                rel = direction[axis] * distance
                for other in range(3):
                    virial_s[3 * axis + other] += rel * grel[other]
            for unit, (_, _, outer) in enumerate(found):
                for axis in range(3):
                    back_ref[axis : axis + 1, outer] -= grel[axis][unit : unit + 1]
                back_ref[3:4, outer] += energy[unit : unit + 1]

            high_part = lax.shift_right_logical(entry_row(turn), 8)
            high_id = lax.broadcasted_iota(jnp.int32, (SPAN, span), 0).astype(f32).astype(bf16)
            mask = high_id == high_part.astype(f32).astype(bf16)
            grads = [
                jnp.concatenate([near[5 + axis, unit : unit + 1, :] for unit in range(units)], 1)
                for axis in range(3)
            ]
            spread = jnp.concatenate(
                [jnp.where(mask, grad.astype(bf16), jnp.zeros((), bf16)) for grad in grads], 0
            )
            added = matmul_nt(spread, low_hot[turn])
            for axis in range(3):
                ghalo_ref[axis, window, :] += added[axis * SPAN : (axis + 1) * SPAN]
            return carry

        lax.fori_loop(0, turns, third, 0)
        return carry

    lax.fori_loop(0, tiles, one_tile, 0)
    for entry in range(9):
        folded = jnp.sum(virial_s[entry], axis=0, keepdims=True)
        part = folded[:, 0:128]
        for chunk in range(1, UNIT // 128):
            part = part + folded[:, 128 * chunk : 128 * (chunk + 1)]
        virial_ref[entry : entry + 1, :] = -part
    virial_ref[9:16, :] = jnp.zeros((7, 128), f32)


def edge_call(place, halo, center, weights, tile, members):
    slots, atoms = 8, center.shape[1]
    rows = halo.shape[1]
    f32, bf16 = jnp.float32, jnp.bfloat16
    vmem = pl.BlockSpec(memory_space=pltpu.VMEM)
    shapes = (
        jax.ShapeDtypeStruct((3, rows, LANES), f32),
        jax.ShapeDtypeStruct((8, atoms), f32),
        jax.ShapeDtypeStruct((16, 128), f32),
    )
    turns = slots * tile // (UNITS * UNIT)
    span = UNITS * UNIT
    scratch = [pltpu.VMEM(part.shape, part.dtype) for part in weights]
    scratch += [
        pltpu.SemaphoreType.DMA((len(weights),)),
        pltpu.VMEM((3, rows, 2 * LANES), bf16),
        pltpu.VMEM((256, 32), bf16),
        pltpu.VMEM((144, 256), bf16),
        pltpu.VMEM((256, 128), bf16),
        pltpu.VMEM((256, 96), bf16),
        pltpu.VMEM((96, 256), bf16),
        pltpu.VMEM((256, 8), f32),
        pltpu.VMEM((16, 256), bf16),
        pltpu.VMEM((64, 8), f32),
        pltpu.VMEM((8, UNITS, UNIT), f32),
        pltpu.VMEM((turns, UNITS, UNIT), jnp.int32),
        pltpu.VMEM((turns, LANES, span), bf16),
        pltpu.VMEM((turns, 8, span), f32),
        pltpu.VMEM((turns, 256, span), bf16),
        pltpu.VMEM((turns, 64, span), f32),
        pltpu.VMEM((turns, 64, span), bf16),
        pltpu.VMEM((turns, 32, span), f32),
        pltpu.VMEM((turns, 32, span), f32),
        pltpu.VMEM((turns, 64, span), f32),
        pltpu.VMEM((turns, 10, UNITS, UNIT), f32),
        pltpu.VMEM((turns, 4, UNITS, UNIT), f32),
        pltpu.VMEM((4, 32, tile), f32),
        pltpu.VMEM((4, 32, tile), f32),
        pltpu.VMEM((9, UNITS, UNIT), f32),
        pltpu.SMEM((slots * (tile // UNIT) + slots + UNITS,), jnp.int32),
        pltpu.SMEM((slots * (tile // UNIT) + slots + UNITS,), jnp.int32),
    ]
    return pl.pallas_call(
        functools.partial(edge_kernel, UNITS, tile, members),
        out_shape=shapes,
        in_specs=[pl.BlockSpec(memory_space=pltpu.SMEM)] + [vmem] * 2
        + [pl.BlockSpec(memory_space=pltpu.HBM)] * len(weights),
        out_specs=(vmem,) * 3,
        scratch_shapes=scratch,
        compiler_params=pltpu.CompilerParams(vmem_limit_bytes=48 * 1024 * 1024),
    )(place, halo, center, *weights)


def send(source, target, send_sem, recv_sem, space, depth):
    return pltpu.make_async_remote_copy(
        src_ref=source,
        dst_ref=target,
        send_sem=send_sem,
        recv_sem=recv_sem,
        device_id=(space, depth),
        device_id_type=pl.DeviceIdType.MESH,
    )


def greet(space, depth):
    pl.semaphore_signal(
        pltpu.get_barrier_semaphore(),
        inc=1,
        device_id=(space, depth),
        device_id_type=pl.DeviceIdType.MESH,
    )


def where_am_i(group):
    spaces, depths = lax.axis_size("space"), lax.axis_size("depth")
    space, depth = lax.axis_index("space"), lax.axis_index("depth")
    spot = lax.rem(space, group)
    first = space - spot
    before = lax.rem(first - 1 + spaces, spaces)
    after = lax.rem(first + group, spaces)
    return spaces, depths, space, depth, spot, first, before, after


def collect_kernel(
    group,
    position_ref,
    species_ref,
    index_ref,
    count_ref,
    halo_ref,
    center_ref,
    packed_ref,
    position_in,
    species_in,
    index_in,
    count_in,
    load,
    own,
    depth_send,
    depth_recv,
    part_send,
    part_recv,
    column_send,
    column_recv,
    edge_send,
    edge_recv,
    relay_send,
    relay_recv,
):
    spaces, depths, space, depth, spot, first, before, after = where_am_i(group)
    loads = [
        pltpu.make_async_copy(source, target, load.at[at])
        for at, (source, target) in enumerate(
            (
                (position_ref, position_in),
                (species_ref, species_in),
                (count_ref, count_in),
                (index_ref, index_in),
            )
        )
    ]
    for copy in loads:
        copy.start()
    slots, atoms = index_ref.shape[0], packed_ref.shape[1]
    share = atoms // group
    up, down = lax.rem(depth + 1, depths), lax.rem(depth + depths - 1, depths)
    mates = [first + lax.rem(spot + off, group) for off in range(1, group)]
    side = lax.rem(space, 2)
    twin = space + 1 - 2 * side
    at_start, at_end = spot == 0, spot == group - 1
    at_edge = jnp.logical_or(at_start, at_end)
    edge_from = jnp.where(side == 0, after, before)

    greet(space, up)
    greet(space, down)
    for mate in mates:
        greet(mate, depth)
    greet(edge_from, depth)
    expected = 2 + (group - 1) + (group // 2) * at_edge.astype(jnp.int32)

    def piece(start, part):
        return halo_ref.at[:, pl.ds(pl.multiple_of(start + 16 * part, 16), 16), :]

    column = (spot + 1) * GAP
    for copy in loads:
        copy.wait()
    for part in range(3):
        packed_ref[part : part + 1, :] = position_in[part]
    packed_ref[3:4, :] = species_in[...].astype(jnp.float32)
    packed_ref[4:5, :] = count_in[...].astype(jnp.float32)
    packed_ref[5:8, :] = jnp.zeros((3, atoms), jnp.float32)
    for slot in range(slots):
        packed_ref[8 + slot : 9 + slot, :] = index_in[slot].astype(jnp.float32)
    for part in range(4):
        for row in range(atoms // LANES):
            own[part, row : row + 1, :] = packed_ref[
                part : part + 1, row * LANES : (row + 1) * LANES
            ]
    piece(column, 1)[...] = own[...]
    pl.semaphore_wait(pltpu.get_barrier_semaphore(), expected)

    jumps = list(range(2, group, 2))
    half = group // 2
    depth_copies = [
        send(own, piece(column, 0), depth_send.at[0], depth_recv.at[0], space, up),
        send(own, piece(column, 2), depth_send.at[1], depth_recv.at[1], space, down),
    ]
    for copy in depth_copies:
        copy.start()

    def edges(part):
        base = jnp.where(at_start, lax.rem(first - group + spaces, spaces), after)
        start = jnp.where(at_start, (group + 1) * GAP, 0)
        return [
            send(
                piece(column, part),
                piece(start, part),
                edge_send.at[3 * member + part],
                edge_recv.at[part],
                base + 2 * member + side,
                depth,
            )
            for member in range(half)
        ]

    direct = {}
    for part in (1, 0, 2):
        if part != 1:
            depth_copies[part // 2].wait_recv()
        block = piece(column, part)

        @pl.when(at_edge)
        def _(part=part):
            for copy in edges(part):
                copy.start()

        for at, off in enumerate(jumps + [0]):
            slot = 3 * at + part
            target = mates[off - 1] if off else twin
            copy = send(block, block, column_send.at[slot], column_recv.at[slot], target, depth)
            copy.start()
            direct[at, part] = copy
        if part == 1:
            mine = pl.ds(pl.multiple_of(spot * share, 128), share)
            part_copies = []
            for off in range(1, group):
                copy = send(
                    packed_ref.at[:, off * share : (off + 1) * share],
                    center_ref.at[:, mine],
                    part_send.at[off - 1],
                    part_recv.at[off - 1],
                    mates[off - 1],
                    depth,
                )
                copy.start()
                part_copies.append(copy)
            center_ref[:, mine] = packed_ref[:, 0:share]

    relays = []
    edge_start = jnp.where(side == 0, (group + 1) * GAP, 0)
    for part in (1, 0, 2):
        for at, off in enumerate(jumps + [0]):
            if off:
                direct[at, part].wait_recv()
                block = piece((lax.rem(spot + group - off, group) + 1) * GAP, part)
            else:
                block = piece(edge_start, part)
                send(
                    block, block, edge_send.at[part], edge_recv.at[part], edge_from, depth
                ).wait_recv()
            slot = 3 * at + part
            copy = send(block, block, relay_send.at[slot], relay_recv.at[slot], twin, depth)
            copy.start()
            relays.append(copy)

    for part in range(3):
        direct[len(jumps), part].wait_recv()
    for copy in part_copies + relays:
        copy.wait_recv()
    for copy in depth_copies + part_copies + list(direct.values()) + relays:
        copy.wait_send()

    @pl.when(at_edge)
    def _():
        for part in range(3):
            for copy in edges(part):
                copy.wait_send()


def collect_call(positions, species, index, count, group):
    slots, _, atoms = index.shape
    kinds = 8 + slots
    rows = (group + 2) * GAP
    f32 = jnp.float32
    vmem = pl.BlockSpec(memory_space=pltpu.VMEM)
    dma = pltpu.SemaphoreType.DMA
    half = group // 2
    return pl.pallas_call(
        functools.partial(collect_kernel, group),
        out_shape=(
            jax.ShapeDtypeStruct((4, rows, LANES), f32),
            jax.ShapeDtypeStruct((kinds, atoms), f32),
        ),
        in_specs=[pl.BlockSpec(memory_space=pltpu.HBM)] * 4,
        out_specs=(vmem,) * 2,
        scratch_shapes=[
            pltpu.VMEM((kinds, atoms), f32),
            pltpu.VMEM((3, 1, atoms), f32),
            pltpu.VMEM((1, atoms), jnp.int32),
            pltpu.VMEM((slots, 1, atoms), jnp.int32),
            pltpu.VMEM((1, atoms), jnp.int32),
            dma((4,)),
            pltpu.VMEM((4, atoms // LANES, LANES), f32),
            dma((2,)),
            dma((2,)),
            dma((group - 1,)),
            dma((group - 1,)),
            dma((3 * half,)),
            dma((3 * half,)),
            dma((3 * half,)),
            dma((3,)),
            dma((3 * half,)),
            dma((3 * half,)),
        ],
        compiler_params=pltpu.CompilerParams(
            collective_id=0, has_side_effects=True, vmem_limit_bytes=24 * 1024 * 1024
        ),
    )(positions, species, index, count)


def return_kernel(
    group,
    ghalo_ref,
    back_ref,
    virial_ref,
    force_ref,
    energy_ref,
    total_ref,
    columns,
    halves,
    sums,
    blocks,
    flat,
    summed,
    by_member,
    by_depth,
    by_group,
    twin_send,
    twin_recv,
    column_send,
    column_recv,
    edge_send,
    edge_recv,
    part_send,
    part_recv,
    block_send,
    block_recv,
    member_send,
    member_recv,
    layer_send,
    layer_recv,
    group_send,
    group_recv,
):
    spaces, depths, space, depth, spot, first, before, after = where_am_i(group)
    atoms = back_ref.shape[1]
    share = atoms // group
    groups = spaces // group
    up, down = lax.rem(depth + 1, depths), lax.rem(depth + depths - 1, depths)
    mates = [first + lax.rem(spot + off, group) for off in range(1, group)]
    layers = [lax.rem(depth + off, depths) for off in range(1, depths)]
    peers = [lax.rem(space + off * group, spaces) for off in range(1, groups)]
    at_start, at_end = spot == 0, spot == group - 1

    for mate in mates:
        greet(mate, depth)
    for layer in layers:
        greet(space, layer)
    for peer in peers:
        greet(peer, depth)
    side = lax.rem(space, 2)
    twin = space + 1 - 2 * side
    twin_spot = spot + 1 - 2 * side
    jumps = list(range(2, group, 2))
    at_edge = jnp.logical_or(at_start, at_end)
    edge_to = jnp.where(side == 0, after, before)

    @pl.when(at_edge)
    def _():
        base = jnp.where(at_start, lax.rem(first - group + spaces, spaces), after)
        for member in range(group // 2):
            greet(base + 2 * member + side, depth)

    pl.semaphore_wait(
        pltpu.get_barrier_semaphore(), (group - 1) + (depths - 1) + (groups - 1) + 1
    )

    started = []

    def go(*args):
        copy = send(*args)
        copy.start()
        started.append(copy)
        return copy

    by_member[spot] = virial_ref[...]
    mine = by_member.at[spot]
    member_copies = [
        go(mine, mine, member_send.at[off], member_recv.at[off], mate, depth)
        for off, mate in enumerate(mates)
    ]

    def column_starts(spot_at, side_at):
        starts = [(lax.rem(spot_at + off, group) + 1) * GAP for off in jumps + [0]]
        return starts + [jnp.where(side_at == 0, (group + 1) * GAP, 0)]

    def rows_at(start, part):
        return pl.ds(pl.multiple_of(start + 16 * part, 16), 16)

    layer_order = (0, 2, 1)
    own_kind, edge_kind = len(jumps), len(jumps) + 1
    kind_order = [edge_kind] + list(range(len(jumps) + 1))
    theirs = column_starts(twin_spot, 1 - side)
    kinds = column_starts(spot, side)
    halfway = {}
    for part in layer_order:
        for kind in kind_order:
            slot = 3 * kind + part
            halfway[kind, part] = go(
                ghalo_ref.at[:, rows_at(theirs[kind], part), :],
                halves.at[kind, :, 16 * part : 16 * part + 16, :],
                twin_send.at[slot],
                twin_recv.at[slot],
                twin,
                depth,
            )
    part_copies = []
    for off, mate in enumerate(mates):
        theirs = pl.ds(pl.multiple_of((mate - first) * share, 128), share)
        part = (group - 1 - off) * share
        part_copies.append(
            go(
                back_ref.at[:, theirs],
                flat.at[:, part : part + share],
                part_send.at[off],
                part_recv.at[off],
                mate,
                depth,
            )
        )
    own_part = pl.ds(pl.multiple_of(spot * share, 128), share)
    flat[:, 0:share] = back_ref[:, own_part]

    crossing = {}
    for part in layer_order:
        rows = slice(16 * part, 16 * part + 16)
        for kind in kind_order[:-1]:
            halfway[kind, part].wait_recv()
            sums[kind, :, rows, :] = (
                ghalo_ref[:, rows_at(kinds[kind], part), :] + halves[kind, :, rows, :]
            )
            if kind == edge_kind:
                slot = len(jumps) + spot // 2
                go(
                    sums.at[kind, :, rows, :],
                    columns.at[slot, :, rows, :],
                    edge_send.at[part],
                    edge_recv.at[3 * (spot // 2) + part],
                    edge_to,
                    depth,
                )
            else:
                crossing[kind, part] = go(
                    sums.at[kind, :, rows, :],
                    columns.at[kind, :, rows, :],
                    column_send.at[3 * kind + part],
                    column_recv.at[3 * kind + part],
                    mates[jumps[kind] - 1],
                    depth,
                )

    for copy in member_copies:
        copy.wait_recv()
    level = by_member[0]
    for member in range(1, group):
        level = level + by_member[member]
    by_depth[depth] = level
    mine_depth = by_depth.at[depth]
    layer_copies = [
        go(mine_depth, mine_depth, layer_send.at[off], layer_recv.at[off], space, layer)
        for off, layer in enumerate(layers)
    ]
    for copy in layer_copies:
        copy.wait_recv()
    level = by_depth[0]
    for layer in range(1, depths):
        level = level + by_depth[layer]
    place = space // group
    by_group[place] = level
    mine_group = by_group.at[place]
    group_copies = [
        go(mine_group, mine_group, group_send.at[off], group_recv.at[off], peer, depth)
        for off, peer in enumerate(peers)
    ]

    block_copies = []
    for part in layer_order:
        rows = slice(16 * part, 16 * part + 16)
        halfway[own_kind, part].wait_recv()
        total = ghalo_ref[:, rows_at(kinds[own_kind], part), :] + halves[own_kind, :, rows, :]
        for kind in range(len(jumps)):
            crossing[kind, part].wait_recv()
            total = total + columns[kind, :, rows, :]
        summed[:, rows, :] = total

        @pl.when(at_edge)
        def _(part=part, rows=rows):
            extra = jnp.zeros((3, 16, LANES), jnp.float32)
            for member in range(group // 2):
                block = columns.at[len(jumps) + member, :, rows, :]
                send(
                    block,
                    block,
                    edge_send.at[part],
                    edge_recv.at[3 * member + part],
                    edge_to,
                    depth,
                ).wait_recv()
                extra = extra + block[...]
            summed[:, rows, :] = summed[:, rows, :] + extra

        if part != 1:
            at, layer = part // 2, (down, up)[part // 2]
            block_copies.append(
                go(
                    summed.at[:, rows, :],
                    blocks.at[at],
                    block_send.at[at],
                    block_recv.at[at],
                    space,
                    layer,
                )
            )

    for copy in part_copies:
        copy.wait_recv()
    energy_ref[...] = flat[3:4, :]
    for copy in group_copies:
        copy.wait_recv()
    level = by_group[0]
    for member in range(1, groups):
        level = level + by_group[member]
    entries = jnp.sum(level, axis=1, keepdims=True)
    shape = (8, 128)
    row_id = lax.broadcasted_iota(jnp.int32, shape, 0)
    column_id = lax.broadcasted_iota(jnp.int32, shape, 1)
    table = jnp.zeros(shape, jnp.float32)
    for entry in range(9):
        here = jnp.logical_and(row_id == entry // 3, column_id == entry % 3)
        table = jnp.where(here, entries[entry : entry + 1, :], table)
    total_ref[...] = table[0:3, 0:3]
    for copy in block_copies:
        copy.wait_recv()
    blocks[0] = summed[:, 16:32, :] + blocks[0] + blocks[1]
    for part in range(3):
        for row in range(atoms // LANES):
            lanes = slice(row * LANES, (row + 1) * LANES)
            force_ref[part, :, lanes] = -(
                blocks[0, part, row : row + 1, :] + flat[part : part + 1, lanes]
            )
    for copy in started:
        copy.wait_send()


def return_call(ghalo, back, virial, group):
    atoms = back.shape[1]
    f32 = jnp.float32
    depths = lax.axis_size("depth")
    groups = lax.axis_size("space") // group
    vmem = pl.BlockSpec(memory_space=pltpu.VMEM)
    dma = pltpu.SemaphoreType.DMA
    half = group // 2
    counts = [
        3 * (half + 1),
        3 * (half + 1),
        3 * half,
        3 * half,
        3,
        3 * half,
        group - 1,
        group - 1,
        2,
        2,
        group - 1,
        group - 1,
        depths - 1,
        depths - 1,
        groups - 1,
        groups - 1,
    ]
    return pl.pallas_call(
        functools.partial(return_kernel, group),
        out_shape=(
            jax.ShapeDtypeStruct((3, 1, atoms), f32),
            jax.ShapeDtypeStruct((1, atoms), f32),
            jax.ShapeDtypeStruct((3, 3), f32),
        ),
        in_specs=[vmem] * 3,
        out_specs=(vmem,) * 3,
        scratch_shapes=[
            pltpu.VMEM((group - 1, 3, GAP, LANES), f32),
            pltpu.VMEM((half + 1, 3, GAP, LANES), f32),
            pltpu.VMEM((half + 1, 3, GAP, LANES), f32),
            pltpu.VMEM((2, 3, 16, LANES), f32),
            pltpu.VMEM((8, atoms), f32),
            pltpu.VMEM((3, GAP, LANES), f32),
            pltpu.VMEM((group, 16, 128), f32),
            pltpu.VMEM((depths, 16, 128), f32),
            pltpu.VMEM((groups, 16, 128), f32),
        ]
        + [dma((count,)) for count in counts],
        compiler_params=pltpu.CompilerParams(
            collective_id=1, has_side_effects=True, vmem_limit_bytes=24 * 1024 * 1024
        ),
    )(ghalo, back, virial)


def per_device(
    positions,
    species,
    neighbours,
    counts,
    species_table,
    w_two_in,
    w_two_out,
    w_env,
    w_lat_in,
    w_lat_out,
    readout,
):
    atom_count = positions.shape[-1]
    weights = [
        pltpu.with_memory_space_constraint(part, pltpu.HBM)
        for part in (
            species_table,
            w_two_in,
            w_two_out.T,
            w_env.T,
            w_lat_in,
            w_lat_out.T,
            readout.reshape(1, -1),
        )
    ]
    halo, center = collect_call(
        pltpu.with_memory_space_constraint(positions.reshape(3, 1, atom_count), pltpu.HBM),
        pltpu.with_memory_space_constraint(species.reshape(1, atom_count), pltpu.HBM),
        pltpu.with_memory_space_constraint(neighbours.reshape(-1, 1, atom_count), pltpu.HBM),
        pltpu.with_memory_space_constraint(counts.reshape(1, atom_count), pltpu.HBM),
        GROUP,
    )
    space = lax.axis_index("space")
    place = jnp.stack([space // GROUP * GROUP, lax.axis_index("depth")]).astype(jnp.int32)
    ghalo, back, virial = edge_call(
        place, halo, center, weights, TILE, GROUP
    )
    forces, energies, virial_total = return_call(ghalo, back, virial, GROUP)
    return (
        forces.reshape(3, 1, 1, atom_count),
        energies.reshape(1, 1, atom_count),
        virial_total,
    )


def solution(mesh):
    placed = (
        P(None, "space", "depth", None),
        P("space", "depth", None),
        P(None, "space", "depth", None),
        P("space", "depth", None),
        P(),
        P(),
        P(),
        P(),
        P(),
        P(),
        P(),
    )
    return jax.shard_map(
        per_device,
        mesh=mesh,
        in_specs=placed,
        out_specs=(P(None, "space", "depth", None), P("space", "depth", None), P()),
        check_vma=False,
    )
```

```python
import functools

import jax
import jax.numpy as jnp
from jax import lax
from jax.experimental import pallas as pl
from jax.experimental.pallas import tpu as pltpu
from jax.sharding import PartitionSpec as P

CUTOFF_RADIUS = 5.0
SOFT_CORE = 0.25

GROUP = 4
TILE = 1024
UNITS = 8
UNIT = 256
SIDE_LENGTH = 32.0
SPREAD = 36.0
GAP = 48
SPAN = 144
LANES = 256


def pieces(value, count):
    parts = []
    rest = value
    for _ in range(count):
        part = rest.astype(jnp.bfloat16)
        parts.append(part)
        rest = rest - part.astype(jnp.float32)
    return parts


def matmul(left, right):
    return jnp.dot(left, right, preferred_element_type=jnp.float32)


def matmul_nt(left, right):
    return lax.dot_general(
        left, right, (((1,), (1,)), ((), ())), preferred_element_type=jnp.float32
    )


def edge_kernel(
    units,
    tile,
    members,
    place_ref,
    halo_ref,
    center_ref,
    emb_ref,
    w_two_in_ref,
    w_two_out_ref,
    w_env_ref,
    w_lat_in_ref,
    w_lat_out_ref,
    readout_ref,
    ghalo_ref,
    back_ref,
    virial_ref,
    emb_in,
    two_in_in,
    two_out_in,
    env_in,
    lat_in_in,
    lat_out_in,
    readout_in,
    fetch,
    table,
    first_w,
    two_out_t,
    two_out,
    lat_in_t,
    lat_back,
    energy_col,
    radial_w,
    readout_col,
    near,
    entry_s,
    low_hot,
    radial_s,
    slope_one,
    raw_s,
    latent_s,
    amp_s,
    mix_s,
    glat_s,
    rows_s,
    rows_back,
    envs,
    genvs,
    virial_s,
    unit_slot,
    unit_chunk,
):
    slots, atoms = 8, center_ref.shape[1]
    tiles = atoms // tile
    rows = halo_ref.shape[1]
    f32, bf16 = jnp.float32, jnp.bfloat16
    base_space = place_ref[0]
    base_depth = place_ref[1]

    fetches = [
        pltpu.make_async_copy(source, target, fetch.at[at])
        for at, (source, target) in enumerate(
            (
                (emb_ref, emb_in),
                (w_two_in_ref, two_in_in),
                (w_two_out_ref, two_out_in),
                (w_env_ref, env_in),
                (w_lat_in_ref, lat_in_in),
                (w_lat_out_ref, lat_out_in),
                (readout_ref, readout_in),
            )
        )
    ]
    for copy in fetches:
        copy.start()

    row_id = lax.broadcasted_iota(jnp.int32, (rows, LANES), 0)
    space_of = (row_id // GAP - 1 + base_space).astype(f32)
    depth_of = (lax.rem(row_id, GAP) // 16 - 1 + base_depth).astype(f32)
    half = SIDE_LENGTH / 2
    local = [
        halo_ref[0] - (SIDE_LENGTH * space_of + half),
        halo_ref[1] - half + SPREAD * (halo_ref[3] - 1.5),
        halo_ref[2] - (SIDE_LENGTH * depth_of + half),
    ]
    for axis in range(3):
        high, low = pieces(local[axis], 2)
        table[axis, :, 0:LANES] = high
        table[axis, :, LANES : 2 * LANES] = low

    ghalo_ref[...] = jnp.zeros_like(ghalo_ref)
    back_ref[...] = jnp.zeros_like(back_ref)
    virial_s[...] = jnp.zeros_like(virial_s)

    for copy in fetches:
        copy.wait()
    w_one = two_in_in[...]
    lat_in = lat_in_in[...].astype(f32)
    two_out_now = two_out_in[...].astype(f32)
    lat_out_now = lat_out_in[...].astype(f32)
    env_now = env_in[...].astype(f32)
    emb = emb_in[...]
    center_part = matmul(emb, w_one[0:64])
    nbr_part = matmul(emb, w_one[64:128])
    species_part = 0.5 * jnp.concatenate([center_part, nbr_part], 0)
    radial_half = 0.5 * w_one[128:136].astype(f32)
    split = [part.astype(f32) for part in pieces(species_part, 3)]
    first_w[...] = jnp.concatenate([radial_half] + split, 0).T.astype(bf16)
    radial_w[...] = jnp.concatenate([radial_half, jnp.zeros_like(radial_half)], 0).astype(bf16)
    amp_high, amp_low = pieces(matmul(env_now.astype(bf16), two_out_now.astype(bf16)), 2)
    latent_rows = jnp.concatenate(
        [two_out_now, amp_high.astype(f32), amp_low.astype(f32)], 0
    )
    readout_row = readout_in[...]
    wide_row = jnp.broadcast_to(readout_row, (8, readout_row.shape[1]))
    line_row = jnp.dot(
        wide_row, two_out_now, precision=lax.Precision.HIGHEST, preferred_element_type=f32
    )
    line_rows = [part.astype(f32)[0:1] for part in pieces(line_row, 3)]
    two_out_t[0:128] = latent_rows.astype(bf16)
    two_out_t[128:144] = jnp.concatenate(
        line_rows + [jnp.zeros((13, two_out_now.shape[1]), f32)], 0
    ).astype(bf16)
    two_out[...] = latent_rows.T.astype(bf16)
    lat_in_t[...] = (0.5 * lat_in).T.astype(bf16)
    last_row = lax.dot_general(
        jnp.broadcast_to(readout_row, (8, readout_row.shape[1])),
        lat_out_now,
        (((1,), (0,)), ((), ())),
        precision=lax.Precision.HIGHEST,
        preferred_element_type=f32,
    )
    lat_back[...] = (0.5 * lat_in * last_row[0:1]).astype(bf16)
    energy_col[...] = last_row.T
    readout_col[...] = jnp.broadcast_to(readout_row, (8, readout_row.shape[1])).T

    chunks = tile // UNIT
    span = units * UNIT
    cuts = [slice(unit * UNIT, (unit + 1) * UNIT) for unit in range(units)]
    sharpness = (7 / CUTOFF_RADIUS) ** 2

    def one_tile(step, carry):
        lanes = pl.ds(pl.multiple_of(step * tile, tile), tile)
        count_row = center_ref[4:5, lanes]

        total = 0
        for chunk in range(chunks):
            depth = jnp.max(count_row[:, chunk * UNIT : (chunk + 1) * UNIT]).astype(jnp.int32)
            for slot in range(slots):
                unit_slot[total + slot] = slot
                unit_chunk[total + slot] = chunk
            total = total + depth
        for unit in range(units - 1):
            unit_slot[total + unit] = slots
            unit_chunk[total + unit] = 0
        turns = (total + (units - 1)) // units

        member = step // (tiles // members)
        window = pl.ds(pl.multiple_of(member * GAP, 16), SPAN)
        origin_x = SIDE_LENGTH * (base_space + member).astype(f32) + half
        origin_z = SIDE_LENGTH * base_depth.astype(f32) + half
        for part in range(4):
            envs[part] = jnp.zeros(envs.shape[1:], f32)
            genvs[part] = jnp.zeros(genvs.shape[1:], f32)

        def places(turn):
            found = []
            for unit in range(units):
                slot = unit_slot[turn * units + unit]
                chunk = unit_chunk[turn * units + unit]
                inner = pl.ds(pl.multiple_of(chunk * UNIT, UNIT), UNIT)
                outer = pl.ds(pl.multiple_of(step * tile + chunk * UNIT, UNIT), UNIT)
                found.append((slot, inner, outer))
            return found

        def row(turn, kind):
            return jnp.concatenate(
                [rows_s[turn, kind, unit : unit + 1, :] for unit in range(units)], 1
            )

        def per_atom(found, ref, part):
            return jnp.concatenate([ref[part, :, inner] for _, inner, _ in found], 1)

        def put_row(ref, kind, value):
            for unit, cut in enumerate(cuts):
                ref[kind, unit : unit + 1, :] = value[:, cut]

        def add_row(ref, kind, value):
            for unit, cut in enumerate(cuts):
                ref[kind, unit : unit + 1, :] += value[:, cut]

        def add_atoms(found, ref, part, value):
            for (_, inner, _), cut in zip(found, cuts):
                ref[part, :, inner] += value[:, cut]

        def entry_row(turn):
            return jnp.concatenate(
                [entry_s[turn, unit : unit + 1, :] for unit in range(units)], 1
            )

        def first(turn, carry):
            found = places(turn)
            for unit, (slot, _, outer) in enumerate(found):
                one = slice(unit, unit + 1)
                entry = center_ref[pl.ds(jnp.minimum(slot, slots - 1) + 8, 1), outer]
                entry_s[turn, one, :] = entry.astype(jnp.int32)
                for kind in range(4):
                    near[3 + kind, one, :] = center_ref[kind : kind + 1, outer]
                near[7, one, :] = center_ref[4:5, outer] - slot.astype(f32)
            entry = entry_row(turn)
            low_part = lax.bitwise_and(entry, LANES - 1)
            high_part = lax.shift_right_logical(entry, 8)
            low_id = lax.broadcasted_iota(jnp.int32, (LANES, span), 0).astype(f32).astype(bf16)
            low_row = low_part.astype(f32).astype(bf16)
            hot = jnp.where(low_id == low_row, jnp.ones((), bf16), jnp.zeros((), bf16))
            low_hot[turn] = hot
            both = jnp.concatenate([hot, hot], 0)
            left = jnp.concatenate([table[axis, window, :] for axis in range(3)], 0)
            mask = lax.broadcasted_iota(jnp.int32, (SPAN, span), 0) == high_part
            for unit, cut in enumerate(cuts):
                seen = matmul(left, both[:, cut])
                for axis in range(3):
                    near[axis, unit : unit + 1, :] = jnp.sum(
                        jnp.where(mask[:, cut], seen[axis * SPAN : (axis + 1) * SPAN], 0.0),
                        axis=0,
                        keepdims=True,
                    )

            block = lax.shift_right_logical(entry_s[turn], 12)
            block_space = lax.shift_right_logical(block * 11, 5)
            block_depth = block - 3 * block_space
            nbr_species = jnp.floor((near[1] + 2.0 * SPREAD) * (1.0 / SPREAD))
            rel = [
                near[0] + SIDE_LENGTH * (block_space - 1).astype(f32) - (near[3] - origin_x),
                near[1] - SPREAD * (nbr_species - 1.5) - (near[4] - half),
                near[2] + SIDE_LENGTH * (block_depth - 1).astype(f32) - (near[5] - origin_z),
            ]
            squared = rel[0] * rel[0] + rel[1] * rel[1] + rel[2] * rel[2] + SOFT_CORE
            inverse = lax.rsqrt(squared)
            distance = squared * inverse
            fraction = jnp.minimum(distance * (1.0 / CUTOFF_RADIUS), 1.0)
            shell = 1.0 - fraction * fraction
            for axis in range(3):
                rows_s[turn, axis] = rel[axis] * inverse
            rows_s[turn, 3] = shell * shell
            rows_s[turn, 4] = jnp.where(near[7] > 0.0, 1.0, 0.0)
            rows_s[turn, 5] = nbr_species
            rows_s[turn, 6] = distance
            rows_s[turn, 7] = inverse
            rows_s[turn, 8] = shell * fraction * (4.0 / CUTOFF_RADIUS)
            rows_s[turn, 9] = near[6]

            basis_id = lax.broadcasted_iota(jnp.int32, (8, span), 0).astype(f32)
            spread = row(turn, 6) - basis_id * (CUTOFF_RADIUS / 7)
            radial = jnp.exp(-sharpness * spread * spread)
            radial_s[turn] = radial * (-2.0 * sharpness * spread)
            species_hot = jnp.where(
                basis_id < 4.0,
                (basis_id == row(turn, 9)).astype(f32),
                (basis_id - 4.0 == row(turn, 5)).astype(f32),
            )
            features = jnp.concatenate([radial, species_hot, species_hot, species_hot], 0)
            pre = matmul(first_w[...], features.astype(bf16))
            bent = jnp.tanh(pre)
            mixed = pre * bent
            hidden = (pre + mixed).astype(bf16)
            slope_one[turn] = ((1.0 + bent) * (1.0 + (pre - mixed))).astype(bf16)
            latents = matmul(two_out_t[...], hidden)
            raw = latents[0:64]
            raw_s[turn] = raw
            latent_s[turn] = (raw * row(turn, 3)).astype(bf16)
            amp = latents[64:96] + latents[96:128]
            line = jnp.sum(latents[128:136], axis=0, keepdims=True)
            put_row(rows_back.at[turn], 0, line * row(turn, 3))
            amp_s[turn] = amp
            amp = amp * (row(turn, 3) * row(turn, 4) * (1.0 / slots))
            add_atoms(found, envs, 0, amp)
            for axis in range(3):
                add_atoms(found, envs, 1 + axis, amp * row(turn, axis))
            return carry

        lax.fori_loop(0, turns, first, 0)
        def second(turn, carry):
            found = places(turn)
            cutoff_row = row(turn, 3)
            weight = cutoff_row * row(turn, 4)
            amp = amp_s[turn] * weight
            ways = [row(turn, axis) for axis in range(3)]
            env = [per_atom(found, envs, part) for part in range(4)]
            mix = env[0] + env[1] * ways[0] + env[2] * ways[1] + env[3] * ways[2]
            scalars = (amp * mix).astype(bf16)
            joined = jnp.concatenate([latent_s[turn], scalars], 0)
            pre = matmul(lat_in_t[...], joined)
            bent = jnp.tanh(pre)
            mixed = pre * bent
            slope = ((1.0 + bent) * (1.0 + (pre - mixed))).astype(bf16)
            rest = jnp.sum((pre + mixed) * energy_col[:, 0:1], axis=0, keepdims=True)
            back_rows = rows_back.at[turn]
            add_row(back_rows, 0, rest)
            back = matmul(lat_back[...], slope) * weight
            glat_s[turn] = back[0:64]
            gscal = back[64:96]
            mix_s[turn] = gscal * mix
            gprod = gscal * amp
            add_atoms(found, genvs, 0, gprod)
            for axis in range(3):
                add_atoms(found, genvs, 1 + axis, gprod * ways[axis])
                put_row(
                    back_rows, 1 + axis, jnp.sum(gprod * env[1 + axis], axis=0, keepdims=True)
                )
            return carry

        lax.fori_loop(0, turns, second, 0)
        def third(turn, carry):
            found = places(turn)
            ways = [row(turn, axis) for axis in range(3)]
            live_row = row(turn, 4)
            cutoff_row = row(turn, 3)
            weight = cutoff_row * live_row
            amp_raw = amp_s[turn]
            amp = amp_raw * weight
            genv = [per_atom(found, genvs, part) for part in range(4)]
            gamp = (
                mix_s[turn]
                + (genv[0] + genv[1] * ways[0] + genv[2] * ways[1] + genv[3] * ways[2])
                * (1.0 / slots)
            ) * live_row
            for axis in range(3):
                along = jnp.sum(amp * genv[1 + axis], axis=0, keepdims=True)
                put_row(near, axis, along * (1.0 / slots))
            glat = glat_s[turn] + readout_col[:, 0:1] * weight
            put_row(
                near,
                3,
                jnp.sum(glat * raw_s[turn], axis=0, keepdims=True)
                + jnp.sum(gamp * amp_raw, axis=0, keepdims=True),
            )
            gamp_b = (gamp * cutoff_row).astype(bf16)
            glatents = jnp.concatenate([(glat * cutoff_row).astype(bf16), gamp_b, gamp_b], 0)
            ghidden = matmul(two_out[...], glatents)
            gpre = (ghidden * slope_one[turn].astype(f32)).astype(bf16)
            gradial = matmul(radial_w[...], gpre)[0:8]
            put_row(near, 4, jnp.sum(gradial * radial_s[turn], axis=0, keepdims=True))

            pair = rows_back[turn, 0]
            direction = [rows_s[turn, axis] for axis in range(3)]
            live, inverse = rows_s[turn, 4], rows_s[turn, 7]
            gdir = [near[axis] + rows_back[turn, 1 + axis] for axis in range(3)]
            gcut = near[3] + pair * live
            gdist = near[4] - gcut * rows_s[turn, 8]
            along = gdir[0] * direction[0] + gdir[1] * direction[1] + gdir[2] * direction[2]
            push = gdist - along * inverse
            grel = [
                (gdir[axis] * inverse + direction[axis] * push) * live for axis in range(3)
            ]
            energy = pair * rows_s[turn, 3] * live
            distance = rows_s[turn, 6]
            for axis in range(3):
                near[5 + axis] = grel[axis]
                rel = direction[axis] * distance
                for other in range(3):
                    virial_s[3 * axis + other] += rel * grel[other]
            for unit, (_, _, outer) in enumerate(found):
                for axis in range(3):
                    back_ref[axis : axis + 1, outer] -= grel[axis][unit : unit + 1]
                back_ref[3:4, outer] += energy[unit : unit + 1]

            high_part = lax.shift_right_logical(entry_row(turn), 8)
            high_id = lax.broadcasted_iota(jnp.int32, (SPAN, span), 0).astype(f32).astype(bf16)
            mask = high_id == high_part.astype(f32).astype(bf16)
            grads = [
                jnp.concatenate([near[5 + axis, unit : unit + 1, :] for unit in range(units)], 1)
                for axis in range(3)
            ]
            spread = jnp.concatenate(
                [jnp.where(mask, grad.astype(bf16), jnp.zeros((), bf16)) for grad in grads], 0
            )
            added = matmul_nt(spread, low_hot[turn])
            for axis in range(3):
                ghalo_ref[axis, window, :] += added[axis * SPAN : (axis + 1) * SPAN]
            return carry

        lax.fori_loop(0, turns, third, 0)
        return carry

    lax.fori_loop(0, tiles, one_tile, 0)
    for entry in range(9):
        folded = jnp.sum(virial_s[entry], axis=0, keepdims=True)
        part = folded[:, 0:128]
        for chunk in range(1, UNIT // 128):
            part = part + folded[:, 128 * chunk : 128 * (chunk + 1)]
        virial_ref[entry : entry + 1, :] = -part
    virial_ref[9:16, :] = jnp.zeros((7, 128), f32)


def edge_call(place, halo, center, weights, tile, members):
    slots, atoms = 8, center.shape[1]
    rows = halo.shape[1]
    f32, bf16 = jnp.float32, jnp.bfloat16
    vmem = pl.BlockSpec(memory_space=pltpu.VMEM)
    shapes = (
        jax.ShapeDtypeStruct((3, rows, LANES), f32),
        jax.ShapeDtypeStruct((8, atoms), f32),
        jax.ShapeDtypeStruct((16, 128), f32),
    )
    turns = slots * tile // (UNITS * UNIT)
    span = UNITS * UNIT
    scratch = [pltpu.VMEM(part.shape, part.dtype) for part in weights]
    scratch += [
        pltpu.SemaphoreType.DMA((len(weights),)),
        pltpu.VMEM((3, rows, 2 * LANES), bf16),
        pltpu.VMEM((256, 32), bf16),
        pltpu.VMEM((144, 256), bf16),
        pltpu.VMEM((256, 128), bf16),
        pltpu.VMEM((256, 96), bf16),
        pltpu.VMEM((96, 256), bf16),
        pltpu.VMEM((256, 8), f32),
        pltpu.VMEM((16, 256), bf16),
        pltpu.VMEM((64, 8), f32),
        pltpu.VMEM((8, UNITS, UNIT), f32),
        pltpu.VMEM((turns, UNITS, UNIT), jnp.int32),
        pltpu.VMEM((turns, LANES, span), bf16),
        pltpu.VMEM((turns, 8, span), f32),
        pltpu.VMEM((turns, 256, span), bf16),
        pltpu.VMEM((turns, 64, span), f32),
        pltpu.VMEM((turns, 64, span), bf16),
        pltpu.VMEM((turns, 32, span), f32),
        pltpu.VMEM((turns, 32, span), f32),
        pltpu.VMEM((turns, 64, span), f32),
        pltpu.VMEM((turns, 10, UNITS, UNIT), f32),
        pltpu.VMEM((turns, 4, UNITS, UNIT), f32),
        pltpu.VMEM((4, 32, tile), f32),
        pltpu.VMEM((4, 32, tile), f32),
        pltpu.VMEM((9, UNITS, UNIT), f32),
        pltpu.SMEM((slots * (tile // UNIT) + slots + UNITS,), jnp.int32),
        pltpu.SMEM((slots * (tile // UNIT) + slots + UNITS,), jnp.int32),
    ]
    return pl.pallas_call(
        functools.partial(edge_kernel, UNITS, tile, members),
        out_shape=shapes,
        in_specs=[pl.BlockSpec(memory_space=pltpu.SMEM)] + [vmem] * 2
        + [pl.BlockSpec(memory_space=pltpu.HBM)] * len(weights),
        out_specs=(vmem,) * 3,
        scratch_shapes=scratch,
        compiler_params=pltpu.CompilerParams(vmem_limit_bytes=48 * 1024 * 1024),
    )(place, halo, center, *weights)


def send(source, target, send_sem, recv_sem, space, depth):
    return pltpu.make_async_remote_copy(
        src_ref=source,
        dst_ref=target,
        send_sem=send_sem,
        recv_sem=recv_sem,
        device_id=(space, depth),
        device_id_type=pl.DeviceIdType.MESH,
    )


def greet(space, depth):
    pl.semaphore_signal(
        pltpu.get_barrier_semaphore(),
        inc=1,
        device_id=(space, depth),
        device_id_type=pl.DeviceIdType.MESH,
    )


def where_am_i(group):
    spaces, depths = lax.axis_size("space"), lax.axis_size("depth")
    space, depth = lax.axis_index("space"), lax.axis_index("depth")
    spot = lax.rem(space, group)
    first = space - spot
    before = lax.rem(first - 1 + spaces, spaces)
    after = lax.rem(first + group, spaces)
    return spaces, depths, space, depth, spot, first, before, after


def collect_kernel(
    group,
    position_ref,
    species_ref,
    index_ref,
    count_ref,
    halo_ref,
    center_ref,
    packed_ref,
    position_in,
    species_in,
    index_in,
    count_in,
    load,
    own,
    depth_send,
    depth_recv,
    part_send,
    part_recv,
    column_send,
    column_recv,
    edge_send,
    edge_recv,
    relay_send,
    relay_recv,
):
    spaces, depths, space, depth, spot, first, before, after = where_am_i(group)
    loads = [
        pltpu.make_async_copy(source, target, load.at[at])
        for at, (source, target) in enumerate(
            (
                (position_ref, position_in),
                (species_ref, species_in),
                (count_ref, count_in),
                (index_ref, index_in),
            )
        )
    ]
    for copy in loads:
        copy.start()
    slots, atoms = index_ref.shape[0], packed_ref.shape[1]
    share = atoms // group
    up, down = lax.rem(depth + 1, depths), lax.rem(depth + depths - 1, depths)
    mates = [first + lax.rem(spot + off, group) for off in range(1, group)]
    side = lax.rem(space, 2)
    twin = space + 1 - 2 * side
    at_start, at_end = spot == 0, spot == group - 1
    at_edge = jnp.logical_or(at_start, at_end)
    edge_from = jnp.where(side == 0, after, before)

    greet(space, up)
    greet(space, down)
    for mate in mates:
        greet(mate, depth)
    greet(edge_from, depth)
    expected = 2 + (group - 1) + (group // 2) * at_edge.astype(jnp.int32)

    def piece(start, part):
        return halo_ref.at[:, pl.ds(pl.multiple_of(start + 16 * part, 16), 16), :]

    column = (spot + 1) * GAP
    for copy in loads[0:3]:
        copy.wait()
    for part in range(3):
        packed_ref[part : part + 1, :] = position_in[part]
    packed_ref[3:4, :] = species_in[...].astype(jnp.float32)
    packed_ref[4:5, :] = count_in[...].astype(jnp.float32)
    packed_ref[5:8, :] = jnp.zeros((3, atoms), jnp.float32)
    for part in range(4):
        for row in range(atoms // LANES):
            own[part, row : row + 1, :] = packed_ref[
                part : part + 1, row * LANES : (row + 1) * LANES
            ]
    piece(column, 1)[...] = own[...]
    pl.semaphore_wait(pltpu.get_barrier_semaphore(), expected)

    jumps = list(range(2, group, 2))
    half = group // 2
    depth_copies = [
        send(own, piece(column, 0), depth_send.at[0], depth_recv.at[0], space, up),
        send(own, piece(column, 2), depth_send.at[1], depth_recv.at[1], space, down),
    ]
    for copy in depth_copies:
        copy.start()

    def edges(part):
        base = jnp.where(at_start, lax.rem(first - group + spaces, spaces), after)
        start = jnp.where(at_start, (group + 1) * GAP, 0)
        return [
            send(
                piece(column, part),
                piece(start, part),
                edge_send.at[3 * member + part],
                edge_recv.at[part],
                base + 2 * member + side,
                depth,
            )
            for member in range(half)
        ]

    direct = {}
    for part in (1, 0, 2):
        if part != 1:
            depth_copies[part // 2].wait_recv()
        block = piece(column, part)

        @pl.when(at_edge)
        def _(part=part):
            for copy in edges(part):
                copy.start()

        for at, off in enumerate(jumps + [0]):
            slot = 3 * at + part
            target = mates[off - 1] if off else twin
            copy = send(block, block, column_send.at[slot], column_recv.at[slot], target, depth)
            copy.start()
            direct[at, part] = copy
        if part == 1:
            loads[3].wait()
            for slot in range(slots):
                packed_ref[8 + slot : 9 + slot, :] = index_in[slot].astype(jnp.float32)
            mine = pl.ds(pl.multiple_of(spot * share, 128), share)
            part_copies = []
            for off in range(1, group):
                copy = send(
                    packed_ref.at[:, off * share : (off + 1) * share],
                    center_ref.at[:, mine],
                    part_send.at[off - 1],
                    part_recv.at[off - 1],
                    mates[off - 1],
                    depth,
                )
                copy.start()
                part_copies.append(copy)
            center_ref[:, mine] = packed_ref[:, 0:share]

    relays = []
    edge_start = jnp.where(side == 0, (group + 1) * GAP, 0)
    for part in (1, 0, 2):
        for at, off in enumerate(jumps + [0]):
            if off:
                direct[at, part].wait_recv()
                block = piece((lax.rem(spot + group - off, group) + 1) * GAP, part)
            else:
                block = piece(edge_start, part)
                send(
                    block, block, edge_send.at[part], edge_recv.at[part], edge_from, depth
                ).wait_recv()
            slot = 3 * at + part
            copy = send(block, block, relay_send.at[slot], relay_recv.at[slot], twin, depth)
            copy.start()
            relays.append(copy)

    for part in range(3):
        direct[len(jumps), part].wait_recv()
    for copy in part_copies + relays:
        copy.wait_recv()
    for copy in depth_copies + part_copies + list(direct.values()) + relays:
        copy.wait_send()

    @pl.when(at_edge)
    def _():
        for part in range(3):
            for copy in edges(part):
                copy.wait_send()


def collect_call(positions, species, index, count, group):
    slots, _, atoms = index.shape
    kinds = 8 + slots
    rows = (group + 2) * GAP
    f32 = jnp.float32
    vmem = pl.BlockSpec(memory_space=pltpu.VMEM)
    dma = pltpu.SemaphoreType.DMA
    half = group // 2
    return pl.pallas_call(
        functools.partial(collect_kernel, group),
        out_shape=(
            jax.ShapeDtypeStruct((4, rows, LANES), f32),
            jax.ShapeDtypeStruct((kinds, atoms), f32),
        ),
        in_specs=[pl.BlockSpec(memory_space=pltpu.HBM)] * 4,
        out_specs=(vmem,) * 2,
        scratch_shapes=[
            pltpu.VMEM((kinds, atoms), f32),
            pltpu.VMEM((3, 1, atoms), f32),
            pltpu.VMEM((1, atoms), jnp.int32),
            pltpu.VMEM((slots, 1, atoms), jnp.int32),
            pltpu.VMEM((1, atoms), jnp.int32),
            dma((4,)),
            pltpu.VMEM((4, atoms // LANES, LANES), f32),
            dma((2,)),
            dma((2,)),
            dma((group - 1,)),
            dma((group - 1,)),
            dma((3 * half,)),
            dma((3 * half,)),
            dma((3 * half,)),
            dma((3,)),
            dma((3 * half,)),
            dma((3 * half,)),
        ],
        compiler_params=pltpu.CompilerParams(
            collective_id=0, has_side_effects=True, vmem_limit_bytes=24 * 1024 * 1024
        ),
    )(positions, species, index, count)


def return_kernel(
    group,
    ghalo_ref,
    back_ref,
    virial_ref,
    force_ref,
    energy_ref,
    total_ref,
    columns,
    halves,
    sums,
    blocks,
    flat,
    summed,
    by_member,
    by_depth,
    by_group,
    twin_send,
    twin_recv,
    column_send,
    column_recv,
    edge_send,
    edge_recv,
    part_send,
    part_recv,
    block_send,
    block_recv,
    member_send,
    member_recv,
    layer_send,
    layer_recv,
    group_send,
    group_recv,
):
    spaces, depths, space, depth, spot, first, before, after = where_am_i(group)
    atoms = back_ref.shape[1]
    share = atoms // group
    groups = spaces // group
    up, down = lax.rem(depth + 1, depths), lax.rem(depth + depths - 1, depths)
    mates = [first + lax.rem(spot + off, group) for off in range(1, group)]
    layers = [lax.rem(depth + off, depths) for off in range(1, depths)]
    peers = [lax.rem(space + off * group, spaces) for off in range(1, groups)]
    at_start, at_end = spot == 0, spot == group - 1

    for mate in mates:
        greet(mate, depth)
    for layer in layers:
        greet(space, layer)
    for peer in peers:
        greet(peer, depth)
    side = lax.rem(space, 2)
    twin = space + 1 - 2 * side
    twin_spot = spot + 1 - 2 * side
    jumps = list(range(2, group, 2))
    at_edge = jnp.logical_or(at_start, at_end)
    edge_to = jnp.where(side == 0, after, before)

    @pl.when(at_edge)
    def _():
        base = jnp.where(at_start, lax.rem(first - group + spaces, spaces), after)
        for member in range(group // 2):
            greet(base + 2 * member + side, depth)

    pl.semaphore_wait(
        pltpu.get_barrier_semaphore(), (group - 1) + (depths - 1) + (groups - 1) + 1
    )

    started = []

    def go(*args):
        copy = send(*args)
        copy.start()
        started.append(copy)
        return copy

    by_member[spot] = virial_ref[...]
    mine = by_member.at[spot]
    member_copies = [
        go(mine, mine, member_send.at[off], member_recv.at[off], mate, depth)
        for off, mate in enumerate(mates)
    ]

    def column_starts(spot_at, side_at):
        starts = [(lax.rem(spot_at + off, group) + 1) * GAP for off in jumps + [0]]
        return starts + [jnp.where(side_at == 0, (group + 1) * GAP, 0)]

    def rows_at(start, part):
        return pl.ds(pl.multiple_of(start + 16 * part, 16), 16)

    layer_order = (0, 2, 1)
    own_kind, edge_kind = len(jumps), len(jumps) + 1
    kind_order = [edge_kind] + list(range(len(jumps) + 1))
    theirs = column_starts(twin_spot, 1 - side)
    kinds = column_starts(spot, side)
    halfway = {}
    for part in layer_order:
        for kind in kind_order:
            slot = 3 * kind + part
            halfway[kind, part] = go(
                ghalo_ref.at[:, rows_at(theirs[kind], part), :],
                halves.at[kind, :, 16 * part : 16 * part + 16, :],
                twin_send.at[slot],
                twin_recv.at[slot],
                twin,
                depth,
            )
    part_copies = []
    for off, mate in enumerate(mates):
        theirs = pl.ds(pl.multiple_of((mate - first) * share, 128), share)
        part = (group - 1 - off) * share
        part_copies.append(
            go(
                back_ref.at[:, theirs],
                flat.at[:, part : part + share],
                part_send.at[off],
                part_recv.at[off],
                mate,
                depth,
            )
        )
    own_part = pl.ds(pl.multiple_of(spot * share, 128), share)
    flat[:, 0:share] = back_ref[:, own_part]

    crossing = {}
    for part in layer_order:
        rows = slice(16 * part, 16 * part + 16)
        for kind in kind_order[:-1]:
            halfway[kind, part].wait_recv()
            sums[kind, :, rows, :] = (
                ghalo_ref[:, rows_at(kinds[kind], part), :] + halves[kind, :, rows, :]
            )
            if kind == edge_kind:
                slot = len(jumps) + spot // 2
                go(
                    sums.at[kind, :, rows, :],
                    columns.at[slot, :, rows, :],
                    edge_send.at[part],
                    edge_recv.at[3 * (spot // 2) + part],
                    edge_to,
                    depth,
                )
            else:
                crossing[kind, part] = go(
                    sums.at[kind, :, rows, :],
                    columns.at[kind, :, rows, :],
                    column_send.at[3 * kind + part],
                    column_recv.at[3 * kind + part],
                    mates[jumps[kind] - 1],
                    depth,
                )

    for copy in member_copies:
        copy.wait_recv()
    level = by_member[0]
    for member in range(1, group):
        level = level + by_member[member]
    by_depth[depth] = level
    mine_depth = by_depth.at[depth]
    layer_copies = [
        go(mine_depth, mine_depth, layer_send.at[off], layer_recv.at[off], space, layer)
        for off, layer in enumerate(layers)
    ]
    for copy in layer_copies:
        copy.wait_recv()
    level = by_depth[0]
    for layer in range(1, depths):
        level = level + by_depth[layer]
    place = space // group
    by_group[place] = level
    mine_group = by_group.at[place]
    group_copies = [
        go(mine_group, mine_group, group_send.at[off], group_recv.at[off], peer, depth)
        for off, peer in enumerate(peers)
    ]

    block_copies = []
    for part in layer_order:
        rows = slice(16 * part, 16 * part + 16)
        halfway[own_kind, part].wait_recv()
        total = ghalo_ref[:, rows_at(kinds[own_kind], part), :] + halves[own_kind, :, rows, :]
        for kind in range(len(jumps)):
            crossing[kind, part].wait_recv()
            total = total + columns[kind, :, rows, :]
        summed[:, rows, :] = total

        @pl.when(at_edge)
        def _(part=part, rows=rows):
            extra = jnp.zeros((3, 16, LANES), jnp.float32)
            for member in range(group // 2):
                block = columns.at[len(jumps) + member, :, rows, :]
                send(
                    block,
                    block,
                    edge_send.at[part],
                    edge_recv.at[3 * member + part],
                    edge_to,
                    depth,
                ).wait_recv()
                extra = extra + block[...]
            summed[:, rows, :] = summed[:, rows, :] + extra

        if part != 1:
            at, layer = part // 2, (down, up)[part // 2]
            block_copies.append(
                go(
                    summed.at[:, rows, :],
                    blocks.at[at],
                    block_send.at[at],
                    block_recv.at[at],
                    space,
                    layer,
                )
            )

    for copy in part_copies:
        copy.wait_recv()
    energy_ref[...] = flat[3:4, :]
    for copy in group_copies:
        copy.wait_recv()
    level = by_group[0]
    for member in range(1, groups):
        level = level + by_group[member]
    entries = jnp.sum(level, axis=1, keepdims=True)
    shape = (8, 128)
    row_id = lax.broadcasted_iota(jnp.int32, shape, 0)
    column_id = lax.broadcasted_iota(jnp.int32, shape, 1)
    table = jnp.zeros(shape, jnp.float32)
    for entry in range(9):
        here = jnp.logical_and(row_id == entry // 3, column_id == entry % 3)
        table = jnp.where(here, entries[entry : entry + 1, :], table)
    total_ref[...] = table[0:3, 0:3]
    for copy in block_copies:
        copy.wait_recv()
    blocks[0] = summed[:, 16:32, :] + blocks[0] + blocks[1]
    for part in range(3):
        for row in range(atoms // LANES):
            lanes = slice(row * LANES, (row + 1) * LANES)
            force_ref[part, :, lanes] = -(
                blocks[0, part, row : row + 1, :] + flat[part : part + 1, lanes]
            )
    for copy in started:
        copy.wait_send()


def return_call(ghalo, back, virial, group):
    atoms = back.shape[1]
    f32 = jnp.float32
    depths = lax.axis_size("depth")
    groups = lax.axis_size("space") // group
    vmem = pl.BlockSpec(memory_space=pltpu.VMEM)
    dma = pltpu.SemaphoreType.DMA
    half = group // 2
    counts = [
        3 * (half + 1),
        3 * (half + 1),
        3 * half,
        3 * half,
        3,
        3 * half,
        group - 1,
        group - 1,
        2,
        2,
        group - 1,
        group - 1,
        depths - 1,
        depths - 1,
        groups - 1,
        groups - 1,
    ]
    return pl.pallas_call(
        functools.partial(return_kernel, group),
        out_shape=(
            jax.ShapeDtypeStruct((3, 1, atoms), f32),
            jax.ShapeDtypeStruct((1, atoms), f32),
            jax.ShapeDtypeStruct((3, 3), f32),
        ),
        in_specs=[vmem] * 3,
        out_specs=(vmem,) * 3,
        scratch_shapes=[
            pltpu.VMEM((group - 1, 3, GAP, LANES), f32),
            pltpu.VMEM((half + 1, 3, GAP, LANES), f32),
            pltpu.VMEM((half + 1, 3, GAP, LANES), f32),
            pltpu.VMEM((2, 3, 16, LANES), f32),
            pltpu.VMEM((8, atoms), f32),
            pltpu.VMEM((3, GAP, LANES), f32),
            pltpu.VMEM((group, 16, 128), f32),
            pltpu.VMEM((depths, 16, 128), f32),
            pltpu.VMEM((groups, 16, 128), f32),
        ]
        + [dma((count,)) for count in counts],
        compiler_params=pltpu.CompilerParams(
            collective_id=1, has_side_effects=True, vmem_limit_bytes=24 * 1024 * 1024
        ),
    )(ghalo, back, virial)


def per_device(
    positions,
    species,
    neighbours,
    counts,
    species_table,
    w_two_in,
    w_two_out,
    w_env,
    w_lat_in,
    w_lat_out,
    readout,
):
    atom_count = positions.shape[-1]
    weights = [
        pltpu.with_memory_space_constraint(part, pltpu.HBM)
        for part in (
            species_table,
            w_two_in,
            w_two_out.T,
            w_env.T,
            w_lat_in,
            w_lat_out.T,
            readout.reshape(1, -1),
        )
    ]
    halo, center = collect_call(
        pltpu.with_memory_space_constraint(positions.reshape(3, 1, atom_count), pltpu.HBM),
        pltpu.with_memory_space_constraint(species.reshape(1, atom_count), pltpu.HBM),
        pltpu.with_memory_space_constraint(neighbours.reshape(-1, 1, atom_count), pltpu.HBM),
        pltpu.with_memory_space_constraint(counts.reshape(1, atom_count), pltpu.HBM),
        GROUP,
    )
    space = lax.axis_index("space")
    place = jnp.stack([space // GROUP * GROUP, lax.axis_index("depth")]).astype(jnp.int32)
    ghalo, back, virial = edge_call(
        place, halo, center, weights, TILE, GROUP
    )
    forces, energies, virial_total = return_call(ghalo, back, virial, GROUP)
    return (
        forces.reshape(3, 1, 1, atom_count),
        energies.reshape(1, 1, atom_count),
        virial_total,
    )


def solution(mesh):
    placed = (
        P(None, "space", "depth", None),
        P("space", "depth", None),
        P(None, "space", "depth", None),
        P("space", "depth", None),
        P(),
        P(),
        P(),
        P(),
        P(),
        P(),
        P(),
    )
    return jax.shard_map(
        per_device,
        mesh=mesh,
        in_specs=placed,
        out_specs=(P(None, "space", "depth", None), P("space", "depth", None), P()),
        check_vma=False,
    )
```
